32 devices in a mesh: clip: 4 (over y, x), chan: 8 (over z, core).
Axes of the slice: x: 2, y: 2, z: 4, core: 2. Of those that a mesh axis runs over, the one named last changes fastest.
Arguments:
- features: bfloat16 [128, 196, 1024], P(('clip', 'chan')), may hold values from -6 to 6
- cotangent: bfloat16 [128, 196, 1024], P(('clip', 'chan')), may hold values from -6 to 6
- frame_counts: int32 [4], replicated, may hold values from 8 to 32, as said below
- weight_first: float32 [3, 1024, 256], P(None, 'chan'), may hold values from -0.109375 to 0.109375
- weight_middle: float32 [9, 256, 256], P(None, 'chan'), may hold values from -0.125 to 0.125
- weight_last: float32 [256, 1024], P('chan'), may hold values from -0.375 to 0.375
- weight_embed: float32 [1024, 3, 512], P('chan'), may hold values from -0.1875 to 0.1875
- weight_back: float32 [512, 1024], P('chan'), may hold values from -0.25 to 0.25
- norm_params: float32 [5120], replicated, may hold values from 0.5 to 1.5
- moment_first: float32 [3, 1024, 256], P(None, 'chan'), may hold values from -0.0008544922 to 0.0008544922
- moment_middle: float32 [9, 256, 256], P(None, 'chan'), may hold values from -0.0008544922 to 0.0008544922
- moment_last: float32 [256, 1024], P('chan'), may hold values from -0.0008544922 to 0.0008544922
- moment_embed: float32 [1024, 3, 512], P('chan'), may hold values from -0.0008544922 to 0.0008544922
- moment_back: float32 [512, 1024], P('chan'), may hold values from -0.0008544922 to 0.0008544922
- moment_norm: float32 [5120], replicated, may hold values from -0.0024414062 to 0.0024414062
- second_first: float32 [3, 1024, 256], P(None, 'chan'), may hold values from 2.6733165e-09 to 1.0693266e-08
- second_middle: float32 [9, 256, 256], P(None, 'chan'), may hold values from 2.6733165e-09 to 1.0693266e-08
- second_last: float32 [256, 1024], P('chan'), may hold values from 2.6733165e-09 to 1.0693266e-08
- second_embed: float32 [1024, 3, 512], P('chan'), may hold values from 2.6733165e-09 to 1.0693266e-08
- second_back: float32 [512, 1024], P('chan'), may hold values from 2.6733165e-09 to 1.0693266e-08
- second_norm: float32 [5120], replicated, may hold values from 1.33665825e-08 to 5.346633e-08
Outputs:
- mixed: bfloat16 [128, 196, 1024], P(('clip', 'chan'))
- features_gradient: bfloat16 [128, 196, 1024], P(('clip', 'chan'))
- first_gradient: float32 [3, 1024, 256], replicated
- middle_gradient: float32 [9, 256, 256], replicated
- last_gradient: float32 [256, 1024], replicated
- embed_gradient: float32 [1024, 3, 512], replicated
- back_gradient: float32 [512, 1024], replicated
- norm_gradient: float32 [5120], replicated
- moment_first_new: float32 [3, 1024, 256], P(None, 'chan')
- moment_middle_new: float32 [9, 256, 256], P(None, 'chan')
- moment_last_new: float32 [256, 1024], P('chan')
- moment_embed_new: float32 [1024, 3, 512], P('chan')
- moment_back_new: float32 [512, 1024], P('chan')
- moment_norm_new: float32 [5120], replicated
- second_first_new: float32 [3, 1024, 256], P(None, 'chan')
- second_middle_new: float32 [9, 256, 256], P(None, 'chan')
- second_last_new: float32 [256, 1024], P('chan')
- second_embed_new: float32 [1024, 3, 512], P('chan')
- second_back_new: float32 [512, 1024], P('chan')
- second_norm_new: float32 [5120], replicated
- weight_first_new: float32 [3, 1024, 256], P(None, 'chan')
- weight_middle_new: float32 [9, 256, 256], P(None, 'chan')
- weight_last_new: float32 [256, 1024], P('chan')
- weight_embed_new: float32 [1024, 3, 512], P('chan')
- weight_back_new: float32 [512, 1024], P('chan')
- norm_params_new: float32 [5120], replicated
- gradient_norm: float32 [], replicated
The draws below stay inside these ranges and needn't reach their ends.
Inputs may be any that keep to these rules, and one draw needn't show every extreme that they name: `frame_counts`: each clip has 8, 16 or 32 valid frames, and some clip has 32.
All inputs are finite; a program needn't handle non-finite values.
Results may differ from the reference program's by a relative error of at most 0.035.
Values may be sent and summed in bfloat16 or wider, within the bound.
No kernel may reach another device: no remote copies, remote signals or barrier semaphores. Data moves between devices by JAX's collectives and lax.ppermute only.
A program may use at most 256 MiB of HBM per device.

```python
import math
from functools import partial
import jax
import jax.numpy as jnp
from jax import lax

D = 1024
BOT = 256
INNER = 512
HH = 14
WW = 14
MAXF = 32
STEP = 10
SPOTS = 196
CLIPS = 4
FRAMES = 128
NPAR = 3740672


def draw_frame_counts(key, part):
    key = jax.random.fold_in(key, 7)
    pick_key, full_key = jax.random.split(key)
    picked = jax.random.randint(pick_key, (CLIPS,), 0, 3)
    counts = jnp.where(picked == 0, MAXF // 4, jnp.where(picked == 1, MAXF // 2, MAXF))
    chosen = jax.random.randint(full_key, (), 0, CLIPS)
    places = jnp.arange(CLIPS, dtype=jnp.int32)
    counts = jnp.where(places == chosen, MAXF, counts)
    return counts.astype(jnp.int32)


def level_of(stream_key, shape, shards, least, high):
    def one(position, blocks):
        draws = jax.random.uniform(jax.random.fold_in(jax.random.fold_in(stream_key, 6), position), (blocks,), jnp.float32, least / len(shards), high / len(shards))
        return jnp.repeat(jnp.exp(draws), shape[position] // blocks).reshape((-1,) + (1,) * (len(shape) - position - 1))

    gain = one(*shards[0])
    for cut in shards[1:]:
        gain = gain * one(*cut)
    return gain


def centred(stream_key, extent, scale, reach, cuts=(), held_as=jnp.bfloat16):
    result = scale * jax.random.normal(stream_key, extent, jnp.float32)
    if cuts:
        result = result * level_of(stream_key, extent, cuts, -0.22, 0.18)
    return jnp.clip(result, -reach, reach).astype(held_as)


def setup_inputs(seed: int = 0) -> dict:
    key_list = jax.random.split(jax.random.key(seed), 22)
    features = centred(key_list[0], (FRAMES, SPOTS, D), 1.0, 6.0, ((0, 32),))
    cotangent = centred(key_list[1], (FRAMES, SPOTS, D), 1.0, 6.0, ((0, 32),))
    frame_counts = draw_frame_counts(jax.random.fold_in(key_list[21], 71), 0)
    weight_first = centred(key_list[3], (3, D, BOT), (3 * D) ** -0.5, 0.109375, ((1, 8),), jnp.float32)
    weight_middle = centred(key_list[4], (9, BOT, BOT), (9 * BOT) ** -0.5, 0.125, ((1, 8),), jnp.float32)
    weight_last = centred(key_list[5], (BOT, D), BOT ** -0.5, 0.375, ((0, 8),), jnp.float32)
    weight_embed = centred(key_list[6], (D, 3, INNER), D ** -0.5, 0.1875, ((0, 8),), jnp.float32)
    weight_back = centred(key_list[7], (INNER, D), INNER ** -0.5, 0.25, ((0, 8),), jnp.float32)
    norm_params = jnp.clip(1.0 + 0.1 * jax.random.normal(key_list[8], (4 * BOT + 4 * D,), jnp.float32), 0.5, 1.5)
    moment_first = centred(key_list[9], (3, D, BOT), (0.11 * NPAR ** -0.5), 0.0008544922, ((1, 8),), jnp.float32)
    moment_middle = centred(key_list[10], (9, BOT, BOT), (0.11 * NPAR ** -0.5), 0.0008544922, ((1, 8),), jnp.float32)
    moment_last = centred(key_list[11], (BOT, D), (0.11 * NPAR ** -0.5), 0.0008544922, ((0, 8),), jnp.float32)
    moment_embed = centred(key_list[12], (D, 3, INNER), (0.11 * NPAR ** -0.5), 0.0008544922, ((0, 8),), jnp.float32)
    moment_back = centred(key_list[13], (INNER, D), (0.11 * NPAR ** -0.5), 0.0008544922, ((0, 8),), jnp.float32)
    moment_norm = centred(key_list[14], (4 * BOT + 4 * D,), (0.33 * NPAR ** -0.5), 0.0024414062, (), jnp.float32)
    second_first = jnp.clip(jnp.exp(math.log(1.0693265828365384e-08) - 1.3862944 * jax.random.uniform(key_list[15], (3, D, BOT), jnp.float32) ** level_of(key_list[15], (3, D, BOT), ((1, 8),), -0.2, 0.2)), 2.673316457091346e-09, 1.0693265828365384e-08)
    second_middle = jnp.clip(jnp.exp(math.log(1.0693265828365384e-08) - 1.3862944 * jax.random.uniform(key_list[16], (9, BOT, BOT), jnp.float32) ** level_of(key_list[16], (9, BOT, BOT), ((1, 8),), -0.2, 0.2)), 2.673316457091346e-09, 1.0693265828365384e-08)
    second_last = jnp.clip(jnp.exp(math.log(1.0693265828365384e-08) - 1.3862944 * jax.random.uniform(key_list[17], (BOT, D), jnp.float32) ** level_of(key_list[17], (BOT, D), ((0, 8),), -0.2, 0.2)), 2.673316457091346e-09, 1.0693265828365384e-08)
    second_embed = jnp.clip(jnp.exp(math.log(1.0693265828365384e-08) - 1.3862944 * jax.random.uniform(key_list[18], (D, 3, INNER), jnp.float32) ** level_of(key_list[18], (D, 3, INNER), ((0, 8),), -0.2, 0.2)), 2.673316457091346e-09, 1.0693265828365384e-08)
    second_back = jnp.clip(jnp.exp(math.log(1.0693265828365384e-08) - 1.3862944 * jax.random.uniform(key_list[19], (INNER, D), jnp.float32) ** level_of(key_list[19], (INNER, D), ((0, 8),), -0.2, 0.2)), 2.673316457091346e-09, 1.0693265828365384e-08)
    second_norm = jnp.clip(jnp.exp(jax.random.uniform(key_list[20], (4 * BOT + 4 * D,), jnp.float32, math.log(1.3366582507501334e-08), math.log(5.346633003000534e-08))), 1.3366582507501334e-08, 5.346633003000534e-08)
    return dict(features=features, cotangent=cotangent, frame_counts=frame_counts, weight_first=weight_first, weight_middle=weight_middle, weight_last=weight_last, weight_embed=weight_embed, weight_back=weight_back, norm_params=norm_params, moment_first=moment_first, moment_middle=moment_middle, moment_last=moment_last, moment_embed=moment_embed, moment_back=moment_back, moment_norm=moment_norm, second_first=second_first, second_middle=second_middle, second_last=second_last, second_embed=second_embed, second_back=second_back, second_norm=second_norm)


EPS_NORM = 1e-05
BETA_ONE = 0.9
BETA_TWO = 0.95
ADAM_EPS = 1e-08
WEIGHT_DECAY = 0.01
CLIP_AT = 1.0
GAIN_RATE = 0.5
MASKED = -1e+30
HIGHEST = lax.Precision.HIGHEST

@jax.custom_vjp
def low(v):
    return lax.optimization_barrier(v.astype(jnp.bfloat16)).astype(jnp.float32)

@jax.custom_vjp
def low_back(v):
    return v

def low_keep(v):
    return (low(v), None)

def low_pass(kept, grad):
    return (grad,)

def back_keep(v):
    return (v, None)

def back_low(kept, grad):
    return (low(grad),)
low.defvjp(low_keep, low_pass)
low_back.defvjp(back_keep, back_low)

def batch_norm(values, gains, shifts, valid_rows, row_total):
    mean = lax.optimization_barrier(jnp.sum(values * valid_rows, axis=0)) / row_total
    square = lax.optimization_barrier(jnp.sum(values * values * valid_rows, axis=0)) / row_total
    scales = lax.rsqrt(square - mean * mean + EPS_NORM)
    return (values - mean) * scales * gains + shifts

def attend(block):
    query, keys, values, key_ok = block
    scores = low_back(jnp.dot(query, keys.T, precision=HIGHEST) * INNER ** (-0.5))
    scores = jnp.where(key_ok[None, :] > 0, scores, MASKED)
    row_peak = lax.optimization_barrier(jnp.max(scores, axis=1, keepdims=True))
    lifted = jnp.exp(scores - row_peak) * key_ok[None, :]
    weights = lifted / lax.optimization_barrier(jnp.sum(lifted, axis=1, keepdims=True))
    return jnp.dot(low(weights), values, precision=HIGHEST)

def forward(features, weight_first, weight_middle, weight_last, weight_embed, weight_back, norm_params, frame_ok=None, valid_rows=None, key_ok=None, row_total=None):
    first_low = low(weight_first)
    middle_low = low(weight_middle)
    last_low = low(weight_last)
    embed_low = low(weight_embed)
    back_low = low(weight_back)
    span_list = [BOT] * 4 + [D] * 4
    starts = [sum(span_list[:index]) for index in range(8)]
    pieces = [norm_params[starts[index]:starts[index] + span_list[index]] for index in range(8)]
    gain_one, shift_one, gain_two, shift_two, gain_three, shift_three, gain_four, shift_four = pieces
    grid = features.reshape(CLIPS, MAXF, SPOTS, D) * frame_ok[:, :, None, None]
    padded = jnp.pad(grid, ((0, 0), (1, 1), (0, 0), (0, 0)))
    first_pre = jnp.zeros((CLIPS, MAXF, SPOTS, BOT), jnp.float32)
    for offset in range(3):
        first_pre = first_pre + jnp.einsum('cfsd,de->cfse', padded[:, offset:offset + MAXF], first_low[offset], precision=HIGHEST)
    first_pre = low_back(first_pre.reshape(-1, BOT))
    act_one = low(jax.nn.silu(batch_norm(first_pre, gain_one, shift_one, valid_rows, row_total)) * valid_rows)
    spatial = jnp.pad(act_one.reshape(CLIPS * MAXF, HH, WW, BOT), ((0, 0), (1, 1), (1, 1), (0, 0)))
    middle_pre = jnp.zeros((CLIPS * MAXF, HH, WW, BOT), jnp.float32)
    for row_tap in range(3):
        for col_tap in range(3):
            middle_pre = middle_pre + jnp.einsum('nhwc,ce->nhwe', spatial[:, row_tap:row_tap + HH, col_tap:col_tap + WW], middle_low[3 * row_tap + col_tap], precision=HIGHEST)
    middle_pre = low_back(middle_pre.reshape(-1, BOT))
    act_two = low(jax.nn.silu(batch_norm(middle_pre, gain_two, shift_two, valid_rows, row_total)) * valid_rows)
    last_pre = low_back(jnp.dot(act_two, last_low, precision=HIGHEST))
    residual_out = jax.nn.silu(features.reshape(-1, D) + batch_norm(last_pre, gain_three, shift_three, valid_rows, row_total)) * valid_rows
    residual_low = low(residual_out)
    projected = [low_back(low(jnp.dot(residual_low, embed_low[:, index], precision=HIGHEST))) for index in range(3)]
    shaped = [item.reshape(CLIPS, MAXF * SPOTS, INNER) for item in projected]
    attended = lax.map(jax.checkpoint(attend), (shaped[0], shaped[1], shaped[2], key_ok))
    attended = low_back(low(attended.reshape(-1, INNER)))
    attn_pre = low_back(jnp.dot(attended, back_low, precision=HIGHEST))
    return (residual_out + batch_norm(attn_pre, gain_four, shift_four, valid_rows, row_total)) * valid_rows

def adam_step(master, gradient, moment, second, factor, rate):
    clipped = gradient * factor
    moment_new = BETA_ONE * moment + (1.0 - BETA_ONE) * clipped
    second_new = BETA_TWO * second + (1.0 - BETA_TWO) * clipped * clipped
    moment_hat = moment_new / (1.0 - BETA_ONE ** STEP)
    second_hat = second_new / (1.0 - BETA_TWO ** STEP)
    master_new = master - rate * (moment_hat / (jnp.sqrt(second_hat) + ADAM_EPS) + WEIGHT_DECAY * master)
    return (moment_new, second_new, master_new)

def reference(features, cotangent, frame_counts, weight_first, weight_middle, weight_last, weight_embed, weight_back, norm_params, moment_first, moment_middle, moment_last, moment_embed, moment_back, moment_norm, second_first, second_middle, second_last, second_embed, second_back, second_norm):
    frame_ok = (jnp.arange(MAXF, dtype=jnp.int32)[None, :] < frame_counts[:, None]).astype(jnp.float32)
    valid_rows = jnp.repeat(frame_ok.reshape(-1), SPOTS)[:, None]
    key_ok = jnp.repeat(frame_ok, SPOTS, axis=1)
    row_total = jnp.sum(frame_counts).astype(jnp.float32) * SPOTS
    bound = partial(forward, frame_ok=frame_ok, valid_rows=valid_rows, key_ok=key_ok, row_total=row_total)
    masters = (weight_first, weight_middle, weight_last, weight_embed, weight_back, norm_params)
    output, pullback = jax.vjp(bound, features.astype(jnp.float32), *masters)
    gradients = pullback(cotangent.reshape(-1, D).astype(jnp.float32))
    mixed = output.astype(jnp.bfloat16).reshape(FRAMES, SPOTS, D)
    features_gradient = gradients[0].astype(jnp.bfloat16).reshape(FRAMES, SPOTS, D)
    weight_grads = gradients[1:]
    gradient_norm = jnp.sqrt(sum((jnp.sum(item * item) for item in weight_grads)))
    factor = jnp.minimum(1.0, CLIP_AT / (gradient_norm + 1e-06))
    moments = (moment_first, moment_middle, moment_last, moment_embed, moment_back, moment_norm)
    seconds = (second_first, second_middle, second_last, second_embed, second_back, second_norm)
    fans = (3 * D, 9 * BOT, BOT, D, INNER)
    rates = [0.5 * fan ** (-0.5) for fan in fans] + [GAIN_RATE]
    results = [adam_step(masters[index], weight_grads[index], moments[index], seconds[index], factor, rates[index]) for index in range(6)]
    return (mixed, features_gradient, weight_grads[0], weight_grads[1], weight_grads[2], weight_grads[3], weight_grads[4], weight_grads[5], results[0][0], results[1][0], results[2][0], results[3][0], results[4][0], results[5][0], results[0][1], results[1][1], results[2][1], results[3][1], results[4][1], results[5][1], results[0][2], results[1][2], results[2][2], results[3][2], results[4][2], results[5][2], gradient_norm)
```

```python
import jax
import jax.numpy as jnp
from jax import lax
from jax.sharding import PartitionSpec as P

D = 1024
BOT = 256
INNER = 512
HH = 14
WW = 14
STEP = 10
DPC = 8


EPS_NORM = 1e-05
BETA_ONE = 0.9
BETA_TWO = 0.95
ADAM_EPS = 1e-08
WEIGHT_DECAY = 0.01
CLIP_AT = 1.0
GAIN_RATE = 0.5
MASKED = -1e30


def with_halo(cells, sides, width):
    for axis, dim in sides:
        count = lax.axis_size(axis)
        ends = count - 1
        head = lax.slice_in_dim(cells, 0, width, axis=dim)
        tail = lax.slice_in_dim(cells, cells.shape[dim] - width, cells.shape[dim], axis=dim)
        cells = jnp.concatenate(
            [
                lax.ppermute(tail, axis, [(i, (i + 1) % count) for i in range(ends)]),
                cells,
                lax.ppermute(head, axis, [((i + 1) % count, i) for i in range(ends)]),
            ],
            axis=dim,
        )
    return cells


def batch_stats(values, valid_rows, row_total):
    sums = total(
        jnp.stack(
            [jnp.sum(values * valid_rows, axis=0), jnp.sum(values * values * valid_rows, axis=0)]
        )
    )
    mean = sums[0] / row_total
    scales = lax.rsqrt(sums[1] / row_total - mean * mean + EPS_NORM)
    return ((values - mean) * scales, scales)


def batch_back(incoming, normal, scales, gains, valid_rows, row_total):
    sums = total(jnp.stack([jnp.sum(incoming, axis=0), jnp.sum(incoming * normal, axis=0)]))
    removed = (sums[0] + normal * sums[1]) / row_total
    return (valid_rows * gains * scales * (incoming - removed), sums[1], sums[0])


def silu_slope(values):
    sigmoid = jax.nn.sigmoid(values)
    return sigmoid * (1.0 + values * (1.0 - sigmoid))


def trim_rims(padded, clip_place):
    left_ok = (clip_place > 0).astype(padded.dtype)
    right_ok = (clip_place < DPC - 1).astype(padded.dtype)
    return jnp.concatenate([padded[:1] * left_ok, padded[1:-1], padded[-1:] * right_ok], axis=0)


def spatial_cols(values, frames):
    channels = values.shape[-1]
    grid = values.reshape(frames, HH, WW, channels)
    padded = jnp.pad(grid, ((0, 0), (1, 1), (1, 1), (0, 0)))
    tap_list = [
        padded[:, row_tap : row_tap + HH, col_tap : col_tap + WW]
        for row_tap in range(3)
        for col_tap in range(3)
    ]
    return jnp.concatenate(tap_list, axis=-1).reshape(frames * HH * WW, 9 * channels)


def spatial_back(columns, frames):
    channels = columns.shape[-1] // 9
    grid = columns.reshape(frames, HH, WW, 9, channels)
    padded = jnp.zeros((frames, HH + 2, WW + 2, channels), jnp.float32)
    for row_tap in range(3):
        for col_tap in range(3):
            padded = padded.at[:, row_tap : row_tap + HH, col_tap : col_tap + WW].add(
                grid[:, :, :, 3 * row_tap + col_tap]
            )
    return padded[:, 1:-1, 1:-1].reshape(frames * HH * WW, channels)


def flipped(value, axis, mask):
    pairs = [(source, source ^ mask) for source in range(lax.axis_size(axis))]
    return lax.ppermute(value, axis, pairs)


def total(value):
    for axis in ("chan", "clip"):
        bits = lax.axis_size(axis).bit_length() - 1
        levels = list(range(bits))
        groups = [levels[:1]] if axis == "chan" else []
        rest = levels[len(groups) :]
        groups += [rest[index : index + 2] for index in range(0, len(rest), 2)]
        for group in groups:
            base = 1 << group[0]
            parts = [flipped(value, axis, base * turn) for turn in range(1, 1 << len(group))]
            value = value + sum(parts[1:], parts[0])
    return value


def adam_step(master, gradient, moment, second, factor, rate):
    clipped = gradient * factor
    moment_new = BETA_ONE * moment + (1.0 - BETA_ONE) * clipped
    second_new = BETA_TWO * second + (1.0 - BETA_TWO) * clipped * clipped
    moment_hat = moment_new / (1.0 - BETA_ONE**STEP)
    second_hat = second_new / (1.0 - BETA_TWO**STEP)
    master_new = master - rate * (
        moment_hat / (jnp.sqrt(second_hat) + ADAM_EPS) + WEIGHT_DECAY * master
    )
    return (moment_new, second_new, master_new)


def body(
    features,
    cotangent,
    frame_counts,
    weight_first,
    weight_middle,
    weight_last,
    weight_embed,
    weight_back,
    norm_params,
    moment_first,
    moment_middle,
    moment_last,
    moment_embed,
    moment_back,
    moment_norm,
    second_first,
    second_middle,
    second_last,
    second_embed,
    second_back,
    second_norm,
):
    chan_at = lax.axis_index("chan")
    device = lax.axis_index("clip") * lax.axis_size("chan") + chan_at
    frames, spot_count, model_width = features.shape
    row_count = frames * spot_count
    narrow = BOT
    inner_width = INNER
    clip_place = chan_at % DPC
    clip_at = device // DPC
    clip_ids = jnp.arange(frame_counts.shape[0], dtype=jnp.int32)
    length = jnp.sum(jnp.where(clip_ids == clip_at, frame_counts, 0))
    local_frames = clip_place * frames + jnp.arange(frames, dtype=jnp.int32)
    frame_ok = (local_frames < length).astype(jnp.float32)
    valid_rows = jnp.repeat(frame_ok, spot_count)[:, None]
    row_total = jnp.sum(frame_counts).astype(jnp.float32) * spot_count
    block_frames = jnp.concatenate(
        [(clip_place ^ turn) * frames + jnp.arange(frames, dtype=jnp.int32) for turn in range(4)]
    )
    key_ok = jnp.repeat((block_frames < length).astype(jnp.float32), spot_count)
    span_list = [narrow] * 4 + [model_width] * 4
    starts = [sum(span_list[:index]) for index in range(8)]
    pieces = [norm_params[starts[index] : starts[index] + span_list[index]] for index in range(8)]
    gain_one, shift_one, gain_two, shift_two, gain_three, shift_three, gain_four, shift_four = (
        pieces
    )
    first_low, middle_low, last_low, embed_low, back_low = (
        lax.all_gather(weight_first.astype(jnp.bfloat16), "chan", axis=1, tiled=True),
        lax.all_gather(weight_middle.astype(jnp.bfloat16), "chan", axis=1, tiled=True),
        lax.all_gather(weight_last.astype(jnp.bfloat16), "chan", axis=0, tiled=True),
        lax.all_gather(weight_embed.astype(jnp.bfloat16), "chan", axis=0, tiled=True),
        lax.all_gather(weight_back.astype(jnp.bfloat16), "chan", axis=0, tiled=True),
    )
    masked = features * frame_ok.astype(jnp.bfloat16)[:, None, None]
    padded = trim_rims(with_halo(masked, (("chan", 0),), 1), clip_place)
    first_cols = jnp.concatenate(
        [padded[offset : offset + frames] for offset in range(3)], axis=-1
    ).reshape(row_count, 3 * model_width)
    first_pre = jnp.dot(
        first_cols, first_low.reshape(3 * model_width, narrow), preferred_element_type=jnp.float32
    )
    normal_one, scale_one = batch_stats(first_pre, valid_rows, row_total)
    act_one_pre = normal_one * gain_one + shift_one
    act_one = (jax.nn.silu(act_one_pre) * valid_rows).astype(jnp.bfloat16)
    middle_cols = spatial_cols(act_one, frames)
    middle_pre = jnp.dot(
        middle_cols, middle_low.reshape(9 * narrow, narrow), preferred_element_type=jnp.float32
    )
    normal_two, scale_two = batch_stats(middle_pre, valid_rows, row_total)
    act_two_pre = normal_two * gain_two + shift_two
    act_two = (jax.nn.silu(act_two_pre) * valid_rows).astype(jnp.bfloat16)
    last_pre = jnp.dot(act_two, last_low, preferred_element_type=jnp.float32)
    normal_three, scale_three = batch_stats(last_pre, valid_rows, row_total)
    residual_pre = features.reshape(row_count, model_width).astype(jnp.float32) + (
        normal_three * gain_three + shift_three
    )
    residual_out = jax.nn.silu(residual_pre) * valid_rows
    residual_low = residual_out.astype(jnp.bfloat16)
    projected = jnp.dot(
        residual_low,
        embed_low.reshape(model_width, 3 * inner_width),
        preferred_element_type=jnp.float32,
    ).astype(jnp.bfloat16)
    query = projected[:, :inner_width]
    pair_own = projected[:, inner_width:]
    pair_far = flipped(pair_own, "chan", 2)
    query_far = flipped(query, "chan", 4)
    clip_pairs = jnp.concatenate(
        [pair_own, flipped(pair_own, "chan", 1), pair_far, flipped(pair_far, "chan", 1)], axis=0
    )
    keys_all = clip_pairs[:, :inner_width]
    values_all = clip_pairs[:, inner_width:]
    scaling = inner_width ** (-0.5)

    def attend(rows):
        scores = (
            jnp.einsum("qd,kd->qk", rows, keys_all, preferred_element_type=jnp.float32) * scaling
        )
        scores = jnp.where(key_ok[None, :] > 0, scores, MASKED)
        row_peak = jnp.max(scores, axis=1, keepdims=True)
        lifted = jnp.exp(scores - row_peak)
        row_sums = jnp.sum(lifted, axis=1, keepdims=True)
        weights = lifted / row_sums
        part = jnp.dot(
            weights.astype(jnp.bfloat16), values_all, preferred_element_type=jnp.float32
        )
        return part, row_peak + jnp.log(row_sums)

    part_far, log_far = attend(query_far)
    part_far = flipped(part_far.astype(jnp.bfloat16), "chan", 4).astype(jnp.float32)
    log_far = flipped(log_far, "chan", 4)
    part_own, log_own = attend(query)
    log_peak = jnp.maximum(log_own, log_far)
    log_total = log_peak + jnp.log(jnp.exp(log_own - log_peak) + jnp.exp(log_far - log_peak))
    attended_wide = part_own * jnp.exp(log_own - log_total) + part_far * jnp.exp(log_far - log_total)
    attended = attended_wide.astype(jnp.bfloat16)
    attn_pre = jnp.dot(attended, back_low, preferred_element_type=jnp.float32)
    outer_grad = cotangent.reshape(row_count, model_width).astype(jnp.float32) * valid_rows
    sums = total(
        jnp.stack(
            [
                jnp.sum(attn_pre * valid_rows, axis=0),
                jnp.sum(attn_pre * attn_pre * valid_rows, axis=0),
                jnp.sum(outer_grad, axis=0),
                jnp.sum(outer_grad * attn_pre, axis=0),
            ]
        )
    )
    mean_four = sums[0] / row_total
    scale_four = lax.rsqrt(sums[1] / row_total - mean_four * mean_four + EPS_NORM)
    normal_four = (attn_pre - mean_four) * scale_four
    shift_four_grad = sums[2]
    gain_four_grad = scale_four * (sums[3] - mean_four * sums[2])
    mixed = (
        ((residual_out + (normal_four * gain_four + shift_four)) * valid_rows)
        .astype(jnp.bfloat16)
        .reshape(frames, spot_count, model_width)
    )
    removed_four = (shift_four_grad + normal_four * gain_four_grad) / row_total
    attn_grad = (valid_rows * gain_four * scale_four * (outer_grad - removed_four)).astype(
        jnp.bfloat16
    )
    back_local = jnp.einsum("rd,re->de", attended, attn_grad, preferred_element_type=jnp.float32)
    attended_grad = jnp.einsum(
        "re,de->rd", attn_grad, back_low, preferred_element_type=jnp.float32
    ).astype(jnp.bfloat16)
    row_term = jnp.sum(attended_grad.astype(jnp.float32) * attended_wide, axis=1, keepdims=True)
    attended_grad_far = flipped(attended_grad, "chan", 4)
    terms_far = flipped(jnp.concatenate([log_total, row_term], axis=1), "chan", 4)

    def attend_back(rows, rows_grad, logs, terms):
        again = jnp.einsum("qd,kd->qk", rows, keys_all, preferred_element_type=jnp.float32) * scaling
        again = jnp.where(key_ok[None, :] > 0, again, MASKED)
        weights = jnp.exp(again - logs)
        prob_grad = jnp.einsum(
            "qd,kd->qk", rows_grad, values_all, preferred_element_type=jnp.float32
        )
        score_grad = (weights * (prob_grad - terms)).astype(jnp.bfloat16)
        rows_back = jnp.dot(score_grad, keys_all, preferred_element_type=jnp.float32) * scaling
        key_part = (
            jnp.einsum("qk,qd->kd", score_grad, rows, preferred_element_type=jnp.float32) * scaling
        )
        value_part = jnp.einsum(
            "qk,qd->kd",
            weights.astype(jnp.bfloat16),
            rows_grad,
            preferred_element_type=jnp.float32,
        )
        return rows_back, jnp.concatenate([key_part, value_part], axis=1)

    query_own, pair_grad_own = attend_back(query, attended_grad, log_total, row_term)
    query_part, pair_grad_far = attend_back(
        query_far, attended_grad_far, terms_far[:, :1], terms_far[:, 1:]
    )
    query_grad = (
        query_own + flipped(query_part.astype(jnp.bfloat16), "chan", 4).astype(jnp.float32)
    ).astype(jnp.bfloat16)
    pair_sum = (pair_grad_own + pair_grad_far).reshape(4, row_count, 2 * inner_width)
    near = flipped(pair_sum[1::2].astype(jnp.bfloat16), "chan", 1).astype(jnp.float32)
    far = flipped((pair_sum[2] + near[1]).astype(jnp.bfloat16), "chan", 2).astype(jnp.float32)
    pair_grad = (pair_sum[0] + near[0] + far).astype(jnp.bfloat16)
    projected_grad = jnp.concatenate([query_grad, pair_grad], axis=1)
    embed_local = jnp.einsum(
        "rd,re->de", residual_low, projected_grad, preferred_element_type=jnp.float32
    ).reshape(model_width, 3, inner_width)
    residual_grad = outer_grad + jnp.einsum(
        "re,de->rd",
        projected_grad,
        embed_low.reshape(model_width, 3 * inner_width),
        preferred_element_type=jnp.float32,
    )
    pre_grad = residual_grad * valid_rows * silu_slope(residual_pre)
    last_grad, gain_three_grad, shift_three_grad = batch_back(
        pre_grad, normal_three, scale_three, gain_three, valid_rows, row_total
    )
    last_grad = last_grad.astype(jnp.bfloat16)
    last_local = jnp.einsum("rc,rd->cd", act_two, last_grad, preferred_element_type=jnp.float32)
    two_grad = (
        jnp.einsum("rd,cd->rc", last_grad, last_low, preferred_element_type=jnp.float32)
        * valid_rows
        * silu_slope(act_two_pre)
    )
    middle_grad, gain_two_grad, shift_two_grad = batch_back(
        two_grad, normal_two, scale_two, gain_two, valid_rows, row_total
    )
    middle_grad = middle_grad.astype(jnp.bfloat16)
    middle_local = jnp.einsum(
        "rk,rc->kc", middle_cols, middle_grad, preferred_element_type=jnp.float32
    ).reshape(9, narrow, narrow)
    column_grad = jnp.einsum(
        "rc,kc->rk",
        middle_grad,
        middle_low.reshape(9 * narrow, narrow),
        preferred_element_type=jnp.float32,
    )
    one_grad = spatial_back(column_grad, frames) * valid_rows * silu_slope(act_one_pre)
    first_grad, gain_one_grad, shift_one_grad = batch_back(
        one_grad, normal_one, scale_one, gain_one, valid_rows, row_total
    )
    first_grad = first_grad.astype(jnp.bfloat16)
    first_local = jnp.einsum(
        "rk,rc->kc", first_cols, first_grad, preferred_element_type=jnp.float32
    ).reshape(3, model_width, narrow)
    grad_padded = trim_rims(
        with_halo(first_grad.reshape(frames, spot_count, narrow), (("chan", 0),), 1), clip_place
    )
    back_cols = jnp.stack(
        [grad_padded[2 - offset : 2 - offset + frames] for offset in range(3)], axis=2
    ).reshape(row_count, 3, narrow)
    conv_back = jnp.einsum("rtc,tdc->rd", back_cols, first_low, preferred_element_type=jnp.float32)
    features_gradient = (
        (conv_back * valid_rows + pre_grad)
        .astype(jnp.bfloat16)
        .reshape(frames, spot_count, model_width)
    )
    local_terms = (first_local, middle_local, last_local, embed_local, back_local)
    summed = [
        lax.psum(item.astype(jnp.bfloat16), ("clip", "chan")).astype(jnp.float32)
        for item in local_terms[:4]
    ] + [lax.psum(local_terms[4], ("clip", "chan"))]
    norm_gradient = jnp.concatenate(
        [
            gain_one_grad,
            shift_one_grad,
            gain_two_grad,
            shift_two_grad,
            gain_three_grad,
            shift_three_grad,
            gain_four_grad,
            shift_four_grad,
        ]
    )
    all_grads = tuple(summed) + (norm_gradient,)
    gradient_norm = jnp.sqrt(sum((jnp.sum(item * item) for item in all_grads)))
    factor = jnp.minimum(1.0, CLIP_AT / (gradient_norm + 1e-06))
    masters = (weight_first, weight_middle, weight_last, weight_embed, weight_back)
    moments = (moment_first, moment_middle, moment_last, moment_embed, moment_back)
    seconds = (second_first, second_middle, second_last, second_embed, second_back)
    shard_axes = (1, 1, 0, 0, 0)
    fans = (3 * D, 9 * BOT, BOT, D, INNER)
    results = []
    for index in range(5):
        span = masters[index].shape[shard_axes[index]]
        owned = lax.dynamic_slice_in_dim(all_grads[index], chan_at * span, span, shard_axes[index])
        results.append(
            adam_step(
                masters[index],
                owned,
                moments[index],
                seconds[index],
                factor,
                0.5 * fans[index] ** (-0.5),
            )
        )
    results.append(
        adam_step(norm_params, norm_gradient, moment_norm, second_norm, factor, GAIN_RATE)
    )
    return (
        mixed,
        features_gradient,
        all_grads[0],
        all_grads[1],
        all_grads[2],
        all_grads[3],
        all_grads[4],
        all_grads[5],
        results[0][0],
        results[1][0],
        results[2][0],
        results[3][0],
        results[4][0],
        results[5][0],
        results[0][1],
        results[1][1],
        results[2][1],
        results[3][1],
        results[4][1],
        results[5][1],
        results[0][2],
        results[1][2],
        results[2][2],
        results[3][2],
        results[4][2],
        results[5][2],
        gradient_norm,
    )


def solution(mesh):
    placed = (
        P(("clip", "chan"), None, None),
        P(("clip", "chan"), None, None),
        P(),
        P(None, "chan", None),
        P(None, "chan", None),
        P("chan", None),
        P("chan", None, None),
        P("chan", None),
        P(),
        P(None, "chan", None),
        P(None, "chan", None),
        P("chan", None),
        P("chan", None, None),
        P("chan", None),
        P(),
        P(None, "chan", None),
        P(None, "chan", None),
        P("chan", None),
        P("chan", None, None),
        P("chan", None),
        P(),
    )
    return jax.shard_map(
        body,
        mesh=mesh,
        in_specs=placed,
        out_specs=(
            P(("clip", "chan"), None, None),
            P(("clip", "chan"), None, None),
            P(),
            P(),
            P(),
            P(),
            P(),
            P(),
            P(None, "chan", None),
            P(None, "chan", None),
            P("chan", None),
            P("chan", None, None),
            P("chan", None),
            P(),
            P(None, "chan", None),
            P(None, "chan", None),
            P("chan", None),
            P("chan", None, None),
            P("chan", None),
            P(),
            P(None, "chan", None),
            P(None, "chan", None),
            P("chan", None),
            P("chan", None, None),
            P("chan", None),
            P(),
            P(),
        ),
        check_vma=False,
    )
```

```python
import functools
import math

import jax
import jax.numpy as jnp
import numpy as np
from jax import lax
from jax.experimental import pallas as pl
from jax.experimental.layout import Layout, with_layout_constraint
from jax.experimental.pallas import tpu as pltpu
from jax.sharding import PartitionSpec as P

D = 1024
BOT = 256
INNER = 512
HH = 14
WW = 14
STEP = 10
DPC = 8


EPS_NORM = 1e-05
BETA_ONE = 0.9
BETA_TWO = 0.95
ADAM_EPS = 1e-08
WEIGHT_DECAY = 0.01
CLIP_AT = 1.0
GAIN_RATE = 0.5


def flipped(value, axis, mask):
    pairs = [(source, source ^ mask) for source in range(lax.axis_size(axis))]
    return lax.ppermute(value, axis, pairs)


def whole_of(shard):
    return lax.all_gather(shard.astype(jnp.bfloat16), "chan", axis=0, tiled=False)


def tap_of(weights, tap):
    return weights[:, tap].reshape(weights.shape[0] * weights.shape[2], weights.shape[3])


def beside(cells, spots):
    ends = lax.axis_size("chan") - 1
    upward = [(index, index + 1) for index in range(ends)]
    downward = [(index + 1, index) for index in range(ends)]
    return (
        lax.ppermute(cells[-1:], "chan", upward).reshape(spots, cells.shape[-1]),
        lax.ppermute(cells[:1], "chan", downward).reshape(spots, cells.shape[-1]),
    )


def total(value):
    for axis in ("chan", "clip"):
        bits = lax.axis_size(axis).bit_length() - 1
        levels = list(range(bits))
        groups = [levels[:1]] if axis == "chan" else []
        rest = levels[len(groups) :]
        groups += [rest[index : index + 2] for index in range(0, len(rest), 2)]
        for group in groups:
            base = 1 << group[0]
            parts = [flipped(value, axis, base * turn) for turn in range(1, 1 << len(group))]
            value = value + sum(parts[1:], parts[0])
    return value


def level_groups(axis):
    bits = lax.axis_size(axis).bit_length() - 1
    levels = list(range(bits))
    groups = [levels[:1]] if axis == "chan" else []
    rest = levels[len(groups) :]
    return groups + [rest[index : index + 2] for index in range(0, len(rest), 2)]


def level_steps():
    order = [("chan", group) for group in level_groups("chan")]
    order = order[:1] + [("clip", group) for group in level_groups("clip")] + order[1:]
    steps = []
    for axis, group in order:
        base, count = 1 << group[0], 1 << len(group)
        steps.append((axis, base, count, (lax.axis_index(axis) >> group[0]) & (count - 1)))
    return steps


def half_kernel(place, value, arrived, out_ref, held, sem):
    size = arrived.shape[0]
    copy = pltpu.make_async_copy(value.at[pl.ds(pl.multiple_of(place[0] * size, 16), size), :], held, sem)
    copy.start()
    copy.wait()
    out_ref[...] = (held[...].astype(F32) + arrived[...].astype(F32)).astype(LOW)


def half_sum(place, value, arrived):
    return call(
        half_kernel,
        [(arrived.shape, LOW)],
        (place.reshape(1), value, arrived),
        scratch=[pltpu.VMEM(arrived.shape, LOW), pltpu.SemaphoreType.DMA],
        far=(1,),
    )[0]


def core_step(value):
    axis, base, count, place = level_steps()[0]
    size = value.shape[0] // count
    outgoing = lax.dynamic_slice_in_dim(value, (1 - place) * size, size)
    return half_sum(place, value, flipped(outgoing, axis, base))


def scatter_sum(value):
    for axis, base, count, place in level_steps()[1:]:
        size = value.shape[0] // count
        mine = lax.dynamic_slice_in_dim(value, place * size, size).astype(F32)
        arrived = [
            flipped(
                lax.dynamic_slice_in_dim(value, (place ^ turn) * size, size), axis, base * turn
            )
            for turn in range(1, count)
        ]
        for item in arrived:
            mine = mine + item.astype(F32)
        value = mine.astype(LOW)
    return value


def laid_out(rows, frames):
    grid = rows.reshape(frames, -1, rows.shape[1])
    return with_layout_constraint(grid, Layout(major_to_minor=(1, 0, 2)))


def tied(*values):
    return lax.optimization_barrier(values)


def gather_sum(value):
    for axis, base, count, place in reversed(level_steps()[1:]):
        size = value.shape[0]
        parts = [value] + [flipped(value, axis, base * turn) for turn in range(1, count)]
        whole = jnp.zeros((count,) + value.shape, LOW)
        for turn, part in enumerate(parts):
            whole = lax.dynamic_update_index_in_dim(whole, part, place ^ turn, 0)
        value = whole.reshape((count * size,) + value.shape[1:])
    return value


NEG = -1e30
MIB = 1 << 20
NN = (((1,), (0,)), ((), ()))
NT = (((1,), (1,)), ((), ()))
TN = (((0,), (0,)), ((), ()))
F32 = jnp.float32
LOW = jnp.bfloat16


def dot(left, right, dims=NN):
    return lax.dot_general(left, right, dims, preferred_element_type=F32)


def sig(values):
    return 1.0 / (1.0 + jnp.exp(-values))


def slope(values):
    gate = sig(values)
    return gate * (1.0 + values * (1.0 - gate))


def moments(sums, inverse):
    mean = sums[0:1] * inverse
    return mean, lax.rsqrt(sums[1:2] * inverse - mean * mean + EPS_NORM)


def column_sums(values):
    return jnp.sum(values, axis=0, keepdims=True)


def call(kernel, outs, args, scalars=1, scratch=(), vmem=48, far=(), far_out=(), micros=2):
    spaces = []
    for index in range(len(args)):
        if index < scalars:
            spaces.append(pl.BlockSpec(memory_space=pltpu.SMEM))
        elif index in far:
            spaces.append(pl.BlockSpec(memory_space=pltpu.HBM))
        else:
            spaces.append(pl.BlockSpec(memory_space=pltpu.VMEM))
    shapes = tuple(jax.ShapeDtypeStruct(shape, dtype) for shape, dtype in outs)
    out_specs = tuple(
        pl.BlockSpec(memory_space=pltpu.HBM if index in far_out else pltpu.VMEM)
        for index in range(len(outs))
    )
    return pl.pallas_call(
        kernel,
        out_shape=shapes,
        in_specs=spaces,
        out_specs=out_specs,
        scratch_shapes=list(scratch),
        compiler_params=pltpu.CompilerParams(vmem_limit_bytes=vmem * MIB),
        cost_estimate=pl.CostEstimate(
            flops=int(micros * 1e9), bytes_accessed=0, transcendentals=0
        ),
    )(*args)


def first_kernel(flags, cells, before, after, weights, pre_ref, sums_ref, early, late):
    rows = cells.shape[0]
    spots = before.shape[0]
    valid = flags[0]
    late[pl.ds(0, rows), :] = dot(cells[...], tap_of(weights, 2)) * valid
    late[pl.ds(rows, spots), :] = dot(after[...], tap_of(weights, 2)) * flags[2]
    early[pl.ds(0, spots), :] = dot(before[...], tap_of(weights, 0)) * flags[1]
    early[pl.ds(spots, rows), :] = dot(cells[...], tap_of(weights, 0)) * valid
    pre = (
        dot(cells[...], tap_of(weights, 1)) * valid
        + early[pl.ds(0, rows), :]
        + late[pl.ds(spots, rows), :]
    )
    pre_ref[...] = pre
    sums_ref[0:1, :] = column_sums(pre) * valid
    sums_ref[1:2, :] = column_sums(pre * pre) * valid


def first_conv(flags, cells, before, after, weights):
    rows, width = cells.shape
    narrow = weights.shape[3]
    spots = before.shape[0]
    return call(
        first_kernel,
        [((rows, narrow), F32), ((2, narrow), F32)],
        (flags, cells, before, after, weights),
        scratch=[pltpu.VMEM((rows + spots, narrow), F32)] * 2,
    )


def spread(values, edges, buffer, columns, rows):
    narrow = values.shape[1]
    margin = 16
    buffer[0, pl.ds(0, margin), :] = jnp.zeros((margin, narrow), F32)
    buffer[0, pl.ds(margin + rows, margin), :] = jnp.zeros((margin, narrow), F32)
    buffer[1, pl.ds(0, margin), :] = jnp.zeros((margin, narrow), F32)
    buffer[1, pl.ds(margin + rows, margin), :] = jnp.zeros((margin, narrow), F32)
    buffer[0, pl.ds(margin, rows), :] = values
    for across in range(3):
        moved = buffer[0, pl.ds(margin + across - 1, rows), :]
        if across == 0:
            moved = moved * edges[:, 0:1]
        if across == 2:
            moved = moved * edges[:, 1:2]
        buffer[1, pl.ds(margin, rows), :] = moved
        for down in range(3):
            part = buffer[1, pl.ds(margin + WW * (down - 1), rows), :]
            if down == 0:
                part = part * edges[:, 2:3]
            if down == 2:
                part = part * edges[:, 3:4]
            at = (3 * down + across) * narrow
            columns[:, at : at + narrow] = part.astype(LOW)


def spread_scratch(rows, narrow):
    return [pltpu.VMEM((2, rows + 32, narrow), F32), pltpu.VMEM((rows, 9 * narrow), LOW)]


def act_of(flags, pre, sums, scale_shift):
    mean, scale = moments(sums, flags[3])
    normal = (pre - mean) * scale
    return normal, normal * scale_shift[0:1] + scale_shift[1:2], scale


def middle_kernel(flags, pre, sums, gains, weights, edges, out_ref, sums_ref, buffer, columns):
    rows, narrow = pre.shape
    valid = flags[0]
    _, act, _ = act_of(flags, pre[...], sums[...], gains[...])
    spread(act * sig(act) * valid, edges[...], buffer, columns, rows)
    out = None
    for tap in range(9):
        part = dot(columns[:, tap * narrow : (tap + 1) * narrow], tap_of(weights, tap))
        out = part if out is None else out + part
    out_ref[...] = out
    sums_ref[0:1, :] = column_sums(out) * valid
    sums_ref[1:2, :] = column_sums(out * out) * valid


def middle_conv(flags, pre, sums, gains, weights, edges):
    rows, narrow = pre.shape
    return call(
        middle_kernel,
        [((rows, narrow), F32), ((2, narrow), F32)],
        (flags, pre, sums, gains, weights, edges),
        scratch=spread_scratch(rows, narrow),
    )


def last_kernel(flags, pre, sums, gains, weights, act_ref, sums_ref):
    valid = flags[0]
    _, act, _ = act_of(flags, pre[...], sums[...], gains[...])
    act_ref[...] = (act * sig(act) * valid).astype(LOW)
    for at in range(0, weights.shape[1], 256):
        out = dot(act_ref[...], weights[:, at : at + 256])
        sums_ref[0:1, at : at + 256] = column_sums(out) * valid
        sums_ref[1:2, at : at + 256] = column_sums(out * out) * valid


def last_conv(flags, pre, sums, gains, weights):
    rows, narrow = pre.shape
    width = weights.shape[1]
    return call(
        last_kernel,
        [((rows, narrow), LOW), ((2, width), F32)],
        (flags, pre, sums, gains, weights),
    )


def residual_tile(flags, act, cells, weights, sums, gains, at):
    mean, scale = moments(sums[:, at : at + 256], flags[3])
    normal = (dot(act[...], weights[:, at : at + 256]) - mean) * scale
    pre = cells[:, at : at + 256].astype(F32) + (
        normal * gains[0:1, at : at + 256] + gains[1:2, at : at + 256]
    )
    return normal, pre, scale


def embed_kernel(flags, act, cells, weights, sums, gains, embed, res_ref, query_ref, pair_ref):
    width = weights.shape[1]
    inner = query_ref.shape[1]
    for at in range(0, width, 256):
        _, pre, _ = residual_tile(flags, act, cells, weights, sums, gains, at)
        res_ref[:, at : at + 256] = (pre * sig(pre) * flags[0]).astype(LOW)
    for at in range(0, inner, 256):
        query_ref[:, at : at + 256] = dot(res_ref[...], embed[:, at : at + 256]).astype(LOW)
    for at in range(0, 2 * inner, 256):
        pair_ref[:, at : at + 256] = dot(
            res_ref[...], embed[:, inner + at : inner + at + 256]
        ).astype(LOW)


def embed_rows(flags, act, cells, weights, sums, gains, embed):
    rows, width = cells.shape
    inner = embed.shape[1] // 3
    return call(
        embed_kernel,
        [((rows, width), LOW), ((rows, inner), LOW), ((rows, 2 * inner), LOW)],
        (flags, act, cells, weights, sums, gains, embed),
        micros=7,
    )


def copies_of(refs, slots, sems):
    return [
        pltpu.make_async_copy(ref, slots.at[index], sems.at[index])
        for index, ref in enumerate(refs)
    ]


def attend_kernel(
    away, count, query, one, two, three, four, out_ref, log_ref, pairs, tails, scores, total, peak, sums, sems
):
    rows, inner = query.shape
    full = rows // 256 * 256
    rest = rows - full
    wide = 4 * rest
    turn = inner**-0.5 * math.log2(math.e)
    blocks = count[0]
    copies = copies_of((one, two, three, four), pairs, sems)
    for copy in copies:
        copy.start()

    @pl.when(blocks == 0)
    def _():
        out_ref[...] = jnp.zeros_like(out_ref)
        if away:
            log_ref[...] = jnp.zeros_like(log_ref)
            log_ref[0:1, :] = jnp.full((1, log_ref.shape[1]), NEG, F32)
        else:
            log_ref[...] = jnp.full_like(log_ref, NEG)

    peak[...] = jnp.full_like(peak, NEG)
    sums[...] = jnp.zeros_like(sums)

    def score(index, _):
        pltpu.make_async_copy(one, pairs.at[index], sems.at[index]).wait()

        @pl.when(index < blocks)
        def _():
            found = dot(query[...], pairs[index, pl.ds(0, full), :inner], NT)
            scores[index] = found
            top = peak[...]
            for at in range(0, full, 128):
                top = jnp.maximum(top, found[:, at : at + 128])
            peak[...] = top

        return 0

    lax.fori_loop(0, 4, score, 0)

    @pl.when(blocks > 0)
    def _():
        for index in range(4):
            tails[pl.ds(index * rest, rest), :] = pairs[index, pl.ds(full, rest), :]
        lane = lax.broadcasted_iota(jnp.int32, (rows, wide), 1)
        end = jnp.where(lane < blocks * rest, dot(query[...], tails[:, :inner], NT), NEG)
        top = jnp.maximum(
            jnp.max(peak[...], axis=1, keepdims=True), jnp.max(end, axis=1, keepdims=True)
        )
        top = top * turn
        lifted = jnp.exp2(end * turn - top)
        end_sum = jnp.sum(lifted, axis=1, keepdims=True)
        total[...] = dot(lifted.astype(LOW), tails[:, inner:])
        peak[...] = jnp.broadcast_to(top, peak.shape)

        def weigh(index, _):
            base = peak[...]
            running = sums[...]
            parts = []
            for at in range(0, full, 128):
                part = jnp.exp2(scores[index, :, at : at + 128] * turn - base)
                running = running + part
                parts.append(part.astype(LOW))
            sums[...] = running
            total[...] += dot(
                jnp.concatenate(parts, axis=1), pairs[index, pl.ds(0, full), inner:]
            )
            return 0

        lax.fori_loop(0, blocks, weigh, 0)
        found = jnp.sum(sums[...], axis=1, keepdims=True) + end_sum
        logs = jnp.broadcast_to(top + jnp.log2(found), peak.shape)
        if away:
            out = total[...] / found
            mean = column_sums(out) * (1.0 / rows)
            out_ref[...] = (out - mean).astype(out_ref.dtype)
            log_ref[...] = row_of(logs, log_ref.shape[1])
            log_ref[1:2, :inner] = mean
        else:
            out_ref[...] = (total[...] / found).astype(out_ref.dtype)
            log_ref[...] = logs


def attend(count, query, blocks, away):
    rows, inner = query.shape
    span = -(-rows // 128) * 128
    full = rows // 256 * 256
    rest = rows - full
    return call(
        functools.partial(attend_kernel, away),
        [((rows, inner), LOW), ((8, span) if away else (rows, 128), F32)],
        (count, query) + tuple(blocks),
        scratch=[
            pltpu.VMEM((4, rows, 2 * inner), LOW),
            pltpu.VMEM((4 * rest, 2 * inner), LOW),
            pltpu.VMEM((4, rows, full), F32),
            pltpu.VMEM((rows, inner), F32),
            pltpu.VMEM((rows, 128), F32),
            pltpu.VMEM((rows, 128), F32),
            pltpu.SemaphoreType.DMA((4,)),
        ],
        vmem=52,
        far=(2, 3, 4, 5),
        micros=10,
    )


def attend_back_kernel(away, held, count, query, grad, *refs):
    size = len(held)
    refs = list(refs)
    if away:
        packed = refs.pop(0)
    else:
        log_ref, term_ref = refs.pop(0), refs.pop(0)
    given_query = refs.pop(0) if away and held[0] == 0 else None
    blocks_in = [refs.pop(0) for _ in held]
    given = [refs.pop(0) for _ in held] if away else None
    query_ref = refs.pop(0)
    outs = [refs.pop(0) for _ in held]
    pairs, tails, stage, total, sems, out_sems = refs[:6]
    if away:
        log_ref, term_ref, in_sems = refs[6:]
    rows, inner = query.shape
    full = rows // 256 * 256
    rest = rows - full
    wide = size * rest
    scaling = inner**-0.5
    turn = scaling * math.log2(math.e)
    blocks = count[0]
    arrivals = copies_of(blocks_in, pairs, sems)
    for copy in arrivals:
        copy.start()
    if away:
        sums_in = copies_of(given, stage, in_sems)
        for copy in sums_in:
            copy.start()
        log_ref[...] = column_of(packed[0:1, :])[:rows]
        term_ref[...] = column_of(packed[1:2, :])[:rows]
    else:
        for index in range(size):

            @pl.when(held[index] >= blocks)
            def _():
                stage[index] = jnp.zeros(stage.shape[1:], LOW)

    for copy in arrivals:
        copy.wait()
    if away:
        for copy in sums_in:
            copy.wait()

    def put(index, at, count_rows, cols, value):
        if away:
            value = value + stage[index, pl.ds(at, count_rows), cols].astype(F32)
        stage[index, pl.ds(at, count_rows), cols] = value.astype(LOW)

    def tile(keys, values, span, mask):
        found = dot(query[...], keys, NT)
        back = dot(grad[...], values, NT)
        logs = log_ref[...]
        terms = term_ref[...]
        kept = []
        slopes = []
        for at in range(0, span, 128):
            end = min(at + 128, span)
            weight = jnp.exp2(found[:, at:end] * turn - logs[:, : end - at])
            if mask is not None:
                weight = jnp.where(mask, weight, 0.0)
            kept.append(weight.astype(LOW))
            slopes.append((weight * (back[:, at:end] - terms[:, : end - at])).astype(LOW))
        kept = kept[0] if len(kept) == 1 else jnp.concatenate(kept, axis=1)
        slopes = slopes[0] if len(slopes) == 1 else jnp.concatenate(slopes, axis=1)
        return slopes, dot(slopes, query[...], TN) * scaling, dot(kept, grad[...], TN)

    active = blocks > held[0]

    @pl.when(jnp.logical_not(active))
    def _():
        if given_query is None:
            query_ref[...] = jnp.zeros_like(query_ref)
        else:
            query_ref[...] = given_query[...].astype(query_ref.dtype)

    @pl.when(active)
    def _():
        for index in range(size):
            tails[pl.ds(index * rest, rest), :] = pairs[index, pl.ds(full, rest), :]
        keys = tails[:, :inner]
        lane = lax.broadcasted_iota(jnp.int32, (rows, wide), 1)
        ok = lane < (blocks - held[0]) * rest
        slopes, key_part, value_part = tile(keys, tails[:, inner:], wide, ok)
        total[...] = dot(slopes, keys)
        for index in range(size):
            span = slice(index * rest, (index + 1) * rest)
            put(index, full, rest, slice(0, inner), key_part[span])
            put(index, full, rest, slice(inner, 2 * inner), value_part[span])

        def one_block(index, _):
            block = pairs[index, pl.ds(0, full), :inner]
            slopes, key_part, value_part = tile(block, pairs[index, pl.ds(0, full), inner:], full, None)
            total[...] += dot(slopes, block)
            put(index, 0, full, slice(0, inner), key_part)
            put(index, 0, full, slice(inner, 2 * inner), value_part)
            return 0

        lax.fori_loop(0, jnp.minimum(blocks - held[0], size), one_block, 0)
        found = total[...] * scaling
        if given_query is not None:
            found = found + given_query[...]
        query_ref[...] = found.astype(query_ref.dtype)

    departures = [
        pltpu.make_async_copy(stage.at[index], ref, out_sems.at[index])
        for index, ref in enumerate(outs)
    ]
    for copy in departures:
        copy.start()
    for copy in departures:
        copy.wait()


def attend_back(count, query, grad, terms, blocks, held, given, given_query, out_type):
    rows, inner = query.shape
    full = rows // 256 * 256
    rest = rows - full
    away = given is not None
    size = len(held)
    more = () if given_query is None else (given_query,)
    near = (count, query, grad) + tuple(terms) + more
    distant = tuple(blocks) + (tuple(given) if away else ())
    scratch = [
        pltpu.VMEM((size, rows, 2 * inner), LOW),
        pltpu.VMEM((size * rest, 2 * inner), LOW),
        pltpu.VMEM((size, rows, 2 * inner), LOW),
        pltpu.VMEM((rows, inner), F32),
        pltpu.SemaphoreType.DMA((size,)),
        pltpu.SemaphoreType.DMA((size,)),
    ]
    if away:
        scratch += [pltpu.VMEM((rows, 128), F32)] * 2 + [pltpu.SemaphoreType.DMA((size,))]
    found = call(
        functools.partial(attend_back_kernel, away, held),
        [((rows, inner), out_type)] + [((rows, 2 * inner), LOW)] * size,
        near + distant,
        scratch=scratch,
        vmem=52,
        far=tuple(range(len(near), len(near) + len(distant))),
        far_out=tuple(range(1, 1 + size)),
        micros=17,
    )
    return found[0], found[1:]


def column_of(row):
    return jnp.transpose(jnp.broadcast_to(row, (128, row.shape[1])))


def row_of(column, span):
    tall = jnp.concatenate([column, jnp.zeros((span - column.shape[0], 128), F32)], axis=0)
    return jnp.transpose(tall)[0:8, :]


def merge_kernel(
    flags, own, own_log, far, far_log, weights, cot, out_ref, log_ref, sums_ref
):
    rows, inner = own.shape
    logs = own_log[...]
    others = column_of(far_log[0:1, :])[:rows]
    top = jnp.maximum(logs, others)
    whole = top + jnp.log2(jnp.exp2(logs - top) + jnp.exp2(others - top))
    log_ref[...] = whole
    share = jnp.exp2(logs - whole)
    other = jnp.exp2(others - whole)
    for at in range(0, inner, 128):
        out_ref[:, at : at + 128] = (
            own[:, at : at + 128].astype(F32) * share + (far[:, at : at + 128].astype(F32) + far_log[1:2, at : at + 128]) * other
        ).astype(LOW)
    valid = flags[0]
    for at in range(0, weights.shape[1], 256):
        out = dot(out_ref[...], weights[:, at : at + 256])
        grad = cot[:, at : at + 256].astype(F32)
        sums_ref[0:1, at : at + 256] = column_sums(out) * valid
        sums_ref[1:2, at : at + 256] = column_sums(out * out) * valid
        sums_ref[2:3, at : at + 256] = column_sums(grad) * valid
        sums_ref[3:4, at : at + 256] = column_sums(grad * out) * valid
    sums_ref[4:5, :] = jnp.zeros((1, weights.shape[1]), F32)
    sums_ref[4:5, :inner] = column_sums(out_ref[...].astype(F32)) * valid


def merge(flags, own, own_log, far, far_log, weights, cot):
    rows, inner = own.shape
    width = weights.shape[1]
    return call(
        merge_kernel,
        [((rows, inner), LOW), ((rows, 128), F32), ((5, width), F32)],
        (flags, own, own_log, far, far_log, weights, cot),
    )


def outer_kernel(
    flags,
    att,
    weights,
    sums,
    gains,
    cot,
    res,
    logs,
    mixed_ref,
    grad_ref,
    back_ref,
    term_ref,
    rows_ref,
    norm_ref,
):
    valid = flags[0]
    inverse = flags[3]
    width = weights.shape[1]
    for at in range(0, width, 256):
        span = slice(at, at + 256)
        mean, scale = moments(sums[0:2, span], inverse)
        normal = (dot(att[...], weights[:, span]) - mean) * scale
        gain = gains[0:1, span]
        mixed_ref[:, span] = (
            (res[:, span].astype(F32) + (normal * gain + gains[1:2, span])) * valid
        ).astype(LOW)
        shift_grad = sums[2:3, span]
        gain_grad = scale * (sums[3:4, span] - mean * shift_grad)
        norm_ref[0:1, span] = gain_grad
        norm_ref[1:2, span] = shift_grad
        removed = (shift_grad + normal * gain_grad) * inverse
        grad = ((gain * scale * valid) * (cot[:, span].astype(F32) - removed)).astype(LOW)
        grad_ref[:, span] = grad
        norm_ref[2:3, span] = column_sums(grad.astype(F32))
    back = dot(grad_ref[...], weights[...], NT).astype(LOW)
    back_ref[...] = back
    term = jnp.sum(back.astype(F32) * att[...].astype(F32), axis=1, keepdims=True)
    term = jnp.broadcast_to(term, term_ref.shape)
    term_ref[...] = term
    rows_ref[...] = row_of(logs[...], rows_ref.shape[1])
    rows_ref[1:2, :] = row_of(term, rows_ref.shape[1])[0:1]


def outer(flags, att, weights, sums, gains, cot, res, logs):
    rows, inner = att.shape
    width = weights.shape[1]
    span = -(-rows // 128) * 128
    return call(
        outer_kernel,
        [
            ((rows, width), LOW),
            ((rows, width), LOW),
            ((rows, inner), LOW),
            ((rows, 128), F32),
            ((8, span), F32),
            ((3, width), F32),
        ],
        (flags, att, weights, sums, gains, cot, res, logs),
        micros=5,
    )


def project_kernel(
    flags,
    query_own,
    query_far,
    keep,
    near,
    far,
    act,
    cells,
    weights,
    sums,
    gains,
    embed,
    cot,
    proj_ref,
    pre_ref,
    sums_ref,
):
    valid = flags[0]
    inner = query_own.shape[1]
    proj_ref[:, :inner] = (query_own[...].astype(F32) + query_far[...].astype(F32)).astype(LOW)
    for at in range(0, 2 * inner, 256):
        span = slice(at, at + 256)
        proj_ref[:, inner + at : inner + at + 256] = (
            keep[:, span].astype(F32) + near[:, span].astype(F32) + far[:, span].astype(F32)
        ).astype(LOW)
    for at in range(0, weights.shape[1], 256):
        span = slice(at, at + 256)
        normal, pre, _ = residual_tile(flags, act, cells, weights, sums, gains, at)
        grad = cot[:, span].astype(F32) + dot(proj_ref[...], embed[span, :], NT)
        out = grad * valid * slope(pre)
        pre_ref[:, span] = out
        sums_ref[0:1, span] = column_sums(out)
        sums_ref[1:2, span] = column_sums(out * normal)


def project_back(flags, query_own, query_far, keep, near, far, act, cells, weights, sums, gains, embed, cot):
    rows, width = cells.shape
    inner = query_own.shape[1]
    return call(
        project_kernel,
        [((rows, 3 * inner), LOW), ((rows, width), F32), ((2, width), F32)],
        (flags, query_own, query_far, keep, near, far, act, cells, weights, sums, gains, embed, cot),
        micros=10,
    )


def last_back_kernel(
    flags, pre_grad, act, weights, sums, gains, back_sums, pre_two, sums_two, gains_two, grad_ref, two_ref, sums_ref
):
    valid = flags[0]
    inverse = flags[3]
    two = None
    for at in range(0, weights.shape[1], 256):
        span = slice(at, at + 256)
        mean, scale = moments(sums[:, span], inverse)
        normal = (dot(act[...], weights[:, span]) - mean) * scale
        removed = (back_sums[0:1, span] + normal * back_sums[1:2, span]) * inverse
        grad = ((gains[0:1, span] * scale * valid) * (pre_grad[:, span] - removed)).astype(LOW)
        grad_ref[:, span] = grad
        part = dot(grad, weights[:, span], NT)
        two = part if two is None else two + part
    normal, active, _ = act_of(flags, pre_two[...], sums_two[...], gains_two[...])
    two = two * valid * slope(active)
    two_ref[...] = two
    sums_ref[0:1, :] = column_sums(two)
    sums_ref[1:2, :] = column_sums(two * normal)


def last_back(flags, pre_grad, act, weights, sums, gains, back_sums, pre_two, sums_two, gains_two):
    rows, width = pre_grad.shape
    narrow = act.shape[1]
    return call(
        last_back_kernel,
        [((rows, width), LOW), ((rows, narrow), F32), ((2, narrow), F32)],
        (flags, pre_grad, act, weights, sums, gains, back_sums, pre_two, sums_two, gains_two),
    )


def middle_back_kernel(
    flags, two, back_sums, pre_two, sums_two, gains_two, pre_one, sums_one, gains_one, weights, edges,
    grad_ref, one_ref, sums_ref, buffer, columns
):
    rows, narrow = two.shape
    valid = flags[0]
    inverse = flags[3]
    normal, _, scale = act_of(flags, pre_two[...], sums_two[...], gains_two[...])
    removed = (back_sums[0:1] + normal * back_sums[1:2]) * inverse
    grad = (gains_two[0:1, :] * scale * valid) * (two[...] - removed)
    grad_ref[...] = grad.astype(LOW)
    spread(grad, edges[...], buffer, columns, rows)
    one = None
    for tap in range(9):
        part = dot(columns[:, tap * narrow : (tap + 1) * narrow], tap_of(weights, 8 - tap), NT)
        one = part if one is None else one + part
    normal, active, _ = act_of(flags, pre_one[...], sums_one[...], gains_one[...])
    one = one * valid * slope(active)
    one_ref[...] = one
    sums_ref[0:1, :] = column_sums(one)
    sums_ref[1:2, :] = column_sums(one * normal)


def middle_back(flags, two, back_sums, pre_two, sums_two, gains_two, pre_one, sums_one, gains_one, weights, edges):
    rows, narrow = two.shape
    return call(
        middle_back_kernel,
        [((rows, narrow), LOW), ((rows, narrow), F32), ((2, narrow), F32)],
        (flags, two, back_sums, pre_two, sums_two, gains_two, pre_one, sums_one, gains_one, weights, edges),
        scratch=spread_scratch(rows, narrow),
    )


def middle_weight_kernel(flags, pre_one, sums_one, gains_one, grad, edges, out_ref, buffer, columns):
    rows, narrow = pre_one.shape
    _, act, _ = act_of(flags, pre_one[...], sums_one[...], gains_one[...])
    spread(act * sig(act) * flags[0], edges[...], buffer, columns, rows)
    for tap in range(9):
        out_ref[pl.ds(tap * narrow, narrow), :] = dot(
            columns[:, tap * narrow : (tap + 1) * narrow], grad[...], TN
        ).astype(LOW)


def middle_weight(flags, pre_one, sums_one, gains_one, grad, edges):
    rows, narrow = pre_one.shape
    return call(
        middle_weight_kernel,
        [((9 * narrow, narrow), LOW)],
        (flags, pre_one, sums_one, gains_one, grad, edges),
        scratch=spread_scratch(rows, narrow),
    )[0]


def first_grad_kernel(flags, one, back_sums, pre_one, sums_one, gains_one, grad_ref):
    normal, _, scale = act_of(flags, pre_one[...], sums_one[...], gains_one[...])
    removed = (back_sums[0:1] + normal * back_sums[1:2]) * flags[3]
    grad_ref[...] = (
        (gains_one[0:1, :] * scale * flags[0]) * (one[...] - removed)
    ).astype(LOW)


def first_grad_of(flags, one, back_sums, pre_one, sums_one, gains_one):
    rows, narrow = one.shape
    return call(
        first_grad_kernel,
        [((rows, narrow), LOW)],
        (flags, one, back_sums, pre_one, sums_one, gains_one),
    )[0]


def first_back_kernel(flags, grad, before, after, cells, middle, last, local_ref, cols_ref, buffer):
    rows, narrow = grad.shape
    width = cells.shape[1]
    spots = before.shape[0]
    buffer[pl.ds(0, spots), :] = before[...].astype(F32) * flags[1]
    buffer[pl.ds(spots, rows), :] = grad[...].astype(F32)
    buffer[pl.ds(spots + rows, spots), :] = after[...].astype(F32) * flags[2]
    at = middle.shape[0]
    local_ref[pl.ds(0, at), :] = middle[...]
    for tap in range(3):
        part = (buffer[pl.ds(spots * (2 - tap), rows), :] * flags[0]).astype(LOW)
        cols_ref[:, tap * narrow : (tap + 1) * narrow] = part
        local_ref[pl.ds(at, width), :] = dot(cells[...], part, TN).astype(LOW)
        at += width
    local_ref[pl.ds(at, last.shape[0]), :] = last[...]


def first_back(flags, grad, before, after, cells, middle, last):
    rows, narrow = grad.shape
    spots = before.shape[0]
    width = cells.shape[1]
    return call(
        first_back_kernel,
        [((middle.shape[0] + 3 * width + last.shape[0], narrow), LOW), ((rows, 3 * narrow), LOW)],
        (flags, grad, before, after, cells, middle, last),
        scratch=[pltpu.VMEM((rows + 2 * spots, narrow), F32)],
    )


def early_weight_kernel(flags, res, proj, att, sums, grad, out_ref):
    height, inner = res.shape[1], att.shape[1]
    left = (att[...].astype(F32) - sums[...] * flags[3]).astype(LOW)
    at = 0
    for index in range(proj.shape[1] // 256):
        out_ref[pl.ds(at, height), :] = dot(
            res[...], proj[:, index * 256 : (index + 1) * 256], TN
        ).astype(LOW)
        at += height
    for index in range(grad.shape[1] // 256):
        out_ref[pl.ds(at, inner), :] = dot(
            left, grad[:, index * 256 : (index + 1) * 256], TN
        ).astype(LOW)
        at += inner


def early_weight(flags, res, proj, att, sums, grad):
    height = res.shape[1] * proj.shape[1] // 256 + att.shape[1] * grad.shape[1] // 256
    return call(
        early_weight_kernel, [((height, 256), LOW)], (flags, res, proj, att, sums, grad),
        micros=8,
    )[0]


def weight_kernel(left, right, out_ref):
    height = left.shape[1]
    for index in range(right.shape[1] // 256):
        out_ref[pl.ds(index * height, height), :] = dot(
            left[...], right[:, index * 256 : (index + 1) * 256], TN
        ).astype(LOW)


def weight_grad(left, right):
    rows, height = left.shape
    width = right.shape[1]
    return call(
        weight_kernel,
        [((height * width // 256, 256), LOW)],
        (left, right),
        scalars=0,
    )[0]


def pieces_of(low_half, high_half, start, stop):
    middle = low_half.shape[0]
    if start < middle:
        yield 0, low_half[pl.ds(start, min(stop, middle) - start), :]
    if stop > middle:
        begin = max(start, middle)
        yield begin - start, high_half[pl.ds(begin - middle, stop - begin), :]


def squares_of(values):
    return jnp.sum((values * values).reshape(-1, 8, values.shape[-1]), axis=0)


def emit(place, half, other, shares, squares):
    def write(low_half, high_half):
        squares[...] = jnp.zeros_like(squares)
        for start, stop, store, extra in shares:
            for offset, rows in pieces_of(low_half, high_half, start, stop):
                values = rows.astype(F32)
                if extra is not None:
                    values = values + extra[offset : offset + values.shape[0]]
                squares[...] += squares_of(values)
                store(offset, values)

    @pl.when(place[0] == 0)
    def _():
        write(half, other)

    @pl.when(place[0] == 1)
    def _():
        write(other, half)


def store_rows(ref, lead, cols):
    def store(offset, values):
        ref[lead + (pl.ds(offset, values.shape[0]), cols)] = values

    return store


def early_shares(embed_ref, back_ref, mean, grad_sum):
    width, inner = embed_ref.shape[1], embed_ref.shape[2]
    shares = []
    at = 0
    for index in range(3 * inner // 256):
        part, col = divmod(index * 256, inner)
        shares.append((at, at + width, store_rows(embed_ref, (part,), slice(col, col + 256)), None))
        at += width
    for index in range(width // 256):
        cols = slice(index * 256, index * 256 + 256)
        extra = mean[:, 0:1] * grad_sum[0:1, cols]
        shares.append((at, at + inner, store_rows(back_ref, (), cols), extra))
        at += inner
    return shares


def early_kernel(place, flags, half, other, sums, grad_sum, embed_ref, back_ref, embed_own, back_own, squares_ref):
    mean = sums[...] * flags[3]
    emit(place, half, other, early_shares(embed_ref, back_ref, column_of(mean), grad_sum), squares_ref)
    span = embed_own.shape[1]
    embed_own[...] = embed_ref[:, pl.ds(pl.multiple_of(place[1] * span, span), span), :]
    span = back_own.shape[0]
    back_own[...] = back_ref[pl.ds(pl.multiple_of(place[1] * span, span), span), :]


def early_grads(place, flags, half, other, sums, grad_sum, width, inner, shards):
    return call(
        early_kernel,
        [
            ((3, width, inner), F32),
            ((inner, width), F32),
            ((3, width // shards, inner), F32),
            ((inner // shards, width), F32),
            ((8, 256), F32),
        ],
        (place, flags, half, other, sums, grad_sum),
        scalars=2,
        micros=6,
    )


def late_shares(first_ref, middle_ref, last_ref):
    shares = []
    at = 0
    for ref in (middle_ref, first_ref):
        for index in range(ref.shape[0]):
            shares.append((at, at + ref.shape[1], store_rows(ref, (index,), slice(None)), None))
            at += ref.shape[1]
    for index in range(last_ref.shape[1] // 256):
        cols = slice(index * 256, index * 256 + 256)
        shares.append((at, at + last_ref.shape[0], store_rows(last_ref, (), cols), None))
        at += last_ref.shape[0]
    return shares


def late_kernel(rates, place, half, other, squares, extra, embed_own, back_own, *refs):
    given = [refs[3 * index : 3 * index + 3] for index in range(5)]
    first_ref, middle_ref, last_ref, norm_ref = refs[15:19]
    made = [refs[19 + 3 * index : 22 + 3 * index] for index in range(5)]
    tally = refs[34]
    emit(place, half, other, late_shares(first_ref, middle_ref, last_ref), tally)
    found = jnp.sum(tally[...] + squares[...], axis=0, keepdims=True)
    norm = jnp.sqrt(jnp.sum(found, axis=1, keepdims=True) + extra[0:1, 0:1])
    factor = jnp.minimum(1.0, CLIP_AT / (norm + 1e-06))
    norm_ref[0:1, :] = jnp.broadcast_to(norm, (1, 128))
    norm_ref[1:2, :] = jnp.broadcast_to(factor, (1, 128))

    def mine(span):
        return pl.ds(pl.multiple_of(place[1] * span, span), span)

    def own(index, part):
        if index == 0:
            return first_ref[part, mine(given[0][0].shape[1]), :]
        if index == 1:
            return middle_ref[part, mine(given[1][0].shape[1]), :]
        if index == 2:
            return last_ref[mine(given[2][0].shape[0]), :]
        return embed_own[part] if index == 3 else back_own[...]

    for index in range(5):
        master, moment, second = given[index]
        outs = made[index]
        for part in range(master.shape[0]) if len(master.shape) == 3 else (slice(None),):
            values = adam_step(
                master[part], own(index, part), moment[part], second[part], factor, rates[index]
            )
            for ref, value in zip(outs, values):
                ref[part] = value


def late_grads(rates, place, half, other, squares, extra, embed_own, back_own, states, shapes):
    flat = tuple(item for state in states for item in state)
    outs = [(shape, F32) for shape in shapes] + [((2, 128), F32)]
    outs += [(state[0].shape, F32) for state in states for _ in range(3)]
    found = call(
        functools.partial(late_kernel, rates),
        outs,
        (place, half, other, squares, extra, embed_own, back_own) + flat,
        scratch=[pltpu.VMEM((8, 256), F32)],
        micros=8,
    )
    return found[:3], found[3], [found[4 + 3 * index : 7 + 3 * index] for index in range(5)]


def unfold(value, height):
    return jnp.moveaxis(value.reshape(-1, height, 256), 0, 1).reshape(height, -1)


def plain_tail(early, late, mean, grad_sum, sizes, norm_square, states, rates, chan_at):
    width, inner, narrow = sizes
    core = chan_at & 1
    early, late = [
        jnp.where(core == 0, jnp.concatenate([half, other]), jnp.concatenate([other, half])).astype(
            F32
        )
        for half, other in (early, late)
    ]
    cut = 3 * inner * width // 256
    embed = unfold(early[:cut], width).reshape(width, 3, inner)
    back = unfold(early[cut:], inner) + mean[:, None] * grad_sum[None, :]
    middle = late[: 9 * narrow].reshape(9, narrow, narrow)
    first = late[9 * narrow : 9 * narrow + 3 * width].reshape(3, width, narrow)
    last = unfold(late[9 * narrow + 3 * width :], narrow)
    grads = (first, middle, last, jnp.moveaxis(embed, 1, 0), back)
    norm = jnp.sqrt(sum(jnp.sum(item * item) for item in grads) + norm_square)
    factor = jnp.minimum(1.0, CLIP_AT / (norm + 1e-06))
    made = []
    for grad, state, rate in zip(grads, states, rates):
        axis = grad.ndim - 2
        span = state[0].shape[axis]
        owned = lax.dynamic_slice_in_dim(grad, chan_at * span, span, axis)
        made.append(adam_step(state[0], owned, state[1], state[2], factor, rate))
    return grads, norm, factor, made


def input_kernel(cols, weights, pre_grad, out_ref):
    shards, _, span, narrow = weights.shape
    each = 256 // span
    for at in range(0, pre_grad.shape[1], 256):
        out = pre_grad[:, at : at + 256]
        begin = at // span
        for tap in range(3):
            rows = weights[pl.ds(begin, each), tap].reshape(256, narrow)
            out = out + dot(cols[:, tap * narrow : (tap + 1) * narrow], rows, NT)
        span_at = slice(at, at + 256)
        out_ref[:, span_at] = out.astype(LOW)


def input_grad(cols, weights, pre_grad):
    rows, width = pre_grad.shape
    return call(
        input_kernel,
        [((rows, width), LOW)],
        (cols, weights, pre_grad),
        scalars=0,
    )[0]


def adam_step(master, gradient, moment, second, factor, rate):
    clipped = gradient * factor
    moment_new = BETA_ONE * moment + (1.0 - BETA_ONE) * clipped
    second_new = BETA_TWO * second + (1.0 - BETA_TWO) * clipped * clipped
    moment_hat = moment_new / (1.0 - BETA_ONE**STEP)
    second_hat = second_new / (1.0 - BETA_TWO**STEP)
    master_new = master - rate * (
        moment_hat / (jnp.sqrt(second_hat) + ADAM_EPS) + WEIGHT_DECAY * master
    )
    return (moment_new, second_new, master_new)


def body(
    features,
    cotangent,
    frame_counts,
    weight_first,
    weight_middle,
    weight_last,
    weight_embed,
    weight_back,
    norm_params,
    moment_first,
    moment_middle,
    moment_last,
    moment_embed,
    moment_back,
    moment_norm,
    second_first,
    second_middle,
    second_last,
    second_embed,
    second_back,
    second_norm,
):
    chan_at = lax.axis_index("chan")
    device = lax.axis_index("clip") * lax.axis_size("chan") + chan_at
    frames, spot_count, model_width = features.shape
    row_count = frames * spot_count
    narrow = BOT
    inner_width = INNER
    clip_place = chan_at % DPC
    clip_at = device // DPC
    clip_ids = jnp.arange(frame_counts.shape[0], dtype=jnp.int32)
    length = jnp.sum(jnp.where(clip_ids == clip_at, frame_counts, 0))

    def valid_at(place):
        return ((place >= 0) & (place < DPC) & (place * frames < length)).astype(jnp.float32)

    own_ok = valid_at(clip_place)
    row_total = jnp.sum(frame_counts).astype(jnp.float32) * spot_count
    zero = jnp.zeros((), jnp.float32)
    flags = jnp.stack(
        [own_ok, valid_at(clip_place - 1), valid_at(clip_place + 1), 1.0 / row_total]
        + [valid_at(clip_place ^ 2)] + [zero] * 3
    )
    held = sum(valid_at(clip_place ^ turn) for turn in range(4)) * own_ok
    blocks_own = held.astype(jnp.int32).reshape(1)
    blocks_far = (held * valid_at(clip_place ^ 4)).astype(jnp.int32).reshape(1)
    span_list = [narrow] * 4 + [model_width] * 4
    starts = [sum(span_list[:index]) for index in range(8)]
    gains_one, gains_two, gains_three, gains_four = [
        norm_params[starts[index] : starts[index] + 2 * span_list[index]].reshape(2, -1)
        for index in range(0, 8, 2)
    ]
    shards = lax.axis_size("chan")
    first_low = whole_of(weight_first)
    tall = weight_middle.shape[0] * weight_middle.shape[1]
    packed = jnp.concatenate(
        [
            weight_middle.reshape(tall, narrow),
            jnp.moveaxis(weight_last.reshape(-1, model_width // 256, 256), 1, 0).reshape(-1, 256),
        ]
    ).astype(LOW)
    packed = lax.all_gather(packed, "chan", axis=0, tiled=False)
    middle_low = packed[:, :tall].reshape((shards,) + weight_middle.shape)
    last_low = jnp.moveaxis(
        packed[:, tall:].reshape(shards, model_width // 256, -1, 256), 1, 2
    ).reshape(narrow, model_width)
    if weight_middle.shape[1] % 16:
        middle_low = jnp.moveaxis(middle_low, 0, 1).reshape(1, 9, narrow, narrow)
    embed_low, back_low = (
        lax.all_gather(weight_embed.astype(LOW).reshape(-1, 3 * inner_width), "chan", axis=0, tiled=True),
        lax.all_gather(weight_back.astype(LOW), "chan", axis=0, tiled=True),
    )
    place = np.arange(row_count)
    across, down = place % WW, place // WW % HH
    edges = jnp.asarray(
        np.stack([across > 0, across < WW - 1, down > 0, down < HH - 1] + [across < 0] * 4, axis=1)
        .astype(np.float32)
    )
    cells = features.reshape(row_count, model_width)
    cot = cotangent.reshape(row_count, model_width)
    before, after = beside(features, spot_count)
    pre_one, sums_one = first_conv(flags, cells, before, after, first_low)
    sums_one = total(sums_one)
    pre_two, sums_two = middle_conv(
        flags, pre_one, sums_one, gains_one, middle_low, edges
    )
    sums_two = total(sums_two)
    act_two, sums_three = last_conv(flags, pre_two, sums_two, gains_two, last_low)
    sums_three = total(sums_three)
    residual_low, query, pair_own = embed_rows(
        flags, act_two, cells, last_low, sums_three, gains_three, embed_low
    )
    pair_core = flipped(pair_own, "chan", 1)
    query_far, pair_far = flipped(query, "chan", 4), flipped(pair_own, "chan", 2)
    query_far, pair_far = lax.optimization_barrier((query_far, pair_far))
    blocks = (pair_own, pair_core, pair_far, flipped(pair_far, "chan", 1))
    part_far, log_far = attend(blocks_far, query_far, blocks, True)
    part_far = flipped(part_far, "chan", 4)
    log_far = flipped(log_far, "chan", 4)
    part_own, log_own = attend(blocks_own, query, blocks, False)
    attended, logs, sums_four = merge(flags, part_own, log_own, part_far, log_far, back_low, cot)
    sums_four = total(sums_four)
    mixed, attn_grad, attended_grad, terms, packed, norm_four = outer(
        flags, attended, back_low, sums_four, gains_four, cot, residual_low, logs
    )
    mixed = laid_out(mixed, frames)
    attended_grad_far = flipped(attended_grad, "chan", 4)
    packed_far = flipped(packed, "chan", 4)
    query_own, held = attend_back(
        blocks_own, query, attended_grad, (logs, terms), blocks, (0, 1, 2, 3), None, None, F32
    )
    query_part, (far, far_core) = attend_back(
        blocks_far, query_far, attended_grad_far, (packed_far,), blocks[2:], (2, 3), held[2:], None, F32
    )
    far = flipped(
        (far.astype(F32) + flipped(far_core, "chan", 1).astype(F32)).astype(LOW), "chan", 2
    )
    query_part, (keep, give) = attend_back(
        blocks_far, query_far, attended_grad_far, (packed_far,), blocks[:2], (0, 1), held[:2],
        query_part, LOW,
    )
    query_part = flipped(query_part, "chan", 4)
    near = flipped(give, "chan", 1)
    projected_grad, pre_grad, back_three = project_back(
        flags, query_own, query_part, keep, near, far, act_two, cells, last_low, sums_three,
        gains_three, embed_low, cot,
    )
    early = early_weight(
        flags, residual_low, projected_grad, attended, sums_four[4:5, :inner_width], attn_grad
    )
    back_three = jnp.concatenate([back_three, norm_four[2:3]])
    early, back_three = tied(early, back_three)
    back_three = total(back_three)
    last_grad, two_grad, back_two = last_back(
        flags, pre_grad, act_two, last_low, sums_three, gains_three, back_three, pre_two, sums_two,
        gains_two,
    )
    back_two = total(back_two)
    last_local = weight_grad(act_two, last_grad)
    middle_grad, one_grad, back_one = middle_back(
        flags, two_grad, back_two, pre_two, sums_two, gains_two, pre_one, sums_one, gains_one,
        middle_low, edges,
    )
    back_one = total(back_one)
    middle_local = middle_weight(flags, pre_one, sums_one, gains_one, middle_grad, edges)
    first_grad = first_grad_of(flags, one_grad, back_one, pre_one, sums_one, gains_one)
    before, after = beside(first_grad.reshape(frames, spot_count, narrow), spot_count)
    late, grad_cols = first_back(flags, first_grad, before, after, cells, middle_local, last_local)
    features_gradient = laid_out(input_grad(grad_cols, first_low, pre_grad), frames)
    gain_one_grad, shift_one_grad = back_one[1], back_one[0]
    gain_two_grad, shift_two_grad = back_two[1], back_two[0]
    gain_three_grad, shift_three_grad = back_three[1], back_three[0]
    gain_four_grad, shift_four_grad = norm_four[0], norm_four[1]
    norm_gradient = jnp.concatenate(
        [
            gain_one_grad,
            shift_one_grad,
            gain_two_grad,
            shift_two_grad,
            gain_three_grad,
            shift_three_grad,
            gain_four_grad,
            shift_four_grad,
        ]
    )
    groups = [list(range(core, shards, 2)) for core in range(2)]
    early = lax.psum_scatter(core_step(early), "clip", scatter_dimension=0, tiled=True)
    early = lax.psum(early, "chan", axis_index_groups=groups)
    late = scatter_sum(core_step(late))
    early, late = tied(early, late)
    early = lax.all_gather(early, "clip", axis=0, tiled=True)
    late = gather_sum(late)
    early, late, mixed, features_gradient = tied(early, late, mixed, features_gradient)
    early = (early, flipped(early, "chan", 1))
    late = (late, flipped(late, "chan", 1))
    fans = (3 * D, 9 * BOT, BOT, D, INNER)
    rates = tuple(0.5 * fan ** (-0.5) for fan in fans)
    states = (
        (weight_first, moment_first, second_first),
        (weight_middle, moment_middle, second_middle),
        (weight_last, moment_last, second_last),
        tuple(jnp.moveaxis(item, 1, 0) for item in (weight_embed, moment_embed, second_embed)),
        (weight_back, moment_back, second_back),
    )
    norm_square = jnp.sum(norm_gradient * norm_gradient)
    if weight_middle.shape[1] % 16 == 0:
        place = jnp.stack([chan_at & 1, chan_at]).astype(jnp.int32)
        embed, back, embed_own, back_own, squares = early_grads(
            place,
            flags,
            *early,
            sums_four[4:5, :inner_width],
            back_three[2:3],
            model_width,
            inner_width,
            shards,
        )
        shapes = ((3, model_width, narrow), (9, narrow, narrow), (narrow, model_width))
        (first, middle, last), norm_row, results = late_grads(
            rates, place, *late, squares, norm_square.reshape(1, 1), embed_own, back_own, states, shapes
        )
        gradient_norm, factor = norm_row[0, 0], norm_row[1, 0]
    else:
        (first, middle, last, embed, back), gradient_norm, factor, results = plain_tail(
            early,
            late,
            sums_four[4, :inner_width] * flags[3],
            back_three[2],
            (model_width, inner_width, narrow), norm_square, states, rates, chan_at
        )
    results = list(results)
    results[3] = tuple(jnp.moveaxis(item, 0, 1) for item in results[3])
    results.append(adam_step(norm_params, norm_gradient, moment_norm, second_norm, factor, GAIN_RATE))
    return (
        mixed,
        features_gradient,
        first,
        middle,
        last,
        jnp.moveaxis(embed, 0, 1),
        back,
        norm_gradient,
    ) + tuple(results[index][kind] for kind in range(3) for index in range(6)) + (gradient_norm,)


def solution(mesh):
    placed = (
        P(("clip", "chan"), None, None),
        P(("clip", "chan"), None, None),
        P(),
        P(None, "chan", None),
        P(None, "chan", None),
        P("chan", None),
        P("chan", None, None),
        P("chan", None),
        P(),
        P(None, "chan", None),
        P(None, "chan", None),
        P("chan", None),
        P("chan", None, None),
        P("chan", None),
        P(),
        P(None, "chan", None),
        P(None, "chan", None),
        P("chan", None),
        P("chan", None, None),
        P("chan", None),
        P(),
    )
    return jax.shard_map(
        body,
        mesh=mesh,
        in_specs=placed,
        out_specs=(
            P(("clip", "chan"), None, None),
            P(("clip", "chan"), None, None),
            P(),
            P(),
            P(),
            P(),
            P(),
            P(),
            P(None, "chan", None),
            P(None, "chan", None),
            P("chan", None),
            P("chan", None, None),
            P("chan", None),
            P(),
            P(None, "chan", None),
            P(None, "chan", None),
            P("chan", None),
            P("chan", None, None),
            P("chan", None),
            P(),
            P(None, "chan", None),
            P(None, "chan", None),
            P("chan", None),
            P("chan", None, None),
            P("chan", None),
            P(),
            P(),
        ),
        check_vma=False,
    )
```

```python
import functools
import math

import jax
import jax.numpy as jnp
import numpy as np
from jax import lax
from jax.experimental import pallas as pl
from jax.experimental.layout import Layout, with_layout_constraint
from jax.experimental.pallas import tpu as pltpu
from jax.sharding import PartitionSpec as P

D = 1024
BOT = 256
INNER = 512
HH = 14
WW = 14
STEP = 10
DPC = 8


EPS_NORM = 1e-05
BETA_ONE = 0.9
BETA_TWO = 0.95
ADAM_EPS = 1e-08
WEIGHT_DECAY = 0.01
CLIP_AT = 1.0
GAIN_RATE = 0.5


def flipped(value, axis, mask):
    pairs = [(source, source ^ mask) for source in range(lax.axis_size(axis))]
    return lax.ppermute(value, axis, pairs)


def whole_of(shard):
    return lax.all_gather(shard.astype(jnp.bfloat16), "chan", axis=0, tiled=False)


def tap_of(weights, tap):
    return weights[:, tap].reshape(weights.shape[0] * weights.shape[2], weights.shape[3])


def beside(cells, spots):
    ends = lax.axis_size("chan") - 1
    upward = [(index, index + 1) for index in range(ends)]
    downward = [(index + 1, index) for index in range(ends)]
    return (
        lax.ppermute(cells[-1:], "chan", upward).reshape(spots, cells.shape[-1]),
        lax.ppermute(cells[:1], "chan", downward).reshape(spots, cells.shape[-1]),
    )


def total(value):
    for axis in ("chan", "clip"):
        bits = lax.axis_size(axis).bit_length() - 1
        levels = list(range(bits))
        groups = [levels[:1]] if axis == "chan" else []
        rest = levels[len(groups) :]
        groups += [rest[index : index + 2] for index in range(0, len(rest), 2)]
        for group in groups:
            base = 1 << group[0]
            parts = [flipped(value, axis, base * turn) for turn in range(1, 1 << len(group))]
            value = value + sum(parts[1:], parts[0])
    return value


def level_groups(axis):
    bits = lax.axis_size(axis).bit_length() - 1
    levels = list(range(bits))
    groups = [levels[:1]] if axis == "chan" else []
    rest = levels[len(groups) :]
    return groups + [rest[index : index + 2] for index in range(0, len(rest), 2)]


def level_steps():
    order = [("chan", group) for group in level_groups("chan")]
    order = order[:1] + [("clip", group) for group in level_groups("clip")] + order[1:]
    steps = []
    for axis, group in order:
        base, count = 1 << group[0], 1 << len(group)
        steps.append((axis, base, count, (lax.axis_index(axis) >> group[0]) & (count - 1)))
    return steps


def half_kernel(mine, arrived, out_ref):
    out_ref[...] = (mine[...].astype(F32) + arrived[...].astype(F32)).astype(LOW)


def core_step(mine, others):
    arrived = flipped(others, "chan", 1)
    return call(half_kernel, [(mine.shape, LOW)], (mine, arrived), scalars=0)[0]


def deal(place, halves, mine, others, sems):
    copies = [
        pltpu.make_async_copy(halves.at[place[0]], mine, sems.at[0]),
        pltpu.make_async_copy(halves.at[1 - place[0]], others, sems.at[1]),
    ]
    for copy in copies:
        copy.start()
    for copy in copies:
        copy.wait()


def put_rows(halves, at, values):
    size = halves.shape[1]
    cut = max(0, min(values.shape[0], size - at))
    if cut:
        halves[0, pl.ds(at, cut), :] = values[:cut]
    if cut < values.shape[0]:
        halves[1, pl.ds(at + cut - size, values.shape[0] - cut), :] = values[cut:]


def scatter_sum(value, steps):
    for axis, base, count, place in steps:
        size = value.shape[0] // count
        mine = lax.dynamic_slice_in_dim(value, place * size, size).astype(F32)
        arrived = [
            flipped(
                lax.dynamic_slice_in_dim(value, (place ^ turn) * size, size), axis, base * turn
            )
            for turn in range(1, count)
        ]
        for item in arrived:
            mine = mine + item.astype(F32)
        value = mine.astype(LOW)
    return value


def laid_out(rows, frames):
    grid = rows.reshape(frames, -1, rows.shape[1])
    return with_layout_constraint(grid, Layout(major_to_minor=(1, 0, 2)))


def tied(*values):
    return lax.optimization_barrier(values)


def gather_sum(value, steps):
    for axis, base, count, place in reversed(steps):
        size = value.shape[0]
        parts = [value] + [flipped(value, axis, base * turn) for turn in range(1, count)]
        whole = jnp.zeros((count,) + value.shape, LOW)
        for turn, part in enumerate(parts):
            whole = lax.dynamic_update_index_in_dim(whole, part, place ^ turn, 0)
        value = whole.reshape((count * size,) + value.shape[1:])
    return value


NEG = -1e30
MIB = 1 << 20
NN = (((1,), (0,)), ((), ()))
NT = (((1,), (1,)), ((), ()))
TN = (((0,), (0,)), ((), ()))
F32 = jnp.float32
LOW = jnp.bfloat16


def dot(left, right, dims=NN):
    return lax.dot_general(left, right, dims, preferred_element_type=F32)


def sig(values):
    return 0.5 * jnp.tanh(0.5 * values) + 0.5


def slope(values):
    gate = sig(values)
    return gate * (1.0 + values * (1.0 - gate))


def moments(sums, inverse):
    mean = sums[0:1] * inverse
    return mean, lax.rsqrt(sums[1:2] * inverse - mean * mean + EPS_NORM)


def column_sums(values):
    return jnp.sum(values, axis=0, keepdims=True)


def call(kernel, outs, args, scalars=1, scratch=(), vmem=16, far=(), far_out=(), micros=2):
    spaces = []
    for index in range(len(args)):
        if index < scalars:
            spaces.append(pl.BlockSpec(memory_space=pltpu.SMEM))
        elif index in far:
            spaces.append(pl.BlockSpec(memory_space=pltpu.HBM))
        else:
            spaces.append(pl.BlockSpec(memory_space=pltpu.VMEM))
    shapes = tuple(jax.ShapeDtypeStruct(shape, dtype) for shape, dtype in outs)
    out_specs = tuple(
        pl.BlockSpec(memory_space=pltpu.HBM if index in far_out else pltpu.VMEM)
        for index in range(len(outs))
    )
    return pl.pallas_call(
        kernel,
        out_shape=shapes,
        in_specs=spaces,
        out_specs=out_specs,
        scratch_shapes=list(scratch),
        compiler_params=pltpu.CompilerParams(vmem_limit_bytes=vmem * MIB),
        cost_estimate=pl.CostEstimate(
            flops=int(micros * 1e9), bytes_accessed=0, transcendentals=0
        ),
    )(*args)


def first_kernel(flags, cells, before, after, weights, pre_ref, sums_ref, early, late):
    rows = cells.shape[0]
    spots = before.shape[0]
    valid = flags[0]
    late[pl.ds(0, rows), :] = dot(cells[...], tap_of(weights, 2)) * valid
    late[pl.ds(rows, spots), :] = dot(after[...], tap_of(weights, 2)) * flags[2]
    early[pl.ds(0, spots), :] = dot(before[...], tap_of(weights, 0)) * flags[1]
    early[pl.ds(spots, rows), :] = dot(cells[...], tap_of(weights, 0)) * valid
    pre = (
        dot(cells[...], tap_of(weights, 1)) * valid
        + early[pl.ds(0, rows), :]
        + late[pl.ds(spots, rows), :]
    )
    pre_ref[...] = pre
    sums_ref[0:1, :] = column_sums(pre) * valid
    sums_ref[1:2, :] = column_sums(pre * pre) * valid


def first_conv(flags, cells, before, after, weights):
    rows, width = cells.shape
    narrow = weights.shape[3]
    spots = before.shape[0]
    return call(
        first_kernel,
        [((rows, narrow), F32), ((2, narrow), F32)],
        (flags, cells, before, after, weights),
        scratch=[pltpu.VMEM((rows + spots, narrow), F32)] * 2,
    )


def spread(values, edges, buffer, columns, rows):
    narrow = values.shape[1]
    margin = 16
    buffer[0, pl.ds(0, margin), :] = jnp.zeros((margin, narrow), F32)
    buffer[0, pl.ds(margin + rows, margin), :] = jnp.zeros((margin, narrow), F32)
    buffer[1, pl.ds(0, margin), :] = jnp.zeros((margin, narrow), F32)
    buffer[1, pl.ds(margin + rows, margin), :] = jnp.zeros((margin, narrow), F32)
    buffer[0, pl.ds(margin, rows), :] = values
    for across in range(3):
        moved = buffer[0, pl.ds(margin + across - 1, rows), :]
        if across == 0:
            moved = moved * edges[:, 0:1]
        if across == 2:
            moved = moved * edges[:, 1:2]
        buffer[1, pl.ds(margin, rows), :] = moved
        for down in range(3):
            part = buffer[1, pl.ds(margin + WW * (down - 1), rows), :]
            if down == 0:
                part = part * edges[:, 2:3]
            if down == 2:
                part = part * edges[:, 3:4]
            at = (3 * down + across) * narrow
            columns[:, at : at + narrow] = part.astype(LOW)


def spread_scratch(rows, narrow):
    return [pltpu.VMEM((2, rows + 32, narrow), F32), pltpu.VMEM((rows, 9 * narrow), LOW)]


def act_of(flags, pre, sums, scale_shift):
    mean, scale = moments(sums, flags[3])
    normal = (pre - mean) * scale
    return normal, normal * scale_shift[0:1] + scale_shift[1:2], scale


def middle_kernel(flags, pre, sums, gains, weights, edges, out_ref, sums_ref, buffer, columns):
    rows, narrow = pre.shape
    valid = flags[0]
    _, act, _ = act_of(flags, pre[...], sums[...], gains[...])
    spread(act * sig(act) * valid, edges[...], buffer, columns, rows)
    out = None
    for tap in range(9):
        part = dot(columns[:, tap * narrow : (tap + 1) * narrow], tap_of(weights, tap))
        out = part if out is None else out + part
    out_ref[...] = out
    sums_ref[0:1, :] = column_sums(out) * valid
    sums_ref[1:2, :] = column_sums(out * out) * valid


def middle_conv(flags, pre, sums, gains, weights, edges):
    rows, narrow = pre.shape
    return call(
        middle_kernel,
        [((rows, narrow), F32), ((2, narrow), F32)],
        (flags, pre, sums, gains, weights, edges),
        scratch=spread_scratch(rows, narrow),
    )


def last_kernel(flags, pre, sums, gains, weights, act_ref, sums_ref):
    valid = flags[0]
    _, act, _ = act_of(flags, pre[...], sums[...], gains[...])
    act_ref[...] = (act * sig(act) * valid).astype(LOW)
    for at in range(0, weights.shape[1], 256):
        out = dot(act_ref[...], weights[:, at : at + 256])
        sums_ref[0:1, at : at + 256] = column_sums(out) * valid
        sums_ref[1:2, at : at + 256] = column_sums(out * out) * valid


def last_conv(flags, pre, sums, gains, weights):
    rows, narrow = pre.shape
    width = weights.shape[1]
    return call(
        last_kernel,
        [((rows, narrow), LOW), ((2, width), F32)],
        (flags, pre, sums, gains, weights),
    )


def residual_tile(flags, act, cells, weights, sums, gains, at):
    mean, scale = moments(sums[:, at : at + 256], flags[3])
    normal = (dot(act[...], weights[:, at : at + 256]) - mean) * scale
    pre = cells[:, at : at + 256].astype(F32) + (
        normal * gains[0:1, at : at + 256] + gains[1:2, at : at + 256]
    )
    return normal, pre, scale


def embed_kernel(flags, act, cells, weights, sums, gains, embed, res_ref, query_ref, pair_ref):
    width = weights.shape[1]
    inner = query_ref.shape[1]
    for at in range(0, width, 256):
        _, pre, _ = residual_tile(flags, act, cells, weights, sums, gains, at)
        res_ref[:, at : at + 256] = (pre * sig(pre) * flags[0]).astype(LOW)
    for at in range(0, inner, 256):
        query_ref[:, at : at + 256] = dot(res_ref[...], embed[:, at : at + 256]).astype(LOW)
    for at in range(0, 2 * inner, 256):
        pair_ref[:, at : at + 256] = dot(
            res_ref[...], embed[:, inner + at : inner + at + 256]
        ).astype(LOW)


def embed_rows(flags, act, cells, weights, sums, gains, embed):
    rows, width = cells.shape
    inner = embed.shape[1] // 3
    return call(
        embed_kernel,
        [((rows, width), LOW), ((rows, inner), LOW), ((rows, 2 * inner), LOW)],
        (flags, act, cells, weights, sums, gains, embed),
        micros=7,
    )


def copies_of(refs, slots, sems):
    return [
        pltpu.make_async_copy(ref, slots.at[index], sems.at[index])
        for index, ref in enumerate(refs)
    ]


def attend_kernel(
    away, count, query, one, two, three, four, out_ref, log_ref, pairs, tails, scores, total, peak, sums, sems
):
    rows, inner = query.shape
    full = rows // 256 * 256
    rest = rows - full
    wide = 4 * rest
    turn = inner**-0.5 * math.log2(math.e)
    blocks = count[0]
    copies = copies_of((one, two, three, four), pairs, sems)
    for copy in copies:
        copy.start()

    @pl.when(blocks == 0)
    def _():
        out_ref[...] = jnp.zeros_like(out_ref)
        if away:
            log_ref[...] = jnp.zeros_like(log_ref)
            log_ref[0:1, :] = jnp.full((1, log_ref.shape[1]), NEG, F32)
        else:
            log_ref[...] = jnp.full_like(log_ref, NEG)

    peak[...] = jnp.full_like(peak, NEG)
    sums[...] = jnp.zeros_like(sums)

    def score(index, _):
        pltpu.make_async_copy(one, pairs.at[index], sems.at[index]).wait()

        @pl.when(index < blocks)
        def _():
            found = dot(query[...], pairs[index, pl.ds(0, full), :inner], NT)
            scores[index] = found
            top = peak[...]
            for at in range(0, full, 128):
                top = jnp.maximum(top, found[:, at : at + 128])
            peak[...] = top

        return 0

    lax.fori_loop(0, 4, score, 0)

    @pl.when(blocks > 0)
    def _():
        for index in range(4):
            tails[pl.ds(index * rest, rest), :] = pairs[index, pl.ds(full, rest), :]
        lane = lax.broadcasted_iota(jnp.int32, (rows, wide), 1)
        end = jnp.where(lane < blocks * rest, dot(query[...], tails[:, :inner], NT), NEG)
        top = jnp.maximum(
            jnp.max(peak[...], axis=1, keepdims=True), jnp.max(end, axis=1, keepdims=True)
        )
        top = top * turn
        lifted = jnp.exp2(end * turn - top)
        end_sum = jnp.sum(lifted, axis=1, keepdims=True)
        total[...] = dot(lifted.astype(LOW), tails[:, inner:])
        peak[...] = jnp.broadcast_to(top, peak.shape)

        def weigh(index, _):
            base = peak[...]
            running = sums[...]
            parts = []
            for at in range(0, full, 128):
                part = jnp.exp2(scores[index, :, at : at + 128] * turn - base)
                running = running + part
                parts.append(part.astype(LOW))
            sums[...] = running
            total[...] += dot(
                jnp.concatenate(parts, axis=1), pairs[index, pl.ds(0, full), inner:]
            )
            return 0

        lax.fori_loop(0, blocks, weigh, 0)
        found = jnp.sum(sums[...], axis=1, keepdims=True) + end_sum
        logs = jnp.broadcast_to(top + jnp.log2(found), peak.shape)
        if away:
            out = total[...] / found
            mean = column_sums(out) * (1.0 / rows)
            out_ref[...] = (out - mean).astype(out_ref.dtype)
            log_ref[...] = row_of(logs, log_ref.shape[1])
            log_ref[1:2, :inner] = mean
        else:
            out_ref[...] = (total[...] / found).astype(out_ref.dtype)
            log_ref[...] = logs


def attend(count, query, blocks, away):
    rows, inner = query.shape
    span = -(-rows // 128) * 128
    full = rows // 256 * 256
    rest = rows - full
    return call(
        functools.partial(attend_kernel, away),
        [((rows, inner), LOW), ((8, span) if away else (rows, 128), F32)],
        (count, query) + tuple(blocks),
        scratch=[
            pltpu.VMEM((4, rows, 2 * inner), LOW),
            pltpu.VMEM((4 * rest, 2 * inner), LOW),
            pltpu.VMEM((4, rows, full), F32),
            pltpu.VMEM((rows, inner), F32),
            pltpu.VMEM((rows, 128), F32),
            pltpu.VMEM((rows, 128), F32),
            pltpu.SemaphoreType.DMA((4,)),
        ],
        vmem=36,
        far=(2, 3, 4, 5),
        micros=10,
    )


def attend_back_kernel(away, held, split, count, query, grad, *refs):
    size = len(held)
    refs = list(refs)
    if away:
        packed = refs.pop(0)
    else:
        log_ref, term_ref = refs.pop(0), refs.pop(0)
    given_query = refs.pop(0) if away and held[0] == 0 else None
    blocks_in = [refs.pop(0) for _ in held]
    given = [refs.pop(0) for _ in held] if away else ()
    query_ref = refs.pop(0)
    outs = [[refs.pop(0) for _ in range(2 if place in split else 1)] for place in held]
    pairs, tails, stage, stage_tails, total, sems, out_sems = refs[:7]
    if away:
        log_ref, term_ref, in_sems = refs[7:]
    rows, inner = query.shape
    full = rows // 256 * 256
    rest = rows - full
    wide = size * rest
    scaling = inner**-0.5
    turn = scaling * math.log2(math.e)
    blocks = count[0]

    def main_of(ref):
        return ref.at[pl.ds(0, full)]

    def tail_of(ref):
        return ref.at[pl.ds(full, rest)]

    def tail_at(index):
        return pl.ds(index * rest, rest)

    begin = [
        pltpu.make_async_copy(tail_of(ref), tails.at[tail_at(index)], sems.at[1, index])
        for index, ref in enumerate(blocks_in)
    ] + [
        pltpu.make_async_copy(tail_of(ref), stage_tails.at[tail_at(index)], in_sems.at[1, index])
        for index, ref in enumerate(given)
    ]
    for copy in begin:
        copy.start()
    for index in range(size):
        pltpu.make_async_copy(main_of(blocks_in[index]), pairs.at[index], sems.at[0, index]).start()
        if away:
            pltpu.make_async_copy(main_of(given[index]), stage.at[index], in_sems.at[0, index]).start()
    if away:
        log_ref[...] = column_of(packed[0:1, :])[:rows]
        term_ref[...] = column_of(packed[1:2, :])[:rows]
    for copy in begin:
        copy.wait()

    def tile(keys, values, span, mask):
        found = dot(query[...], keys, NT)
        back = dot(grad[...], values, NT)
        logs = log_ref[...]
        terms = term_ref[...]
        kept = []
        slopes = []
        for at in range(0, span, 128):
            end = min(at + 128, span)
            weight = jnp.exp2(found[:, at:end] * turn - logs[:, : end - at])
            if mask is not None:
                weight = jnp.where(mask, weight, 0.0)
            kept.append(weight.astype(LOW))
            slopes.append((weight * (back[:, at:end] - terms[:, : end - at])).astype(LOW))
        kept = kept[0] if len(kept) == 1 else jnp.concatenate(kept, axis=1)
        slopes = slopes[0] if len(slopes) == 1 else jnp.concatenate(slopes, axis=1)
        return slopes, dot(slopes, query[...], TN) * scaling, dot(kept, grad[...], TN)

    active = blocks > held[0]

    @pl.when(jnp.logical_not(active))
    def _():
        if given_query is None:
            query_ref[...] = jnp.zeros_like(query_ref)
        else:
            query_ref[...] = given_query[...].astype(query_ref.dtype)
        if not away:
            stage_tails[...] = jnp.zeros_like(stage_tails)

    @pl.when(active)
    def _():
        keys = tails[:, :inner]
        lane = lax.broadcasted_iota(jnp.int32, (rows, wide), 1)
        ok = lane < (blocks - held[0]) * rest
        slopes, key_part, value_part = tile(keys, tails[:, inner:], wide, ok)
        total[...] = dot(slopes, keys)
        if away:
            key_part = key_part + stage_tails[:, :inner].astype(F32)
            value_part = value_part + stage_tails[:, inner:].astype(F32)
        stage_tails[:, :inner] = key_part.astype(LOW)
        stage_tails[:, inner:] = value_part.astype(LOW)

    def columns(which, part):
        width = 2 * inner // len(outs[which])
        return pl.ds(part * width, width)

    def main_outs(which):
        return [
            pltpu.make_async_copy(
                stage.at[which, :, columns(which, part)], main_of(ref), out_sems.at[0, which, part]
            )
            for part, ref in enumerate(outs[which])
        ]

    def one_block(index, _):
        pltpu.make_async_copy(main_of(blocks_in[0]), pairs.at[index], sems.at[0, index]).wait()
        if away:
            pltpu.make_async_copy(main_of(given[0]), stage.at[index], in_sems.at[0, index]).wait()

        @pl.when(index < blocks - held[0])
        def _():
            block = pairs[index, :, :inner]
            slopes, key_part, value_part = tile(block, pairs[index, :, inner:], full, None)
            total[...] += dot(slopes, block)
            if away:
                key_part = key_part + stage[index, :, :inner].astype(F32)
                value_part = value_part + stage[index, :, inner:].astype(F32)
            stage[index, :, :inner] = key_part.astype(LOW)
            stage[index, :, inner:] = value_part.astype(LOW)

        if not away:

            @pl.when(index >= blocks - held[0])
            def _():
                stage[index] = jnp.zeros(stage.shape[1:], LOW)

        for which in range(size):

            @pl.when(index == which)
            def _():
                for copy in main_outs(which):
                    copy.start()

        return 0

    lax.fori_loop(0, size, one_block, 0)
    ends = [
        pltpu.make_async_copy(
            stage_tails.at[tail_at(index), columns(index, part)],
            tail_of(ref),
            out_sems.at[1, index, part],
        )
        for index in range(size)
        for part, ref in enumerate(outs[index])
    ]
    for copy in ends:
        copy.start()

    @pl.when(active)
    def _():
        found = total[...] * scaling
        if given_query is not None:
            found = found + given_query[...]
        query_ref[...] = found.astype(query_ref.dtype)

    for index in range(size):
        for copy in main_outs(index):
            copy.wait()
    for copy in ends:
        copy.wait()


def attend_back(
    count, query, grad, terms, blocks, held, given, given_query, out_type, split=()
):
    rows, inner = query.shape
    full = rows // 256 * 256
    rest = rows - full
    away = given is not None
    size = len(held)
    more = () if given_query is None else (given_query,)
    near = (count, query, grad) + tuple(terms) + more
    distant = tuple(blocks) + (tuple(given) if away else ())
    scratch = [
        pltpu.VMEM((size, full, 2 * inner), LOW),
        pltpu.VMEM((size * rest, 2 * inner), LOW),
        pltpu.VMEM((size, full, 2 * inner), LOW),
        pltpu.VMEM((size * rest, 2 * inner), LOW),
        pltpu.VMEM((rows, inner), F32),
        pltpu.SemaphoreType.DMA((2, size)),
        pltpu.SemaphoreType.DMA((2, size, 2)),
    ]
    widths = []
    for at in held:
        widths += [inner] * 2 if at in split else [2 * inner]
    if away:
        scratch += [pltpu.VMEM((rows, 128), F32)] * 2 + [pltpu.SemaphoreType.DMA((2, size))]
    found = call(
        functools.partial(attend_back_kernel, away, held, split),
        [((rows, inner), out_type)] + [((rows, width), LOW) for width in widths],
        near + distant,
        scratch=scratch,
        vmem=36,
        far=tuple(range(len(near), len(near) + len(distant))),
        far_out=tuple(range(1, 1 + len(widths))),
        micros=17,
    )
    return found[0], found[1:]


def column_of(row):
    return jnp.transpose(jnp.broadcast_to(row, (128, row.shape[1])))


def row_of(column, span):
    tall = jnp.concatenate([column, jnp.zeros((span - column.shape[0], 128), F32)], axis=0)
    return jnp.transpose(tall)[0:8, :]


def merge_kernel(
    flags, own, own_log, far, far_log, weights, cot, out_ref, log_ref, sums_ref
):
    rows, inner = own.shape
    logs = own_log[...]
    others = column_of(far_log[0:1, :])[:rows]
    top = jnp.maximum(logs, others)
    whole = top + jnp.log2(jnp.exp2(logs - top) + jnp.exp2(others - top))
    log_ref[...] = whole
    share = jnp.exp2(logs - whole)
    other = jnp.exp2(others - whole)
    for at in range(0, inner, 128):
        out_ref[:, at : at + 128] = (
            own[:, at : at + 128].astype(F32) * share + (far[:, at : at + 128].astype(F32) + far_log[1:2, at : at + 128]) * other
        ).astype(LOW)
    valid = flags[0]
    for at in range(0, weights.shape[1], 256):
        out = dot(out_ref[...], weights[:, at : at + 256])
        grad = cot[:, at : at + 256].astype(F32)
        sums_ref[0:1, at : at + 256] = column_sums(out) * valid
        sums_ref[1:2, at : at + 256] = column_sums(out * out) * valid
        sums_ref[2:3, at : at + 256] = column_sums(grad) * valid
        sums_ref[3:4, at : at + 256] = column_sums(grad * out) * valid
    sums_ref[4:5, :] = jnp.zeros((1, weights.shape[1]), F32)
    sums_ref[4:5, :inner] = column_sums(out_ref[...].astype(F32)) * valid


def merge(flags, own, own_log, far, far_log, weights, cot):
    rows, inner = own.shape
    width = weights.shape[1]
    return call(
        merge_kernel,
        [((rows, inner), LOW), ((rows, 128), F32), ((5, width), F32)],
        (flags, own, own_log, far, far_log, weights, cot),
    )


def outer_kernel(
    flags,
    att,
    weights,
    sums,
    gains,
    cot,
    res,
    logs,
    mixed_ref,
    grad_ref,
    back_ref,
    term_ref,
    rows_ref,
    norm_ref,
):
    valid = flags[0]
    inverse = flags[3]
    width = weights.shape[1]
    for at in range(0, width, 256):
        span = slice(at, at + 256)
        mean, scale = moments(sums[0:2, span], inverse)
        normal = (dot(att[...], weights[:, span]) - mean) * scale
        gain = gains[0:1, span]
        mixed_ref[:, span] = (
            (res[:, span].astype(F32) + (normal * gain + gains[1:2, span])) * valid
        ).astype(LOW)
        shift_grad = sums[2:3, span]
        gain_grad = scale * (sums[3:4, span] - mean * shift_grad)
        norm_ref[0:1, span] = gain_grad
        norm_ref[1:2, span] = shift_grad
        removed = (shift_grad + normal * gain_grad) * inverse
        grad = ((gain * scale * valid) * (cot[:, span].astype(F32) - removed)).astype(LOW)
        grad_ref[:, span] = grad
        norm_ref[2:3, span] = column_sums(grad.astype(F32))
    back = dot(grad_ref[...], weights[...], NT).astype(LOW)
    back_ref[...] = back
    term = jnp.sum(back.astype(F32) * att[...].astype(F32), axis=1, keepdims=True)
    term = jnp.broadcast_to(term, term_ref.shape)
    term_ref[...] = term
    rows_ref[...] = row_of(logs[...], rows_ref.shape[1])
    rows_ref[1:2, :] = row_of(term, rows_ref.shape[1])[0:1]


def outer(flags, att, weights, sums, gains, cot, res, logs):
    rows, inner = att.shape
    width = weights.shape[1]
    span = -(-rows // 128) * 128
    return call(
        outer_kernel,
        [
            ((rows, width), LOW),
            ((rows, width), LOW),
            ((rows, inner), LOW),
            ((rows, 128), F32),
            ((8, span), F32),
            ((3, width), F32),
        ],
        (flags, att, weights, sums, gains, cot, res, logs),
        micros=5,
    )


def project_kernel(
    flags,
    query_own,
    query_far,
    keep,
    near_keys,
    near_values,
    far,
    act,
    cells,
    weights,
    sums,
    gains,
    embed_far,
    cot_far,
    proj_ref,
    pre_ref,
    sums_ref,
    embed,
    cot,
    sems,
):
    valid = flags[0]
    inner = query_own.shape[1]
    copies = [
        pltpu.make_async_copy(embed_far, embed, sems.at[0]),
        pltpu.make_async_copy(cot_far, cot, sems.at[1]),
    ]
    for copy in copies:
        copy.start()
    proj_ref[:, :inner] = (query_own[...].astype(F32) + query_far[...].astype(F32)).astype(LOW)
    for at in range(0, 2 * inner, 256):
        span = slice(at, at + 256)
        near = near_keys[:, span] if at < inner else near_values[:, at - inner : at - inner + 256]
        proj_ref[:, inner + at : inner + at + 256] = (
            keep[:, span].astype(F32) + near.astype(F32) + far[:, span].astype(F32)
        ).astype(LOW)
    for copy in copies:
        copy.wait()
    for at in range(0, weights.shape[1], 256):
        span = slice(at, at + 256)
        normal, pre, _ = residual_tile(flags, act, cells, weights, sums, gains, at)
        grad = cot[:, span].astype(F32) + dot(proj_ref[...], embed[span, :], NT)
        out = grad * valid * slope(pre)
        pre_ref[:, span] = out
        sums_ref[0:1, span] = column_sums(out)
        sums_ref[1:2, span] = column_sums(out * normal)


def project_back(flags, query_own, query_far, keep, near_keys, near_values, far, act, cells, weights, sums, gains, embed, cot):
    rows, width = cells.shape
    inner = query_own.shape[1]
    return call(
        project_kernel,
        [((rows, 3 * inner), LOW), ((rows, width), F32), ((2, width), F32)],
        (flags, query_own, query_far, keep, near_keys, near_values, far, act, cells, weights, sums, gains, embed, cot),
        scratch=[
            pltpu.VMEM(embed.shape, LOW),
            pltpu.VMEM(cot.shape, LOW),
            pltpu.SemaphoreType.DMA((2,)),
        ],
        far=(12, 13),
        micros=10,
    )


def last_back_kernel(
    flags, pre_grad, act, weights, sums, gains, back_sums, pre_two, sums_two, gains_two, grad_ref, two_ref, sums_ref
):
    valid = flags[0]
    inverse = flags[3]
    two = None
    for at in range(0, weights.shape[1], 256):
        span = slice(at, at + 256)
        mean, scale = moments(sums[:, span], inverse)
        normal = (dot(act[...], weights[:, span]) - mean) * scale
        removed = (back_sums[0:1, span] + normal * back_sums[1:2, span]) * inverse
        grad = ((gains[0:1, span] * scale * valid) * (pre_grad[:, span] - removed)).astype(LOW)
        grad_ref[:, span] = grad
        part = dot(grad, weights[:, span], NT)
        two = part if two is None else two + part
    normal, active, _ = act_of(flags, pre_two[...], sums_two[...], gains_two[...])
    two = two * valid * slope(active)
    two_ref[...] = two
    sums_ref[0:1, :] = column_sums(two)
    sums_ref[1:2, :] = column_sums(two * normal)


def last_back(flags, pre_grad, act, weights, sums, gains, back_sums, pre_two, sums_two, gains_two):
    rows, width = pre_grad.shape
    narrow = act.shape[1]
    return call(
        last_back_kernel,
        [((rows, width), LOW), ((rows, narrow), F32), ((2, narrow), F32)],
        (flags, pre_grad, act, weights, sums, gains, back_sums, pre_two, sums_two, gains_two),
    )


def middle_back_kernel(
    flags, two, back_sums, pre_two, sums_two, gains_two, pre_one, sums_one, gains_one, weights, edges,
    grad_ref, one_ref, sums_ref, buffer, columns
):
    rows, narrow = two.shape
    valid = flags[0]
    inverse = flags[3]
    normal, _, scale = act_of(flags, pre_two[...], sums_two[...], gains_two[...])
    removed = (back_sums[0:1] + normal * back_sums[1:2]) * inverse
    grad = (gains_two[0:1, :] * scale * valid) * (two[...] - removed)
    grad_ref[...] = grad.astype(LOW)
    spread(grad, edges[...], buffer, columns, rows)
    one = None
    for tap in range(9):
        part = dot(columns[:, tap * narrow : (tap + 1) * narrow], tap_of(weights, 8 - tap), NT)
        one = part if one is None else one + part
    normal, active, _ = act_of(flags, pre_one[...], sums_one[...], gains_one[...])
    one = one * valid * slope(active)
    one_ref[...] = one
    sums_ref[0:1, :] = column_sums(one)
    sums_ref[1:2, :] = column_sums(one * normal)


def middle_back(flags, two, back_sums, pre_two, sums_two, gains_two, pre_one, sums_one, gains_one, weights, edges):
    rows, narrow = two.shape
    return call(
        middle_back_kernel,
        [((rows, narrow), LOW), ((rows, narrow), F32), ((2, narrow), F32)],
        (flags, two, back_sums, pre_two, sums_two, gains_two, pre_one, sums_one, gains_one, weights, edges),
        scratch=spread_scratch(rows, narrow),
    )


def middle_weight_kernel(flags, pre_one, sums_one, gains_one, grad, edges, out_ref, buffer, columns):
    rows, narrow = pre_one.shape
    _, act, _ = act_of(flags, pre_one[...], sums_one[...], gains_one[...])
    spread(act * sig(act) * flags[0], edges[...], buffer, columns, rows)
    for tap in range(9):
        out_ref[pl.ds(tap * narrow, narrow), :] = dot(
            columns[:, tap * narrow : (tap + 1) * narrow], grad[...], TN
        ).astype(LOW)


def middle_weight(flags, pre_one, sums_one, gains_one, grad, edges):
    rows, narrow = pre_one.shape
    return call(
        middle_weight_kernel,
        [((9 * narrow, narrow), LOW)],
        (flags, pre_one, sums_one, gains_one, grad, edges),
        scratch=spread_scratch(rows, narrow),
    )[0]


def first_grad_kernel(flags, one, back_sums, pre_one, sums_one, gains_one, grad_ref):
    normal, _, scale = act_of(flags, pre_one[...], sums_one[...], gains_one[...])
    removed = (back_sums[0:1] + normal * back_sums[1:2]) * flags[3]
    grad_ref[...] = (
        (gains_one[0:1, :] * scale * flags[0]) * (one[...] - removed)
    ).astype(LOW)


def first_grad_of(flags, one, back_sums, pre_one, sums_one, gains_one):
    rows, narrow = one.shape
    return call(
        first_grad_kernel,
        [((rows, narrow), LOW)],
        (flags, one, back_sums, pre_one, sums_one, gains_one),
    )[0]


def first_back_kernel(
    place, flags, grad, before, after, cells, middle, last, mine, others, cols_ref, buffer, halves, sems
):
    rows, narrow = grad.shape
    width = cells.shape[1]
    spots = before.shape[0]
    buffer[pl.ds(0, spots), :] = before[...].astype(F32) * flags[1]
    buffer[pl.ds(spots, rows), :] = grad[...].astype(F32)
    buffer[pl.ds(spots + rows, spots), :] = after[...].astype(F32) * flags[2]
    at = middle.shape[0]
    put_rows(halves, 0, middle[...])
    for tap in range(3):
        part = (buffer[pl.ds(spots * (2 - tap), rows), :] * flags[0]).astype(LOW)
        cols_ref[:, tap * narrow : (tap + 1) * narrow] = part
        put_rows(halves, at, dot(cells[...], part, TN).astype(LOW))
        at += width
    put_rows(halves, at, last[...])
    deal(place, halves, mine, others, sems)


def first_back(place, flags, grad, before, after, cells, middle, last):
    rows, narrow = grad.shape
    spots = before.shape[0]
    width = cells.shape[1]
    mine, others, cols = halves_call(
        first_back_kernel,
        middle.shape[0] + 3 * width + last.shape[0],
        [((rows, 3 * narrow), LOW)],
        (place, flags, grad, before, after, cells, middle, last),
        scratch=[pltpu.VMEM((rows + 2 * spots, narrow), F32)],
    )
    return (mine, others), cols


def early_weight_kernel(
    place, flags, res, proj, att, sums, grad, mine, others, halves, sems
):
    height, inner = res.shape[1], att.shape[1]
    left = (att[...].astype(F32) - sums[...] * flags[3]).astype(LOW)
    at = 0
    for index in range(proj.shape[1] // 256):
        put_rows(
            halves, at, dot(res[...], proj[:, index * 256 : (index + 1) * 256], TN).astype(LOW)
        )
        at += height
    for index in range(grad.shape[1] // 256):
        put_rows(
            halves, at, dot(left, grad[:, index * 256 : (index + 1) * 256], TN).astype(LOW)
        )
        at += inner
    deal(place, halves, mine, others, sems)


def halves_call(kernel, height, outs, args, scratch=()):
    shape = (height // 2, 256)
    return call(
        kernel,
        [(shape, LOW), (shape, LOW)] + outs,
        args,
        scalars=2,
        scratch=list(scratch)
        + [pltpu.VMEM((2,) + shape, LOW), pltpu.SemaphoreType.DMA((2,))],
        far_out=(0, 1),
        micros=8,
    )


def early_weight(place, flags, res, proj, att, sums, grad):
    height = res.shape[1] * proj.shape[1] // 256 + att.shape[1] * grad.shape[1] // 256
    return halves_call(
        early_weight_kernel, height, [], (place, flags, res, proj, att, sums, grad)
    )


def weight_kernel(left, right, out_ref):
    height = left.shape[1]
    for index in range(right.shape[1] // 256):
        out_ref[pl.ds(index * height, height), :] = dot(
            left[...], right[:, index * 256 : (index + 1) * 256], TN
        ).astype(LOW)


def weight_grad(left, right):
    rows, height = left.shape
    width = right.shape[1]
    return call(
        weight_kernel,
        [((height * width // 256, 256), LOW)],
        (left, right),
        scalars=0,
    )[0]


def pieces_of(low_half, high_half, start, stop):
    middle = low_half.shape[0]
    if start < middle:
        yield 0, low_half[pl.ds(start, min(stop, middle) - start), :]
    if stop > middle:
        begin = max(start, middle)
        yield begin - start, high_half[pl.ds(begin - middle, stop - begin), :]


def squares_of(values):
    return jnp.sum((values * values).reshape(-1, 8, values.shape[-1]), axis=0)


def emit(place, half, other, shares, squares):
    def write(low_half, high_half):
        squares[...] = jnp.zeros_like(squares)
        for start, stop, store, extra in shares:
            for offset, rows in pieces_of(low_half, high_half, start, stop):
                values = rows.astype(F32)
                if extra is not None:
                    values = values + extra[offset : offset + values.shape[0]]
                squares[...] += squares_of(values)
                store(offset, values)

    @pl.when(place[0] == 0)
    def _():
        write(half, other)

    @pl.when(place[0] == 1)
    def _():
        write(other, half)


def store_rows(ref, lead, cols):
    def store(offset, values):
        ref[lead + (pl.ds(offset, values.shape[0]), cols)] = values

    return store


def early_shares(embed_ref, back_ref, mean, grad_sum):
    width, inner = embed_ref.shape[1], embed_ref.shape[2]
    shares = []
    at = 0
    for index in range(3 * inner // 256):
        part, col = divmod(index * 256, inner)
        shares.append((at, at + width, store_rows(embed_ref, (part,), slice(col, col + 256)), None))
        at += width
    for index in range(width // 256):
        cols = slice(index * 256, index * 256 + 256)
        extra = mean[:, 0:1] * grad_sum[0:1, cols]
        shares.append((at, at + inner, store_rows(back_ref, (), cols), extra))
        at += inner
    return shares


def early_kernel(place, flags, half, other, sums, grad_sum, embed_ref, back_ref, embed_own, back_own, squares_ref):
    mean = sums[...] * flags[3]
    emit(place, half, other, early_shares(embed_ref, back_ref, column_of(mean), grad_sum), squares_ref)
    span = embed_own.shape[1]
    embed_own[...] = embed_ref[:, pl.ds(pl.multiple_of(place[1] * span, span), span), :]
    span = back_own.shape[0]
    back_own[...] = back_ref[pl.ds(pl.multiple_of(place[1] * span, span), span), :]


def early_grads(place, flags, half, other, sums, grad_sum, width, inner, shards):
    return call(
        early_kernel,
        [
            ((3, width, inner), F32),
            ((inner, width), F32),
            ((3, width // shards, inner), F32),
            ((inner // shards, width), F32),
            ((8, 256), F32),
        ],
        (place, flags, half, other, sums, grad_sum),
        scalars=2,
        micros=6,
    )


def late_shares(first_ref, middle_ref, last_ref):
    shares = []
    at = 0
    for ref in (middle_ref, first_ref):
        for index in range(ref.shape[0]):
            shares.append((at, at + ref.shape[1], store_rows(ref, (index,), slice(None)), None))
            at += ref.shape[1]
    for index in range(last_ref.shape[1] // 256):
        cols = slice(index * 256, index * 256 + 256)
        shares.append((at, at + last_ref.shape[0], store_rows(last_ref, (), cols), None))
        at += last_ref.shape[0]
    return shares


def late_kernel(rates, place, half, other, squares, extra, embed_own, back_own, *refs):
    given = [refs[3 * index : 3 * index + 3] for index in range(5)]
    first_ref, middle_ref, last_ref, norm_ref = refs[15:19]
    made = [refs[19 + 3 * index : 22 + 3 * index] for index in range(5)]
    tally = refs[34]
    emit(place, half, other, late_shares(first_ref, middle_ref, last_ref), tally)
    found = jnp.sum(tally[...] + squares[...], axis=0, keepdims=True)
    norm = jnp.sqrt(jnp.sum(found, axis=1, keepdims=True) + extra[0:1, 0:1])
    factor = jnp.minimum(1.0, CLIP_AT / (norm + 1e-06))
    norm_ref[0:1, :] = jnp.broadcast_to(norm, (1, 128))
    norm_ref[1:2, :] = jnp.broadcast_to(factor, (1, 128))

    def mine(span):
        return pl.ds(pl.multiple_of(place[1] * span, span), span)

    def own(index, part):
        if index == 0:
            return first_ref[part, mine(given[0][0].shape[1]), :]
        if index == 1:
            return middle_ref[part, mine(given[1][0].shape[1]), :]
        if index == 2:
            return last_ref[mine(given[2][0].shape[0]), :]
        return embed_own[part] if index == 3 else back_own[...]

    for index in range(5):
        master, moment, second = given[index]
        outs = made[index]
        for part in range(master.shape[0]) if len(master.shape) == 3 else (slice(None),):
            values = adam_step(
                master[part], own(index, part), moment[part], second[part], factor, rates[index]
            )
            for ref, value in zip(outs, values):
                ref[part] = value


def late_grads(rates, place, half, other, squares, extra, embed_own, back_own, states, shapes):
    flat = tuple(item for state in states for item in state)
    outs = [(shape, F32) for shape in shapes] + [((2, 128), F32)]
    outs += [(state[0].shape, F32) for state in states for _ in range(3)]
    found = call(
        functools.partial(late_kernel, rates),
        outs,
        (place, half, other, squares, extra, embed_own, back_own) + flat,
        scratch=[pltpu.VMEM((8, 256), F32)],
        micros=8,
    )
    return found[:3], found[3], [found[4 + 3 * index : 7 + 3 * index] for index in range(5)]


def unfold(value, height):
    return jnp.moveaxis(value.reshape(-1, height, 256), 0, 1).reshape(height, -1)


def plain_tail(early, late, mean, grad_sum, sizes, norm_square, states, rates, chan_at):
    width, inner, narrow = sizes
    core = chan_at & 1
    early, late = [
        jnp.where(core == 0, jnp.concatenate([half, other]), jnp.concatenate([other, half])).astype(
            F32
        )
        for half, other in (early, late)
    ]
    cut = 3 * inner * width // 256
    embed = unfold(early[:cut], width).reshape(width, 3, inner)
    back = unfold(early[cut:], inner) + mean[:, None] * grad_sum[None, :]
    middle = late[: 9 * narrow].reshape(9, narrow, narrow)
    first = late[9 * narrow : 9 * narrow + 3 * width].reshape(3, width, narrow)
    last = unfold(late[9 * narrow + 3 * width :], narrow)
    grads = (first, middle, last, jnp.moveaxis(embed, 1, 0), back)
    norm = jnp.sqrt(sum(jnp.sum(item * item) for item in grads) + norm_square)
    factor = jnp.minimum(1.0, CLIP_AT / (norm + 1e-06))
    made = []
    for grad, state, rate in zip(grads, states, rates):
        axis = grad.ndim - 2
        span = state[0].shape[axis]
        owned = lax.dynamic_slice_in_dim(grad, chan_at * span, span, axis)
        made.append(adam_step(state[0], owned, state[1], state[2], factor, rate))
    return grads, norm, factor, made


def input_kernel(cols, weights, pre_grad, out_ref):
    shards, _, span, narrow = weights.shape
    each = 256 // span
    for at in range(0, pre_grad.shape[1], 256):
        out = pre_grad[:, at : at + 256]
        begin = at // span
        for tap in range(3):
            rows = weights[pl.ds(begin, each), tap].reshape(256, narrow)
            out = out + dot(cols[:, tap * narrow : (tap + 1) * narrow], rows, NT)
        span_at = slice(at, at + 256)
        out_ref[:, span_at] = out.astype(LOW)


def input_grad(cols, weights, pre_grad):
    rows, width = pre_grad.shape
    return call(
        input_kernel,
        [((rows, width), LOW)],
        (cols, weights, pre_grad),
        scalars=0,
    )[0]


def adam_step(master, gradient, moment, second, factor, rate):
    clipped = gradient * factor
    moment_new = BETA_ONE * moment + (1.0 - BETA_ONE) * clipped
    second_new = BETA_TWO * second + (1.0 - BETA_TWO) * clipped * clipped
    moment_hat = moment_new / (1.0 - BETA_ONE**STEP)
    second_hat = second_new / (1.0 - BETA_TWO**STEP)
    master_new = master - rate * (
        moment_hat / (jnp.sqrt(second_hat) + ADAM_EPS) + WEIGHT_DECAY * master
    )
    return (moment_new, second_new, master_new)


def body(
    features,
    cotangent,
    frame_counts,
    weight_first,
    weight_middle,
    weight_last,
    weight_embed,
    weight_back,
    norm_params,
    moment_first,
    moment_middle,
    moment_last,
    moment_embed,
    moment_back,
    moment_norm,
    second_first,
    second_middle,
    second_last,
    second_embed,
    second_back,
    second_norm,
):
    chan_at = lax.axis_index("chan")
    device = lax.axis_index("clip") * lax.axis_size("chan") + chan_at
    frames, spot_count, model_width = features.shape
    row_count = frames * spot_count
    narrow = BOT
    inner_width = INNER
    clip_place = chan_at % DPC
    clip_at = device // DPC
    clip_ids = jnp.arange(frame_counts.shape[0], dtype=jnp.int32)
    length = jnp.sum(jnp.where(clip_ids == clip_at, frame_counts, 0))

    def valid_at(place):
        return ((place >= 0) & (place < DPC) & (place * frames < length)).astype(jnp.float32)

    place = jnp.stack([chan_at & 1, chan_at]).astype(jnp.int32)
    own_ok = valid_at(clip_place)
    row_total = jnp.sum(frame_counts).astype(jnp.float32) * spot_count
    zero = jnp.zeros((), jnp.float32)
    flags = jnp.stack(
        [own_ok, valid_at(clip_place - 1), valid_at(clip_place + 1), 1.0 / row_total]
        + [valid_at(clip_place ^ 2)] + [zero] * 3
    )
    held = sum(valid_at(clip_place ^ turn) for turn in range(4)) * own_ok
    blocks_own = held.astype(jnp.int32).reshape(1)
    blocks_far = (held * valid_at(clip_place ^ 4)).astype(jnp.int32).reshape(1)
    span_list = [narrow] * 4 + [model_width] * 4
    starts = [sum(span_list[:index]) for index in range(8)]
    gains_one, gains_two, gains_three, gains_four = [
        norm_params[starts[index] : starts[index] + 2 * span_list[index]].reshape(2, -1)
        for index in range(0, 8, 2)
    ]
    shards = lax.axis_size("chan")
    first_low = whole_of(weight_first)
    tall = weight_middle.shape[0] * weight_middle.shape[1]
    packed = jnp.concatenate(
        [
            weight_middle.reshape(tall, narrow),
            jnp.moveaxis(weight_last.reshape(-1, model_width // 256, 256), 1, 0).reshape(-1, 256),
        ]
    ).astype(LOW)
    packed = lax.all_gather(packed, "chan", axis=0, tiled=False)
    middle_low = packed[:, :tall].reshape((shards,) + weight_middle.shape)
    last_low = jnp.moveaxis(
        packed[:, tall:].reshape(shards, model_width // 256, -1, 256), 1, 2
    ).reshape(narrow, model_width)
    if weight_middle.shape[1] % 16:
        middle_low = jnp.moveaxis(middle_low, 0, 1).reshape(1, 9, narrow, narrow)
    embed_low, back_low = (
        lax.all_gather(weight_embed.astype(LOW).reshape(-1, 3 * inner_width), "chan", axis=0, tiled=True),
        lax.all_gather(weight_back.astype(LOW), "chan", axis=0, tiled=True),
    )
    spots = np.arange(row_count)
    across, down = spots % WW, spots // WW % HH
    edges = jnp.asarray(
        np.stack([across > 0, across < WW - 1, down > 0, down < HH - 1] + [across < 0] * 4, axis=1)
        .astype(np.float32)
    )
    cells = features.reshape(row_count, model_width)
    cot = cotangent.reshape(row_count, model_width)
    before, after = beside(features, spot_count)
    pre_one, sums_one = first_conv(flags, cells, before, after, first_low)
    sums_one = total(sums_one)
    pre_two, sums_two = middle_conv(
        flags, pre_one, sums_one, gains_one, middle_low, edges
    )
    sums_two = total(sums_two)
    act_two, sums_three = last_conv(flags, pre_two, sums_two, gains_two, last_low)
    sums_three, cot = tied(total(sums_three), cot)
    residual_low, query, pair_own = embed_rows(
        flags, act_two, cells, last_low, sums_three, gains_three, embed_low
    )
    pair_core = flipped(pair_own, "chan", 1)
    query_far, pair_far = flipped(query, "chan", 4), flipped(pair_own, "chan", 2)
    query_far, pair_far, back_low = tied(query_far, pair_far, back_low)
    blocks = (pair_own, pair_core, pair_far, flipped(pair_far, "chan", 1))
    part_far, log_far = attend(blocks_far, query_far, blocks, True)
    part_far = flipped(part_far, "chan", 4)
    log_far = flipped(log_far, "chan", 4)
    part_own, log_own = attend(blocks_own, query, blocks, False)
    attended, logs, sums_four = merge(flags, part_own, log_own, part_far, log_far, back_low, cot)
    sums_four = total(sums_four)
    mixed, attn_grad, attended_grad, terms, packed, norm_four = outer(
        flags, attended, back_low, sums_four, gains_four, cot, residual_low, logs
    )
    mixed = laid_out(mixed, frames)
    attended_grad_far = flipped(attended_grad, "chan", 4)
    packed_far = flipped(packed, "chan", 4)
    query_own, held = attend_back(
        blocks_own, query, attended_grad, (logs, terms), blocks, (0, 1, 2, 3), None, None, F32
    )
    query_part, (far, far_core) = attend_back(
        blocks_far, query_far, attended_grad_far, (packed_far,), blocks[2:], (2, 3), held[2:], None, F32
    )
    far = (far.astype(F32) + flipped(far_core, "chan", 1).astype(F32)).astype(LOW)
    far, near_own = tied(far, held[0])
    far = flipped(far, "chan", 2)
    query_part, (keep, give_keys, give_values) = attend_back(
        blocks_far, query_far, attended_grad_far, (packed_far,), blocks[:2], (0, 1), (near_own, held[1]),
        query_part, LOW, (1,),
    )
    query_part = flipped(query_part, "chan", 4)
    near_keys, near_values = flipped(give_keys, "chan", 1), flipped(give_values, "chan", 1)
    projected_grad, pre_grad, back_three = project_back(
        flags, query_own, query_part, keep, near_keys, near_values, far, act_two, cells, last_low, sums_three,
        gains_three, embed_low, cot,
    )
    early = early_weight(
        place, flags, residual_low, projected_grad, attended, sums_four[4:5, :inner_width], attn_grad
    )
    back_three = total(jnp.concatenate([back_three, norm_four[2:3]]))
    early, back_three = tied(early, back_three)
    last_grad, two_grad, back_two = last_back(
        flags, pre_grad, act_two, last_low, sums_three, gains_three, back_three, pre_two, sums_two,
        gains_two,
    )
    back_two = total(back_two)
    last_local = weight_grad(act_two, last_grad)
    middle_grad, one_grad, back_one = middle_back(
        flags, two_grad, back_two, pre_two, sums_two, gains_two, pre_one, sums_one, gains_one,
        middle_low, edges,
    )
    back_one = total(back_one)
    middle_local = middle_weight(flags, pre_one, sums_one, gains_one, middle_grad, edges)
    first_grad = first_grad_of(flags, one_grad, back_one, pre_one, sums_one, gains_one)
    before, after = beside(first_grad.reshape(frames, spot_count, narrow), spot_count)
    late, grad_cols = first_back(place, flags, first_grad, before, after, cells, middle_local, last_local)
    features_gradient = laid_out(input_grad(grad_cols, first_low, pre_grad), frames)
    gain_one_grad, shift_one_grad = back_one[1], back_one[0]
    gain_two_grad, shift_two_grad = back_two[1], back_two[0]
    gain_three_grad, shift_three_grad = back_three[1], back_three[0]
    gain_four_grad, shift_four_grad = norm_four[0], norm_four[1]
    norm_gradient = jnp.concatenate(
        [
            gain_one_grad,
            shift_one_grad,
            gain_two_grad,
            shift_two_grad,
            gain_three_grad,
            shift_three_grad,
            gain_four_grad,
            shift_four_grad,
        ]
    )
    groups = [list(range(core, shards, 2)) for core in range(2)]
    early = lax.psum_scatter(core_step(*early), "clip", scatter_dimension=0, tiled=True)
    early = lax.psum(early, "chan", axis_index_groups=groups)
    steps = level_steps()[1:]
    late = scatter_sum(core_step(*late), steps)
    early, late = tied(early, late)
    early = lax.all_gather(early, "clip", axis=0, tiled=True)
    late = gather_sum(late, steps)
    early, late, mixed, features_gradient = tied(early, late, mixed, features_gradient)
    early = (early, flipped(early, "chan", 1))
    late = (late, flipped(late, "chan", 1))
    fans = (3 * D, 9 * BOT, BOT, D, INNER)
    rates = tuple(0.5 * fan ** (-0.5) for fan in fans)
    states = (
        (weight_first, moment_first, second_first),
        (weight_middle, moment_middle, second_middle),
        (weight_last, moment_last, second_last),
        tuple(jnp.moveaxis(item, 1, 0) for item in (weight_embed, moment_embed, second_embed)),
        (weight_back, moment_back, second_back),
    )
    norm_square = jnp.sum(norm_gradient * norm_gradient)
    if weight_middle.shape[1] % 16 == 0:
        embed, back, embed_own, back_own, squares = early_grads(
            place,
            flags,
            *early,
            sums_four[4:5, :inner_width],
            back_three[2:3],
            model_width,
            inner_width,
            shards,
        )
        shapes = ((3, model_width, narrow), (9, narrow, narrow), (narrow, model_width))
        (first, middle, last), norm_row, results = late_grads(
            rates, place, *late, squares, norm_square.reshape(1, 1), embed_own, back_own, states, shapes
        )
        gradient_norm, factor = norm_row[0, 0], norm_row[1, 0]
    else:
        (first, middle, last, embed, back), gradient_norm, factor, results = plain_tail(
            early,
            late,
            sums_four[4, :inner_width] * flags[3],
            back_three[2],
            (model_width, inner_width, narrow), norm_square, states, rates, chan_at
        )
    results = list(results)
    results[3] = tuple(jnp.moveaxis(item, 0, 1) for item in results[3])
    results.append(adam_step(norm_params, norm_gradient, moment_norm, second_norm, factor, GAIN_RATE))
    return (
        mixed,
        features_gradient,
        first,
        middle,
        last,
        jnp.moveaxis(embed, 0, 1),
        back,
        norm_gradient,
    ) + tuple(results[index][kind] for kind in range(3) for index in range(6)) + (gradient_norm,)


def solution(mesh):
    placed = (
        P(("clip", "chan"), None, None),
        P(("clip", "chan"), None, None),
        P(),
        P(None, "chan", None),
        P(None, "chan", None),
        P("chan", None),
        P("chan", None, None),
        P("chan", None),
        P(),
        P(None, "chan", None),
        P(None, "chan", None),
        P("chan", None),
        P("chan", None, None),
        P("chan", None),
        P(),
        P(None, "chan", None),
        P(None, "chan", None),
        P("chan", None),
        P("chan", None, None),
        P("chan", None),
        P(),
    )
    return jax.shard_map(
        body,
        mesh=mesh,
        in_specs=placed,
        out_specs=(
            P(("clip", "chan"), None, None),
            P(("clip", "chan"), None, None),
            P(),
            P(),
            P(),
            P(),
            P(),
            P(),
            P(None, "chan", None),
            P(None, "chan", None),
            P("chan", None),
            P("chan", None, None),
            P("chan", None),
            P(),
            P(None, "chan", None),
            P(None, "chan", None),
            P("chan", None),
            P("chan", None, None),
            P("chan", None),
            P(),
            P(None, "chan", None),
            P(None, "chan", None),
            P("chan", None),
            P("chan", None, None),
            P("chan", None),
            P(),
            P(),
        ),
        check_vma=False,
    )
```

```python
import functools
import math

import jax
import jax.numpy as jnp
import numpy as np
from jax import lax
from jax.experimental import pallas as pl
from jax.experimental.layout import Layout, with_layout_constraint
from jax.experimental.pallas import tpu as pltpu
from jax.sharding import PartitionSpec as P

D = 1024
BOT = 256
INNER = 512
HH = 14
WW = 14
STEP = 10
DPC = 8


EPS_NORM = 1e-05
BETA_ONE = 0.9
BETA_TWO = 0.95
ADAM_EPS = 1e-08
WEIGHT_DECAY = 0.01
CLIP_AT = 1.0
GAIN_RATE = 0.5


def flipped(value, axis, mask):
    pairs = [(source, source ^ mask) for source in range(lax.axis_size(axis))]
    return lax.ppermute(value, axis, pairs)


def whole_of(shard):
    return lax.all_gather(shard.astype(jnp.bfloat16), "chan", axis=0, tiled=False)


def quarters_of(shard):
    span = shard.shape[1] // 4
    piece = lax.dynamic_slice_in_dim(
        shard.astype(jnp.bfloat16), lax.axis_index("clip") * span, span, axis=1
    )[None]
    chips = jnp.concatenate(
        [piece] + [flipped(piece, "chan", 2 * turn) for turn in range(1, 4)]
    )[None]
    mine = jnp.concatenate([chips] + [flipped(chips, "clip", turn) for turn in range(1, 4)])
    return mine, flipped(mine, "chan", 1)


def tap_of(weights, tap):
    return weights[:, tap].reshape(weights.shape[0] * weights.shape[2], weights.shape[3])


def beside(cells, spots):
    ends = lax.axis_size("chan") - 1
    upward = [(index, index + 1) for index in range(ends)]
    downward = [(index + 1, index) for index in range(ends)]
    return (
        lax.ppermute(cells[-1:], "chan", upward).reshape(spots, cells.shape[-1]),
        lax.ppermute(cells[:1], "chan", downward).reshape(spots, cells.shape[-1]),
    )


def total(value):
    for axis in ("chan", "clip"):
        bits = lax.axis_size(axis).bit_length() - 1
        levels = list(range(bits))
        groups = [levels[:1]] if axis == "chan" else []
        rest = levels[len(groups) :]
        groups += [rest[index : index + 2] for index in range(0, len(rest), 2)]
        for group in groups:
            base = 1 << group[0]
            parts = [flipped(value, axis, base * turn) for turn in range(1, 1 << len(group))]
            value = value + sum(parts[1:], parts[0])
    return value


def level_groups(axis):
    bits = lax.axis_size(axis).bit_length() - 1
    levels = list(range(bits))
    groups = [levels[:1]] if axis == "chan" else []
    rest = levels[len(groups) :]
    return groups + [rest[index : index + 2] for index in range(0, len(rest), 2)]


def level_steps():
    order = [("chan", group) for group in level_groups("chan")]
    order = order[:1] + [("clip", group) for group in level_groups("clip")] + order[1:]
    steps = []
    for axis, group in order:
        base, count = 1 << group[0], 1 << len(group)
        steps.append((axis, base, count, (lax.axis_index(axis) >> group[0]) & (count - 1)))
    return steps


def half_kernel(mine, arrived, out_ref):
    out_ref[...] = (mine[...].astype(F32) + arrived[...].astype(F32)).astype(LOW)


def core_step(mine, others):
    arrived = flipped(others, "chan", 1)
    return call(half_kernel, [(mine.shape, LOW)], (mine, arrived), scalars=0)[0]


def deal(place, halves, mine, others, sems):
    copies = [
        pltpu.make_async_copy(halves.at[place[0]], mine, sems.at[0]),
        pltpu.make_async_copy(halves.at[1 - place[0]], others, sems.at[1]),
    ]
    for copy in copies:
        copy.start()
    for copy in copies:
        copy.wait()


def put_rows(halves, at, values):
    size = halves.shape[1]
    cut = max(0, min(values.shape[0], size - at))
    if cut:
        halves[0, pl.ds(at, cut), :] = values[:cut]
    if cut < values.shape[0]:
        halves[1, pl.ds(at + cut - size, values.shape[0] - cut), :] = values[cut:]


def scatter_sum(value, steps):
    for axis, base, count, place in steps:
        size = value.shape[0] // count
        mine = lax.dynamic_slice_in_dim(value, place * size, size).astype(F32)
        arrived = [
            flipped(
                lax.dynamic_slice_in_dim(value, (place ^ turn) * size, size), axis, base * turn
            )
            for turn in range(1, count)
        ]
        for item in arrived:
            mine = mine + item.astype(F32)
        value = mine.astype(LOW)
    return value


def laid_out(rows, frames):
    grid = rows.reshape(frames, -1, rows.shape[1])
    return with_layout_constraint(grid, Layout(major_to_minor=(1, 0, 2)))


def tied(*values):
    return lax.optimization_barrier(values)


def gather_sum(value, steps):
    for axis, base, count, place in reversed(steps):
        size = value.shape[0]
        parts = [value] + [flipped(value, axis, base * turn) for turn in range(1, count)]
        whole = jnp.zeros((count,) + value.shape, LOW)
        for turn, part in enumerate(parts):
            whole = lax.dynamic_update_index_in_dim(whole, part, place ^ turn, 0)
        value = whole.reshape((count * size,) + value.shape[1:])
    return value


NEG = -1e30
MIB = 1 << 20
NN = (((1,), (0,)), ((), ()))
NT = (((1,), (1,)), ((), ()))
TN = (((0,), (0,)), ((), ()))
F32 = jnp.float32
LOW = jnp.bfloat16


def dot(left, right, dims=NN):
    return lax.dot_general(left, right, dims, preferred_element_type=F32)


def sig(values):
    return 0.5 * jnp.tanh(0.5 * values) + 0.5


def slope(values):
    gate = sig(values)
    return gate * (1.0 + values * (1.0 - gate))


def moments(sums, inverse):
    mean = sums[0:1] * inverse
    return mean, lax.rsqrt(sums[1:2] * inverse - mean * mean + EPS_NORM)


def column_sums(values):
    return jnp.sum(values, axis=0, keepdims=True)


def call(kernel, outs, args, scalars=1, scratch=(), vmem=16, far=(), far_out=(), micros=2):
    spaces = []
    for index in range(len(args)):
        if index < scalars:
            spaces.append(pl.BlockSpec(memory_space=pltpu.SMEM))
        elif index in far:
            spaces.append(pl.BlockSpec(memory_space=pltpu.HBM))
        else:
            spaces.append(pl.BlockSpec(memory_space=pltpu.VMEM))
    shapes = tuple(jax.ShapeDtypeStruct(shape, dtype) for shape, dtype in outs)
    out_specs = tuple(
        pl.BlockSpec(memory_space=pltpu.HBM if index in far_out else pltpu.VMEM)
        for index in range(len(outs))
    )
    return pl.pallas_call(
        kernel,
        out_shape=shapes,
        in_specs=spaces,
        out_specs=out_specs,
        scratch_shapes=list(scratch),
        compiler_params=pltpu.CompilerParams(vmem_limit_bytes=vmem * MIB),
        cost_estimate=pl.CostEstimate(
            flops=int(micros * 1e9), bytes_accessed=0, transcendentals=0
        ),
    )(*args)


def first_tail(flags, cells, before, after, weights, pre_ref, sums_ref, early, late):
    rows = cells.shape[0]
    spots = before.shape[0]
    valid = flags[0]
    late[pl.ds(0, rows), :] = dot(cells[...], tap_of(weights, 2)) * valid
    late[pl.ds(rows, spots), :] = dot(after[...], tap_of(weights, 2)) * flags[2]
    early[pl.ds(0, spots), :] = dot(before[...], tap_of(weights, 0)) * flags[1]
    early[pl.ds(spots, rows), :] = dot(cells[...], tap_of(weights, 0)) * valid
    pre = (
        dot(cells[...], tap_of(weights, 1)) * valid
        + early[pl.ds(0, rows), :]
        + late[pl.ds(spots, rows), :]
    )
    pre_ref[...] = pre
    sums_ref[0:1, :] = column_sums(pre) * valid
    sums_ref[1:2, :] = column_sums(pre * pre) * valid


def first_parts_kernel(place, flags, cells, before, after, mine, others, pre_ref, sums_ref, weights, early, late):
    for index in range(mine.shape[0]):
        span = mine.shape[3]
        rows = pl.ds(pl.multiple_of((place[2] ^ index) * span, span), span)
        for turn in range(mine.shape[1]):
            weights[place[1] ^ (2 * turn), :, rows, :] = mine[index, turn]
            weights[place[1] ^ (2 * turn + 1), :, rows, :] = others[index, turn]
    first_tail(flags, cells, before, after, weights, pre_ref, sums_ref, early, late)


def first_conv_parts(place, flags, cells, before, after, mine, others):
    rows = cells.shape[0]
    clips, chips, taps, span, narrow = mine.shape
    spots = before.shape[0]
    return call(
        first_parts_kernel,
        [
            ((rows, narrow), F32),
            ((2, narrow), F32),
            ((2 * chips, taps, clips * span, narrow), LOW),
        ],
        (place, flags, cells, before, after, mine, others),
        scalars=2,
        scratch=[pltpu.VMEM((rows + spots, narrow), F32)] * 2,
    )


def first_conv(flags, cells, before, after, weights):
    rows, width = cells.shape
    narrow = weights.shape[3]
    spots = before.shape[0]
    return call(
        first_tail,
        [((rows, narrow), F32), ((2, narrow), F32)],
        (flags, cells, before, after, weights),
        scratch=[pltpu.VMEM((rows + spots, narrow), F32)] * 2,
    )


def spread(values, edges, buffer, columns, rows):
    narrow = values.shape[1]
    margin = 16
    buffer[0, pl.ds(0, margin), :] = jnp.zeros((margin, narrow), F32)
    buffer[0, pl.ds(margin + rows, margin), :] = jnp.zeros((margin, narrow), F32)
    buffer[1, pl.ds(0, margin), :] = jnp.zeros((margin, narrow), F32)
    buffer[1, pl.ds(margin + rows, margin), :] = jnp.zeros((margin, narrow), F32)
    buffer[0, pl.ds(margin, rows), :] = values
    for across in range(3):
        moved = buffer[0, pl.ds(margin + across - 1, rows), :]
        if across == 0:
            moved = moved * edges[:, 0:1]
        if across == 2:
            moved = moved * edges[:, 1:2]
        buffer[1, pl.ds(margin, rows), :] = moved
        for down in range(3):
            part = buffer[1, pl.ds(margin + WW * (down - 1), rows), :]
            if down == 0:
                part = part * edges[:, 2:3]
            if down == 2:
                part = part * edges[:, 3:4]
            at = (3 * down + across) * narrow
            columns[:, at : at + narrow] = part.astype(LOW)


def spread_scratch(rows, narrow):
    return [pltpu.VMEM((2, rows + 32, narrow), F32), pltpu.VMEM((rows, 9 * narrow), LOW)]


def act_of(flags, pre, sums, scale_shift):
    mean, scale = moments(sums, flags[3])
    normal = (pre - mean) * scale
    return normal, normal * scale_shift[0:1] + scale_shift[1:2], scale


def middle_kernel(flags, pre, sums, gains, weights, edges, out_ref, sums_ref, buffer, columns):
    rows, narrow = pre.shape
    valid = flags[0]
    _, act, _ = act_of(flags, pre[...], sums[...], gains[...])
    spread(act * sig(act) * valid, edges[...], buffer, columns, rows)
    out = None
    for tap in range(9):
        part = dot(columns[:, tap * narrow : (tap + 1) * narrow], tap_of(weights, tap))
        out = part if out is None else out + part
    out_ref[...] = out
    sums_ref[0:1, :] = column_sums(out) * valid
    sums_ref[1:2, :] = column_sums(out * out) * valid


def middle_conv(flags, pre, sums, gains, weights, edges):
    rows, narrow = pre.shape
    return call(
        middle_kernel,
        [((rows, narrow), F32), ((2, narrow), F32)],
        (flags, pre, sums, gains, weights, edges),
        scratch=spread_scratch(rows, narrow),
    )


def last_kernel(flags, pre, sums, gains, weights, act_ref, sums_ref):
    valid = flags[0]
    _, act, _ = act_of(flags, pre[...], sums[...], gains[...])
    act_ref[...] = (act * sig(act) * valid).astype(LOW)
    for at in range(0, weights.shape[1], 256):
        out = dot(act_ref[...], weights[:, at : at + 256])
        sums_ref[0:1, at : at + 256] = column_sums(out) * valid
        sums_ref[1:2, at : at + 256] = column_sums(out * out) * valid


def last_conv(flags, pre, sums, gains, weights):
    rows, narrow = pre.shape
    width = weights.shape[1]
    return call(
        last_kernel,
        [((rows, narrow), LOW), ((2, width), F32)],
        (flags, pre, sums, gains, weights),
    )


def residual_tile(flags, act, cells, weights, sums, gains, at):
    mean, scale = moments(sums[:, at : at + 256], flags[3])
    normal = (dot(act[...], weights[:, at : at + 256]) - mean) * scale
    pre = cells[:, at : at + 256].astype(F32) + (
        normal * gains[0:1, at : at + 256] + gains[1:2, at : at + 256]
    )
    return normal, pre, scale


def embed_kernel(flags, act, cells, weights, sums, gains, embed, res_ref, query_ref, pair_ref):
    width = weights.shape[1]
    inner = query_ref.shape[1]
    for at in range(0, width, 256):
        _, pre, _ = residual_tile(flags, act, cells, weights, sums, gains, at)
        res_ref[:, at : at + 256] = (pre * sig(pre) * flags[0]).astype(LOW)
    for at in range(0, inner, 256):
        query_ref[:, at : at + 256] = dot(res_ref[...], embed[:, at : at + 256]).astype(LOW)
    for at in range(0, 2 * inner, 256):
        pair_ref[:, at : at + 256] = dot(
            res_ref[...], embed[:, inner + at : inner + at + 256]
        ).astype(LOW)


def embed_rows(flags, act, cells, weights, sums, gains, embed):
    rows, width = cells.shape
    inner = embed.shape[1] // 3
    return call(
        embed_kernel,
        [((rows, width), LOW), ((rows, inner), LOW), ((rows, 2 * inner), LOW)],
        (flags, act, cells, weights, sums, gains, embed),
        micros=7,
    )


def copies_of(refs, slots, sems):
    return [
        pltpu.make_async_copy(ref, slots.at[index], sems.at[index])
        for index, ref in enumerate(refs)
    ]


def attend_kernel(
    away, count, query, one, two, three, four, out_ref, log_ref, pairs, tails, scores, total, peak, sums, sems
):
    rows, inner = query.shape
    full = rows // 256 * 256
    rest = rows - full
    wide = 4 * rest
    turn = inner**-0.5 * math.log2(math.e)
    blocks = count[0]
    copies = copies_of((one, two, three, four), pairs, sems)
    for copy in copies:
        copy.start()

    @pl.when(blocks == 0)
    def _():
        out_ref[...] = jnp.zeros_like(out_ref)
        if away:
            log_ref[...] = jnp.zeros_like(log_ref)
            log_ref[0:1, :] = jnp.full((1, log_ref.shape[1]), NEG, F32)
        else:
            log_ref[...] = jnp.full_like(log_ref, NEG)

    peak[...] = jnp.full_like(peak, NEG)
    sums[...] = jnp.zeros_like(sums)

    def score(index, _):
        pltpu.make_async_copy(one, pairs.at[index], sems.at[index]).wait()

        @pl.when(index < blocks)
        def _():
            found = dot(query[...], pairs[index, pl.ds(0, full), :inner], NT)
            scores[index] = found
            top = peak[...]
            for at in range(0, full, 128):
                top = jnp.maximum(top, found[:, at : at + 128])
            peak[...] = top

        return 0

    lax.fori_loop(0, 4, score, 0)

    @pl.when(blocks > 0)
    def _():
        for index in range(4):
            tails[pl.ds(index * rest, rest), :] = pairs[index, pl.ds(full, rest), :]
        lane = lax.broadcasted_iota(jnp.int32, (rows, wide), 1)
        end = jnp.where(lane < blocks * rest, dot(query[...], tails[:, :inner], NT), NEG)
        top = jnp.maximum(
            jnp.max(peak[...], axis=1, keepdims=True), jnp.max(end, axis=1, keepdims=True)
        )
        top = top * turn
        lifted = jnp.exp2(end * turn - top)
        end_sum = jnp.sum(lifted, axis=1, keepdims=True)
        total[...] = dot(lifted.astype(LOW), tails[:, inner:])
        peak[...] = jnp.broadcast_to(top, peak.shape)

        def weigh(index, _):
            base = peak[...]
            running = sums[...]
            parts = []
            for at in range(0, full, 128):
                part = jnp.exp2(scores[index, :, at : at + 128] * turn - base)
                running = running + part
                parts.append(part.astype(LOW))
            sums[...] = running
            total[...] += dot(
                jnp.concatenate(parts, axis=1), pairs[index, pl.ds(0, full), inner:]
            )
            return 0

        lax.fori_loop(0, blocks, weigh, 0)
        found = jnp.sum(sums[...], axis=1, keepdims=True) + end_sum
        logs = jnp.broadcast_to(top + jnp.log2(found), peak.shape)
        if away:
            out = total[...] / found
            mean = column_sums(out) * (1.0 / rows)
            out_ref[...] = (out - mean).astype(out_ref.dtype)
            log_ref[...] = row_of(logs, log_ref.shape[1])
            log_ref[1:2, :inner] = mean
        else:
            out_ref[...] = (total[...] / found).astype(out_ref.dtype)
            log_ref[...] = logs


def attend(count, query, blocks, away):
    rows, inner = query.shape
    span = -(-rows // 128) * 128
    full = rows // 256 * 256
    rest = rows - full
    return call(
        functools.partial(attend_kernel, away),
        [((rows, inner), LOW), ((8, span) if away else (rows, 128), F32)],
        (count, query) + tuple(blocks),
        scratch=[
            pltpu.VMEM((4, rows, 2 * inner), LOW),
            pltpu.VMEM((4 * rest, 2 * inner), LOW),
            pltpu.VMEM((4, rows, full), F32),
            pltpu.VMEM((rows, inner), F32),
            pltpu.VMEM((rows, 128), F32),
            pltpu.VMEM((rows, 128), F32),
            pltpu.SemaphoreType.DMA((4,)),
        ],
        vmem=36,
        far=(2, 3, 4, 5),
        micros=10,
    )


def attend_back_kernel(away, held, split, count, query, grad, *refs):
    size = len(held)
    refs = list(refs)
    if away:
        packed = refs.pop(0)
    else:
        log_ref, term_ref = refs.pop(0), refs.pop(0)
    given_query = refs.pop(0) if away and held[0] == 0 else None
    blocks_in = [refs.pop(0) for _ in held]
    given = [refs.pop(0) for _ in held] if away else ()
    query_ref = refs.pop(0)
    outs = [[refs.pop(0) for _ in range(2 if place in split else 1)] for place in held]
    pairs, tails, stage, stage_tails, total, sems, out_sems = refs[:7]
    if away:
        log_ref, term_ref, in_sems = refs[7:]
    rows, inner = query.shape
    full = rows // 256 * 256
    rest = rows - full
    wide = size * rest
    scaling = inner**-0.5
    turn = scaling * math.log2(math.e)
    blocks = count[0]

    def main_of(ref):
        return ref.at[pl.ds(0, full)]

    def tail_of(ref):
        return ref.at[pl.ds(full, rest)]

    def tail_at(index):
        return pl.ds(index * rest, rest)

    begin = [
        pltpu.make_async_copy(tail_of(ref), tails.at[tail_at(index)], sems.at[1, index])
        for index, ref in enumerate(blocks_in)
    ] + [
        pltpu.make_async_copy(tail_of(ref), stage_tails.at[tail_at(index)], in_sems.at[1, index])
        for index, ref in enumerate(given)
    ]
    for copy in begin:
        copy.start()
    for index in range(size):
        pltpu.make_async_copy(main_of(blocks_in[index]), pairs.at[index], sems.at[0, index]).start()
        if away:
            pltpu.make_async_copy(main_of(given[index]), stage.at[index], in_sems.at[0, index]).start()
    if away:
        log_ref[...] = column_of(packed[0:1, :])[:rows]
        term_ref[...] = column_of(packed[1:2, :])[:rows]
    for copy in begin:
        copy.wait()

    def tile(keys, values, span, mask):
        found = dot(query[...], keys, NT)
        back = dot(grad[...], values, NT)
        logs = log_ref[...]
        terms = term_ref[...]
        kept = []
        slopes = []
        for at in range(0, span, 128):
            end = min(at + 128, span)
            weight = jnp.exp2(found[:, at:end] * turn - logs[:, : end - at])
            if mask is not None:
                weight = jnp.where(mask, weight, 0.0)
            kept.append(weight.astype(LOW))
            slopes.append((weight * (back[:, at:end] - terms[:, : end - at])).astype(LOW))
        kept = kept[0] if len(kept) == 1 else jnp.concatenate(kept, axis=1)
        slopes = slopes[0] if len(slopes) == 1 else jnp.concatenate(slopes, axis=1)
        return slopes, dot(slopes, query[...], TN) * scaling, dot(kept, grad[...], TN)

    active = blocks > held[0]

    @pl.when(jnp.logical_not(active))
    def _():
        if given_query is None:
            query_ref[...] = jnp.zeros_like(query_ref)
        else:
            query_ref[...] = given_query[...].astype(query_ref.dtype)
        if not away:
            stage_tails[...] = jnp.zeros_like(stage_tails)

    @pl.when(active)
    def _():
        keys = tails[:, :inner]
        lane = lax.broadcasted_iota(jnp.int32, (rows, wide), 1)
        ok = lane < (blocks - held[0]) * rest
        slopes, key_part, value_part = tile(keys, tails[:, inner:], wide, ok)
        total[...] = dot(slopes, keys)
        if away:
            key_part = key_part + stage_tails[:, :inner].astype(F32)
            value_part = value_part + stage_tails[:, inner:].astype(F32)
        stage_tails[:, :inner] = key_part.astype(LOW)
        stage_tails[:, inner:] = value_part.astype(LOW)

    def columns(which, part):
        width = 2 * inner // len(outs[which])
        return pl.ds(part * width, width)

    def main_outs(which):
        return [
            pltpu.make_async_copy(
                stage.at[which, :, columns(which, part)], main_of(ref), out_sems.at[0, which, part]
            )
            for part, ref in enumerate(outs[which])
        ]

    def one_block(index, _):
        pltpu.make_async_copy(main_of(blocks_in[0]), pairs.at[index], sems.at[0, index]).wait()
        if away:
            pltpu.make_async_copy(main_of(given[0]), stage.at[index], in_sems.at[0, index]).wait()

        @pl.when(index < blocks - held[0])
        def _():
            block = pairs[index, :, :inner]
            slopes, key_part, value_part = tile(block, pairs[index, :, inner:], full, None)
            total[...] += dot(slopes, block)
            if away:
                key_part = key_part + stage[index, :, :inner].astype(F32)
                value_part = value_part + stage[index, :, inner:].astype(F32)
            stage[index, :, :inner] = key_part.astype(LOW)
            stage[index, :, inner:] = value_part.astype(LOW)

        if not away:

            @pl.when(index >= blocks - held[0])
            def _():
                stage[index] = jnp.zeros(stage.shape[1:], LOW)

        for which in range(size):

            @pl.when(index == which)
            def _():
                for copy in main_outs(which):
                    copy.start()

        return 0

    lax.fori_loop(0, size, one_block, 0)
    ends = [
        pltpu.make_async_copy(
            stage_tails.at[tail_at(index), columns(index, part)],
            tail_of(ref),
            out_sems.at[1, index, part],
        )
        for index in range(size)
        for part, ref in enumerate(outs[index])
    ]
    for copy in ends:
        copy.start()

    @pl.when(active)
    def _():
        found = total[...] * scaling
        if given_query is not None:
            found = found + given_query[...]
        query_ref[...] = found.astype(query_ref.dtype)

    for index in range(size):
        for copy in main_outs(index):
            copy.wait()
    for copy in ends:
        copy.wait()


def attend_back(
    count, query, grad, terms, blocks, held, given, given_query, out_type, split=()
):
    rows, inner = query.shape
    full = rows // 256 * 256
    rest = rows - full
    away = given is not None
    size = len(held)
    more = () if given_query is None else (given_query,)
    near = (count, query, grad) + tuple(terms) + more
    distant = tuple(blocks) + (tuple(given) if away else ())
    scratch = [
        pltpu.VMEM((size, full, 2 * inner), LOW),
        pltpu.VMEM((size * rest, 2 * inner), LOW),
        pltpu.VMEM((size, full, 2 * inner), LOW),
        pltpu.VMEM((size * rest, 2 * inner), LOW),
        pltpu.VMEM((rows, inner), F32),
        pltpu.SemaphoreType.DMA((2, size)),
        pltpu.SemaphoreType.DMA((2, size, 2)),
    ]
    widths = []
    for at in held:
        widths += [inner] * 2 if at in split else [2 * inner]
    if away:
        scratch += [pltpu.VMEM((rows, 128), F32)] * 2 + [pltpu.SemaphoreType.DMA((2, size))]
    found = call(
        functools.partial(attend_back_kernel, away, held, split),
        [((rows, inner), out_type)] + [((rows, width), LOW) for width in widths],
        near + distant,
        scratch=scratch,
        vmem=36,
        far=tuple(range(len(near), len(near) + len(distant))),
        far_out=tuple(range(1, 1 + len(widths))),
        micros=17,
    )
    return found[0], found[1:]


def column_of(row):
    return jnp.transpose(jnp.broadcast_to(row, (128, row.shape[1])))


def row_of(column, span):
    tall = jnp.concatenate([column, jnp.zeros((span - column.shape[0], 128), F32)], axis=0)
    return jnp.transpose(tall)[0:8, :]


def merge_kernel(
    flags, own, own_log, far, far_log, weights, cot, out_ref, log_ref, sums_ref
):
    rows, inner = own.shape
    logs = own_log[...]
    others = column_of(far_log[0:1, :])[:rows]
    top = jnp.maximum(logs, others)
    whole = top + jnp.log2(jnp.exp2(logs - top) + jnp.exp2(others - top))
    log_ref[...] = whole
    share = jnp.exp2(logs - whole)
    other = jnp.exp2(others - whole)
    for at in range(0, inner, 128):
        out_ref[:, at : at + 128] = (
            own[:, at : at + 128].astype(F32) * share + (far[:, at : at + 128].astype(F32) + far_log[1:2, at : at + 128]) * other
        ).astype(LOW)
    valid = flags[0]
    for at in range(0, weights.shape[1], 256):
        out = dot(out_ref[...], weights[:, at : at + 256])
        grad = cot[:, at : at + 256].astype(F32)
        sums_ref[0:1, at : at + 256] = column_sums(out) * valid
        sums_ref[1:2, at : at + 256] = column_sums(out * out) * valid
        sums_ref[2:3, at : at + 256] = column_sums(grad) * valid
        sums_ref[3:4, at : at + 256] = column_sums(grad * out) * valid
    sums_ref[4:5, :] = jnp.zeros((1, weights.shape[1]), F32)
    sums_ref[4:5, :inner] = column_sums(out_ref[...].astype(F32)) * valid


def merge(flags, own, own_log, far, far_log, weights, cot):
    rows, inner = own.shape
    width = weights.shape[1]
    return call(
        merge_kernel,
        [((rows, inner), LOW), ((rows, 128), F32), ((5, width), F32)],
        (flags, own, own_log, far, far_log, weights, cot),
    )


def outer_kernel(
    flags,
    att,
    weights,
    sums,
    gains,
    cot,
    res,
    logs,
    mixed_ref,
    grad_ref,
    back_ref,
    term_ref,
    rows_ref,
    norm_ref,
):
    valid = flags[0]
    inverse = flags[3]
    width = weights.shape[1]
    for at in range(0, width, 256):
        span = slice(at, at + 256)
        mean, scale = moments(sums[0:2, span], inverse)
        normal = (dot(att[...], weights[:, span]) - mean) * scale
        gain = gains[0:1, span]
        mixed_ref[:, span] = (
            (res[:, span].astype(F32) + (normal * gain + gains[1:2, span])) * valid
        ).astype(LOW)
        shift_grad = sums[2:3, span]
        gain_grad = scale * (sums[3:4, span] - mean * shift_grad)
        norm_ref[0:1, span] = gain_grad
        norm_ref[1:2, span] = shift_grad
        removed = (shift_grad + normal * gain_grad) * inverse
        grad = ((gain * scale * valid) * (cot[:, span].astype(F32) - removed)).astype(LOW)
        grad_ref[:, span] = grad
        norm_ref[2:3, span] = column_sums(grad.astype(F32))
    back = dot(grad_ref[...], weights[...], NT).astype(LOW)
    back_ref[...] = back
    term = jnp.sum(back.astype(F32) * att[...].astype(F32), axis=1, keepdims=True)
    term = jnp.broadcast_to(term, term_ref.shape)
    term_ref[...] = term
    rows_ref[...] = row_of(logs[...], rows_ref.shape[1])
    rows_ref[1:2, :] = row_of(term, rows_ref.shape[1])[0:1]


def outer(flags, att, weights, sums, gains, cot, res, logs):
    rows, inner = att.shape
    width = weights.shape[1]
    span = -(-rows // 128) * 128
    return call(
        outer_kernel,
        [
            ((rows, width), LOW),
            ((rows, width), LOW),
            ((rows, inner), LOW),
            ((rows, 128), F32),
            ((8, span), F32),
            ((3, width), F32),
        ],
        (flags, att, weights, sums, gains, cot, res, logs),
        micros=5,
    )


def project_kernel(
    flags,
    query_own,
    query_far,
    keep,
    near_keys,
    near_values,
    far,
    act,
    cells,
    weights,
    sums,
    gains,
    embed_far,
    cot_far,
    proj_ref,
    pre_ref,
    sums_ref,
    embed,
    cot,
    sems,
):
    valid = flags[0]
    inner = query_own.shape[1]
    copies = [
        pltpu.make_async_copy(embed_far, embed, sems.at[0]),
        pltpu.make_async_copy(cot_far, cot, sems.at[1]),
    ]
    for copy in copies:
        copy.start()
    proj_ref[:, :inner] = (query_own[...].astype(F32) + query_far[...].astype(F32)).astype(LOW)
    for at in range(0, 2 * inner, 256):
        span = slice(at, at + 256)
        near = near_keys[:, span] if at < inner else near_values[:, at - inner : at - inner + 256]
        proj_ref[:, inner + at : inner + at + 256] = (
            keep[:, span].astype(F32) + near.astype(F32) + far[:, span].astype(F32)
        ).astype(LOW)
    for copy in copies:
        copy.wait()
    for at in range(0, weights.shape[1], 256):
        span = slice(at, at + 256)
        normal, pre, _ = residual_tile(flags, act, cells, weights, sums, gains, at)
        grad = cot[:, span].astype(F32) + dot(proj_ref[...], embed[span, :], NT)
        out = grad * valid * slope(pre)
        pre_ref[:, span] = out
        sums_ref[0:1, span] = column_sums(out)
        sums_ref[1:2, span] = column_sums(out * normal)


def project_back(flags, query_own, query_far, keep, near_keys, near_values, far, act, cells, weights, sums, gains, embed, cot):
    rows, width = cells.shape
    inner = query_own.shape[1]
    return call(
        project_kernel,
        [((rows, 3 * inner), LOW), ((rows, width), F32), ((2, width), F32)],
        (flags, query_own, query_far, keep, near_keys, near_values, far, act, cells, weights, sums, gains, embed, cot),
        scratch=[
            pltpu.VMEM(embed.shape, LOW),
            pltpu.VMEM(cot.shape, LOW),
            pltpu.SemaphoreType.DMA((2,)),
        ],
        far=(12, 13),
        micros=10,
    )


def last_back_kernel(
    flags, pre_grad, act, weights, sums, gains, back_sums, pre_two, sums_two, gains_two, grad_ref, two_ref, sums_ref
):
    valid = flags[0]
    inverse = flags[3]
    two = None
    for at in range(0, weights.shape[1], 256):
        span = slice(at, at + 256)
        mean, scale = moments(sums[:, span], inverse)
        normal = (dot(act[...], weights[:, span]) - mean) * scale
        removed = (back_sums[0:1, span] + normal * back_sums[1:2, span]) * inverse
        grad = ((gains[0:1, span] * scale * valid) * (pre_grad[:, span] - removed)).astype(LOW)
        grad_ref[:, span] = grad
        part = dot(grad, weights[:, span], NT)
        two = part if two is None else two + part
    normal, active, _ = act_of(flags, pre_two[...], sums_two[...], gains_two[...])
    two = two * valid * slope(active)
    two_ref[...] = two
    sums_ref[0:1, :] = column_sums(two)
    sums_ref[1:2, :] = column_sums(two * normal)


def last_back(flags, pre_grad, act, weights, sums, gains, back_sums, pre_two, sums_two, gains_two):
    rows, width = pre_grad.shape
    narrow = act.shape[1]
    return call(
        last_back_kernel,
        [((rows, width), LOW), ((rows, narrow), F32), ((2, narrow), F32)],
        (flags, pre_grad, act, weights, sums, gains, back_sums, pre_two, sums_two, gains_two),
    )


def middle_back_kernel(
    flags, two, back_sums, pre_two, sums_two, gains_two, pre_one, sums_one, gains_one, weights, edges,
    grad_ref, one_ref, sums_ref, buffer, columns
):
    rows, narrow = two.shape
    valid = flags[0]
    inverse = flags[3]
    normal, _, scale = act_of(flags, pre_two[...], sums_two[...], gains_two[...])
    removed = (back_sums[0:1] + normal * back_sums[1:2]) * inverse
    grad = (gains_two[0:1, :] * scale * valid) * (two[...] - removed)
    grad_ref[...] = grad.astype(LOW)
    spread(grad, edges[...], buffer, columns, rows)
    one = None
    for tap in range(9):
        part = dot(columns[:, tap * narrow : (tap + 1) * narrow], tap_of(weights, 8 - tap), NT)
        one = part if one is None else one + part
    normal, active, _ = act_of(flags, pre_one[...], sums_one[...], gains_one[...])
    one = one * valid * slope(active)
    one_ref[...] = one
    sums_ref[0:1, :] = column_sums(one)
    sums_ref[1:2, :] = column_sums(one * normal)


def middle_back(flags, two, back_sums, pre_two, sums_two, gains_two, pre_one, sums_one, gains_one, weights, edges):
    rows, narrow = two.shape
    return call(
        middle_back_kernel,
        [((rows, narrow), LOW), ((rows, narrow), F32), ((2, narrow), F32)],
        (flags, two, back_sums, pre_two, sums_two, gains_two, pre_one, sums_one, gains_one, weights, edges),
        scratch=spread_scratch(rows, narrow),
    )


def middle_weight_kernel(flags, pre_one, sums_one, gains_one, grad, edges, out_ref, buffer, columns):
    rows, narrow = pre_one.shape
    _, act, _ = act_of(flags, pre_one[...], sums_one[...], gains_one[...])
    spread(act * sig(act) * flags[0], edges[...], buffer, columns, rows)
    for tap in range(9):
        out_ref[pl.ds(tap * narrow, narrow), :] = dot(
            columns[:, tap * narrow : (tap + 1) * narrow], grad[...], TN
        ).astype(LOW)


def middle_weight(flags, pre_one, sums_one, gains_one, grad, edges):
    rows, narrow = pre_one.shape
    return call(
        middle_weight_kernel,
        [((9 * narrow, narrow), LOW)],
        (flags, pre_one, sums_one, gains_one, grad, edges),
        scratch=spread_scratch(rows, narrow),
    )[0]


def first_grad_kernel(flags, one, back_sums, pre_one, sums_one, gains_one, grad_ref):
    normal, _, scale = act_of(flags, pre_one[...], sums_one[...], gains_one[...])
    removed = (back_sums[0:1] + normal * back_sums[1:2]) * flags[3]
    grad_ref[...] = (
        (gains_one[0:1, :] * scale * flags[0]) * (one[...] - removed)
    ).astype(LOW)


def first_grad_of(flags, one, back_sums, pre_one, sums_one, gains_one):
    rows, narrow = one.shape
    return call(
        first_grad_kernel,
        [((rows, narrow), LOW)],
        (flags, one, back_sums, pre_one, sums_one, gains_one),
    )[0]


def first_back_kernel(
    place, flags, grad, before, after, cells, middle, last, mine, others, cols_ref, buffer, halves, sems
):
    rows, narrow = grad.shape
    width = cells.shape[1]
    spots = before.shape[0]
    buffer[pl.ds(0, spots), :] = before[...].astype(F32) * flags[1]
    buffer[pl.ds(spots, rows), :] = grad[...].astype(F32)
    buffer[pl.ds(spots + rows, spots), :] = after[...].astype(F32) * flags[2]
    at = middle.shape[0]
    put_rows(halves, 0, middle[...])
    for tap in range(3):
        part = (buffer[pl.ds(spots * (2 - tap), rows), :] * flags[0]).astype(LOW)
        cols_ref[:, tap * narrow : (tap + 1) * narrow] = part
        put_rows(halves, at, dot(cells[...], part, TN).astype(LOW))
        at += width
    put_rows(halves, at, last[...])
    deal(place, halves, mine, others, sems)


def first_back(place, flags, grad, before, after, cells, middle, last):
    rows, narrow = grad.shape
    spots = before.shape[0]
    width = cells.shape[1]
    mine, others, cols = halves_call(
        first_back_kernel,
        middle.shape[0] + 3 * width + last.shape[0],
        [((rows, 3 * narrow), LOW)],
        (place, flags, grad, before, after, cells, middle, last),
        scratch=[pltpu.VMEM((rows + 2 * spots, narrow), F32)],
    )
    return (mine, others), cols


def early_weight_kernel(
    place, flags, res, proj, att, sums, grad, mine, others, halves, sems
):
    height, inner = res.shape[1], att.shape[1]
    left = (att[...].astype(F32) - sums[...] * flags[3]).astype(LOW)
    at = 0
    for index in range(proj.shape[1] // 256):
        put_rows(
            halves, at, dot(res[...], proj[:, index * 256 : (index + 1) * 256], TN).astype(LOW)
        )
        at += height
    for index in range(grad.shape[1] // 256):
        put_rows(
            halves, at, dot(left, grad[:, index * 256 : (index + 1) * 256], TN).astype(LOW)
        )
        at += inner
    deal(place, halves, mine, others, sems)


def halves_call(kernel, height, outs, args, scratch=()):
    shape = (height // 2, 256)
    return call(
        kernel,
        [(shape, LOW), (shape, LOW)] + outs,
        args,
        scalars=2,
        scratch=list(scratch)
        + [pltpu.VMEM((2,) + shape, LOW), pltpu.SemaphoreType.DMA((2,))],
        far_out=(0, 1),
        micros=8,
    )


def early_weight(place, flags, res, proj, att, sums, grad):
    height = res.shape[1] * proj.shape[1] // 256 + att.shape[1] * grad.shape[1] // 256
    return halves_call(
        early_weight_kernel, height, [], (place, flags, res, proj, att, sums, grad)
    )


def weight_kernel(left, right, out_ref):
    height = left.shape[1]
    for index in range(right.shape[1] // 256):
        out_ref[pl.ds(index * height, height), :] = dot(
            left[...], right[:, index * 256 : (index + 1) * 256], TN
        ).astype(LOW)


def weight_grad(left, right):
    rows, height = left.shape
    width = right.shape[1]
    return call(
        weight_kernel,
        [((height * width // 256, 256), LOW)],
        (left, right),
        scalars=0,
    )[0]


def pieces_of(low_half, high_half, start, stop):
    middle = low_half.shape[0]
    if start < middle:
        yield 0, low_half[pl.ds(start, min(stop, middle) - start), :]
    if stop > middle:
        begin = max(start, middle)
        yield begin - start, high_half[pl.ds(begin - middle, stop - begin), :]


def squares_of(values):
    return jnp.sum((values * values).reshape(-1, 8, values.shape[-1]), axis=0)


def emit(place, half, other, shares, squares):
    def write(low_half, high_half):
        squares[...] = jnp.zeros_like(squares)
        for start, stop, store, extra in shares:
            for offset, rows in pieces_of(low_half, high_half, start, stop):
                values = rows.astype(F32)
                if extra is not None:
                    values = values + extra[offset : offset + values.shape[0]]
                squares[...] += squares_of(values)
                store(offset, values)

    @pl.when(place[0] == 0)
    def _():
        write(half, other)

    @pl.when(place[0] == 1)
    def _():
        write(other, half)


def store_rows(ref, lead, cols):
    def store(offset, values):
        ref[lead + (pl.ds(offset, values.shape[0]), cols)] = values

    return store


def early_shares(embed_ref, back_ref, mean, grad_sum):
    width, inner = embed_ref.shape[1], embed_ref.shape[2]
    shares = []
    at = 0
    for index in range(3 * inner // 256):
        part, col = divmod(index * 256, inner)
        shares.append((at, at + width, store_rows(embed_ref, (part,), slice(col, col + 256)), None))
        at += width
    for index in range(width // 256):
        cols = slice(index * 256, index * 256 + 256)
        extra = mean[:, 0:1] * grad_sum[0:1, cols]
        shares.append((at, at + inner, store_rows(back_ref, (), cols), extra))
        at += inner
    return shares


def early_kernel(place, flags, half, other, sums, grad_sum, embed_ref, back_ref, embed_own, back_own, squares_ref):
    mean = sums[...] * flags[3]
    emit(place, half, other, early_shares(embed_ref, back_ref, column_of(mean), grad_sum), squares_ref)
    span = embed_own.shape[1]
    embed_own[...] = embed_ref[:, pl.ds(pl.multiple_of(place[1] * span, span), span), :]
    span = back_own.shape[0]
    back_own[...] = back_ref[pl.ds(pl.multiple_of(place[1] * span, span), span), :]


def early_grads(place, flags, half, other, sums, grad_sum, width, inner, shards):
    return call(
        early_kernel,
        [
            ((3, width, inner), F32),
            ((inner, width), F32),
            ((3, width // shards, inner), F32),
            ((inner // shards, width), F32),
            ((8, 256), F32),
        ],
        (place, flags, half, other, sums, grad_sum),
        scalars=2,
        micros=6,
    )


def late_shares(first_ref, middle_ref, last_ref):
    shares = []
    at = 0
    for ref in (middle_ref, first_ref):
        for index in range(ref.shape[0]):
            shares.append((at, at + ref.shape[1], store_rows(ref, (index,), slice(None)), None))
            at += ref.shape[1]
    for index in range(last_ref.shape[1] // 256):
        cols = slice(index * 256, index * 256 + 256)
        shares.append((at, at + last_ref.shape[0], store_rows(last_ref, (), cols), None))
        at += last_ref.shape[0]
    return shares


def late_kernel(rates, place, half, other, squares, extra, embed_own, back_own, *refs):
    given = [refs[3 * index : 3 * index + 3] for index in range(5)]
    first_ref, middle_ref, last_ref, norm_ref = refs[15:19]
    made = [refs[19 + 3 * index : 22 + 3 * index] for index in range(5)]
    tally = refs[34]
    emit(place, half, other, late_shares(first_ref, middle_ref, last_ref), tally)
    found = jnp.sum(tally[...] + squares[...], axis=0, keepdims=True)
    norm = jnp.sqrt(jnp.sum(found, axis=1, keepdims=True) + extra[0:1, 0:1])
    factor = jnp.minimum(1.0, CLIP_AT / (norm + 1e-06))
    norm_ref[0:1, :] = jnp.broadcast_to(norm, (1, 128))
    norm_ref[1:2, :] = jnp.broadcast_to(factor, (1, 128))

    def mine(span):
        return pl.ds(pl.multiple_of(place[1] * span, span), span)

    def own(index, part):
        if index == 0:
            return first_ref[part, mine(given[0][0].shape[1]), :]
        if index == 1:
            return middle_ref[part, mine(given[1][0].shape[1]), :]
        if index == 2:
            return last_ref[mine(given[2][0].shape[0]), :]
        return embed_own[part] if index == 3 else back_own[...]

    for index in range(5):
        master, moment, second = given[index]
        outs = made[index]
        for part in range(master.shape[0]) if len(master.shape) == 3 else (slice(None),):
            values = adam_step(
                master[part], own(index, part), moment[part], second[part], factor, rates[index]
            )
            for ref, value in zip(outs, values):
                ref[part] = value


def late_grads(rates, place, half, other, squares, extra, embed_own, back_own, states, shapes):
    flat = tuple(item for state in states for item in state)
    outs = [(shape, F32) for shape in shapes] + [((2, 128), F32)]
    outs += [(state[0].shape, F32) for state in states for _ in range(3)]
    found = call(
        functools.partial(late_kernel, rates),
        outs,
        (place, half, other, squares, extra, embed_own, back_own) + flat,
        scratch=[pltpu.VMEM((8, 256), F32)],
        micros=8,
    )
    return found[:3], found[3], [found[4 + 3 * index : 7 + 3 * index] for index in range(5)]


def unfold(value, height):
    return jnp.moveaxis(value.reshape(-1, height, 256), 0, 1).reshape(height, -1)


def plain_tail(early, late, mean, grad_sum, sizes, norm_square, states, rates, chan_at):
    width, inner, narrow = sizes
    core = chan_at & 1
    early, late = [
        jnp.where(core == 0, jnp.concatenate([half, other]), jnp.concatenate([other, half])).astype(
            F32
        )
        for half, other in (early, late)
    ]
    cut = 3 * inner * width // 256
    embed = unfold(early[:cut], width).reshape(width, 3, inner)
    back = unfold(early[cut:], inner) + mean[:, None] * grad_sum[None, :]
    middle = late[: 9 * narrow].reshape(9, narrow, narrow)
    first = late[9 * narrow : 9 * narrow + 3 * width].reshape(3, width, narrow)
    last = unfold(late[9 * narrow + 3 * width :], narrow)
    grads = (first, middle, last, jnp.moveaxis(embed, 1, 0), back)
    norm = jnp.sqrt(sum(jnp.sum(item * item) for item in grads) + norm_square)
    factor = jnp.minimum(1.0, CLIP_AT / (norm + 1e-06))
    made = []
    for grad, state, rate in zip(grads, states, rates):
        axis = grad.ndim - 2
        span = state[0].shape[axis]
        owned = lax.dynamic_slice_in_dim(grad, chan_at * span, span, axis)
        made.append(adam_step(state[0], owned, state[1], state[2], factor, rate))
    return grads, norm, factor, made


def input_kernel(cols, weights, pre_grad, out_ref):
    shards, _, span, narrow = weights.shape
    each = 256 // span
    for at in range(0, pre_grad.shape[1], 256):
        out = pre_grad[:, at : at + 256]
        begin = at // span
        for tap in range(3):
            rows = weights[pl.ds(begin, each), tap].reshape(256, narrow)
            out = out + dot(cols[:, tap * narrow : (tap + 1) * narrow], rows, NT)
        span_at = slice(at, at + 256)
        out_ref[:, span_at] = out.astype(LOW)


def input_grad(cols, weights, pre_grad):
    rows, width = pre_grad.shape
    return call(
        input_kernel,
        [((rows, width), LOW)],
        (cols, weights, pre_grad),
        scalars=0,
    )[0]


def adam_step(master, gradient, moment, second, factor, rate):
    clipped = gradient * factor
    moment_new = BETA_ONE * moment + (1.0 - BETA_ONE) * clipped
    second_new = BETA_TWO * second + (1.0 - BETA_TWO) * clipped * clipped
    moment_hat = moment_new / (1.0 - BETA_ONE**STEP)
    second_hat = second_new / (1.0 - BETA_TWO**STEP)
    master_new = master - rate * (
        moment_hat / (jnp.sqrt(second_hat) + ADAM_EPS) + WEIGHT_DECAY * master
    )
    return (moment_new, second_new, master_new)


def body(
    features,
    cotangent,
    frame_counts,
    weight_first,
    weight_middle,
    weight_last,
    weight_embed,
    weight_back,
    norm_params,
    moment_first,
    moment_middle,
    moment_last,
    moment_embed,
    moment_back,
    moment_norm,
    second_first,
    second_middle,
    second_last,
    second_embed,
    second_back,
    second_norm,
):
    chan_at = lax.axis_index("chan")
    device = lax.axis_index("clip") * lax.axis_size("chan") + chan_at
    frames, spot_count, model_width = features.shape
    row_count = frames * spot_count
    narrow = BOT
    inner_width = INNER
    clip_place = chan_at % DPC
    clip_at = device // DPC
    clip_ids = jnp.arange(frame_counts.shape[0], dtype=jnp.int32)
    length = jnp.sum(jnp.where(clip_ids == clip_at, frame_counts, 0))

    def valid_at(place):
        return ((place >= 0) & (place < DPC) & (place * frames < length)).astype(jnp.float32)

    place = jnp.stack([chan_at & 1, chan_at, lax.axis_index("clip")]).astype(jnp.int32)
    own_ok = valid_at(clip_place)
    row_total = jnp.sum(frame_counts).astype(jnp.float32) * spot_count
    zero = jnp.zeros((), jnp.float32)
    flags = jnp.stack(
        [own_ok, valid_at(clip_place - 1), valid_at(clip_place + 1), 1.0 / row_total]
        + [valid_at(clip_place ^ 2)] + [zero] * 3
    )
    held = sum(valid_at(clip_place ^ turn) for turn in range(4)) * own_ok
    blocks_own = held.astype(jnp.int32).reshape(1)
    blocks_far = (held * valid_at(clip_place ^ 4)).astype(jnp.int32).reshape(1)
    span_list = [narrow] * 4 + [model_width] * 4
    starts = [sum(span_list[:index]) for index in range(8)]
    gains_one, gains_two, gains_three, gains_four = [
        norm_params[starts[index] : starts[index] + 2 * span_list[index]].reshape(2, -1)
        for index in range(0, 8, 2)
    ]
    shards = lax.axis_size("chan")
    tall = weight_middle.shape[0] * weight_middle.shape[1]
    packed = jnp.concatenate(
        [
            weight_middle.reshape(tall, narrow),
            jnp.moveaxis(weight_last.reshape(-1, model_width // 256, 256), 1, 0).reshape(-1, 256),
        ]
    ).astype(LOW)
    packed = lax.all_gather(packed, "chan", axis=0, tiled=False)
    middle_low = packed[:, :tall].reshape((shards,) + weight_middle.shape)
    last_low = jnp.moveaxis(
        packed[:, tall:].reshape(shards, model_width // 256, -1, 256), 1, 2
    ).reshape(narrow, model_width)
    if weight_middle.shape[1] % 16:
        middle_low = jnp.moveaxis(middle_low, 0, 1).reshape(1, 9, narrow, narrow)
    embed_low, back_low = (
        lax.all_gather(weight_embed.astype(LOW).reshape(-1, 3 * inner_width), "chan", axis=0, tiled=True),
        lax.all_gather(weight_back.astype(LOW), "chan", axis=0, tiled=True),
    )
    spots = np.arange(row_count)
    across, down = spots % WW, spots // WW % HH
    edges = jnp.asarray(
        np.stack([across > 0, across < WW - 1, down > 0, down < HH - 1] + [across < 0] * 4, axis=1)
        .astype(np.float32)
    )
    cells = features.reshape(row_count, model_width)
    cot = cotangent.reshape(row_count, model_width)
    before, after = beside(features, spot_count)
    if shards == 8 and lax.axis_size("clip") == 4:
        pre_one, sums_one, first_low = first_conv_parts(
            place, flags, cells, before, after, *quarters_of(weight_first)
        )
    else:
        first_low = whole_of(weight_first)
        pre_one, sums_one = first_conv(flags, cells, before, after, first_low)
    sums_one = total(sums_one)
    pre_two, sums_two = middle_conv(
        flags, pre_one, sums_one, gains_one, middle_low, edges
    )
    sums_two = total(sums_two)
    act_two, sums_three = last_conv(flags, pre_two, sums_two, gains_two, last_low)
    sums_three, cot = tied(total(sums_three), cot)
    residual_low, query, pair_own = embed_rows(
        flags, act_two, cells, last_low, sums_three, gains_three, embed_low
    )
    pair_core = flipped(pair_own, "chan", 1)
    query_far, pair_far = flipped(query, "chan", 4), flipped(pair_own, "chan", 2)
    query_far, pair_far, back_low = tied(query_far, pair_far, back_low)
    blocks = (pair_own, pair_core, pair_far, flipped(pair_far, "chan", 1))
    part_far, log_far = attend(blocks_far, query_far, blocks, True)
    part_far = flipped(part_far, "chan", 4)
    log_far = flipped(log_far, "chan", 4)
    part_own, log_own = attend(blocks_own, query, blocks, False)
    attended, logs, sums_four = merge(flags, part_own, log_own, part_far, log_far, back_low, cot)
    sums_four = total(sums_four)
    mixed, attn_grad, attended_grad, terms, packed, norm_four = outer(
        flags, attended, back_low, sums_four, gains_four, cot, residual_low, logs
    )
    mixed = laid_out(mixed, frames)
    attended_grad_far = flipped(attended_grad, "chan", 4)
    packed_far = flipped(packed, "chan", 4)
    query_own, held = attend_back(
        blocks_own, query, attended_grad, (logs, terms), blocks, (0, 1, 2, 3), None, None, F32
    )
    query_part, (far, far_core) = attend_back(
        blocks_far, query_far, attended_grad_far, (packed_far,), blocks[2:], (2, 3), held[2:], None, F32
    )
    far = (far.astype(F32) + flipped(far_core, "chan", 1).astype(F32)).astype(LOW)
    far, near_own = tied(far, held[0])
    far = flipped(far, "chan", 2)
    query_part, (keep, give_keys, give_values) = attend_back(
        blocks_far, query_far, attended_grad_far, (packed_far,), blocks[:2], (0, 1), (near_own, held[1]),
        query_part, LOW, (1,),
    )
    query_part = flipped(query_part, "chan", 4)
    near_keys, near_values = flipped(give_keys, "chan", 1), flipped(give_values, "chan", 1)
    projected_grad, pre_grad, back_three = project_back(
        flags, query_own, query_part, keep, near_keys, near_values, far, act_two, cells, last_low, sums_three,
        gains_three, embed_low, cot,
    )
    early = early_weight(
        place, flags, residual_low, projected_grad, attended, sums_four[4:5, :inner_width], attn_grad
    )
    back_three = total(jnp.concatenate([back_three, norm_four[2:3]]))
    early, back_three = tied(early, back_three)
    last_grad, two_grad, back_two = last_back(
        flags, pre_grad, act_two, last_low, sums_three, gains_three, back_three, pre_two, sums_two,
        gains_two,
    )
    back_two = total(back_two)
    last_local = weight_grad(act_two, last_grad)
    middle_grad, one_grad, back_one = middle_back(
        flags, two_grad, back_two, pre_two, sums_two, gains_two, pre_one, sums_one, gains_one,
        middle_low, edges,
    )
    back_one = total(back_one)
    middle_local = middle_weight(flags, pre_one, sums_one, gains_one, middle_grad, edges)
    first_grad = first_grad_of(flags, one_grad, back_one, pre_one, sums_one, gains_one)
    before, after = beside(first_grad.reshape(frames, spot_count, narrow), spot_count)
    late, grad_cols = first_back(place, flags, first_grad, before, after, cells, middle_local, last_local)
    features_gradient = laid_out(input_grad(grad_cols, first_low, pre_grad), frames)
    gain_one_grad, shift_one_grad = back_one[1], back_one[0]
    gain_two_grad, shift_two_grad = back_two[1], back_two[0]
    gain_three_grad, shift_three_grad = back_three[1], back_three[0]
    gain_four_grad, shift_four_grad = norm_four[0], norm_four[1]
    norm_gradient = jnp.concatenate(
        [
            gain_one_grad,
            shift_one_grad,
            gain_two_grad,
            shift_two_grad,
            gain_three_grad,
            shift_three_grad,
            gain_four_grad,
            shift_four_grad,
        ]
    )
    groups = [list(range(core, shards, 2)) for core in range(2)]
    early = lax.psum_scatter(core_step(*early), "clip", scatter_dimension=0, tiled=True)
    early = lax.psum(early, "chan", axis_index_groups=groups)
    steps = level_steps()[1:]
    late = scatter_sum(core_step(*late), steps)
    early, late = tied(early, late)
    early = lax.all_gather(early, "clip", axis=0, tiled=True)
    late = gather_sum(late, steps)
    early, late, mixed, features_gradient = tied(early, late, mixed, features_gradient)
    early = (early, flipped(early, "chan", 1))
    late = (late, flipped(late, "chan", 1))
    fans = (3 * D, 9 * BOT, BOT, D, INNER)
    rates = tuple(0.5 * fan ** (-0.5) for fan in fans)
    states = (
        (weight_first, moment_first, second_first),
        (weight_middle, moment_middle, second_middle),
        (weight_last, moment_last, second_last),
        tuple(jnp.moveaxis(item, 1, 0) for item in (weight_embed, moment_embed, second_embed)),
        (weight_back, moment_back, second_back),
    )
    norm_square = jnp.sum(norm_gradient * norm_gradient)
    if weight_middle.shape[1] % 16 == 0:
        embed, back, embed_own, back_own, squares = early_grads(
            place,
            flags,
            *early,
            sums_four[4:5, :inner_width],
            back_three[2:3],
            model_width,
            inner_width,
            shards,
        )
        shapes = ((3, model_width, narrow), (9, narrow, narrow), (narrow, model_width))
        (first, middle, last), norm_row, results = late_grads(
            rates, place, *late, squares, norm_square.reshape(1, 1), embed_own, back_own, states, shapes
        )
        gradient_norm, factor = norm_row[0, 0], norm_row[1, 0]
    else:
        (first, middle, last, embed, back), gradient_norm, factor, results = plain_tail(
            early,
            late,
            sums_four[4, :inner_width] * flags[3],
            back_three[2],
            (model_width, inner_width, narrow), norm_square, states, rates, chan_at
        )
    results = list(results)
    results[3] = tuple(jnp.moveaxis(item, 0, 1) for item in results[3])
    results.append(adam_step(norm_params, norm_gradient, moment_norm, second_norm, factor, GAIN_RATE))
    return (
        mixed,
        features_gradient,
        first,
        middle,
        last,
        jnp.moveaxis(embed, 0, 1),
        back,
        norm_gradient,
    ) + tuple(results[index][kind] for kind in range(3) for index in range(6)) + (gradient_norm,)


def solution(mesh):
    placed = (
        P(("clip", "chan"), None, None),
        P(("clip", "chan"), None, None),
        P(),
        P(None, "chan", None),
        P(None, "chan", None),
        P("chan", None),
        P("chan", None, None),
        P("chan", None),
        P(),
        P(None, "chan", None),
        P(None, "chan", None),
        P("chan", None),
        P("chan", None, None),
        P("chan", None),
        P(),
        P(None, "chan", None),
        P(None, "chan", None),
        P("chan", None),
        P("chan", None, None),
        P("chan", None),
        P(),
    )
    return jax.shard_map(
        body,
        mesh=mesh,
        in_specs=placed,
        out_specs=(
            P(("clip", "chan"), None, None),
            P(("clip", "chan"), None, None),
            P(),
            P(),
            P(),
            P(),
            P(),
            P(),
            P(None, "chan", None),
            P(None, "chan", None),
            P("chan", None),
            P("chan", None, None),
            P("chan", None),
            P(),
            P(None, "chan", None),
            P(None, "chan", None),
            P("chan", None),
            P("chan", None, None),
            P("chan", None),
            P(),
            P(None, "chan", None),
            P(None, "chan", None),
            P("chan", None),
            P("chan", None, None),
            P("chan", None),
            P(),
            P(),
        ),
        check_vma=False,
    )
```

```python
import functools
import math

import jax
import jax.numpy as jnp
import numpy as np
from jax import lax
from jax.experimental import pallas as pl
from jax.experimental.layout import Layout, with_layout_constraint
from jax.experimental.pallas import tpu as pltpu
from jax.sharding import PartitionSpec as P

D = 1024
BOT = 256
INNER = 512
HH = 14
WW = 14
STEP = 10
DPC = 8


EPS_NORM = 1e-05
BETA_ONE = 0.9
BETA_TWO = 0.95
ADAM_EPS = 1e-08
WEIGHT_DECAY = 0.01
CLIP_AT = 1.0
GAIN_RATE = 0.5


def flipped(value, axis, mask):
    pairs = [(source, source ^ mask) for source in range(lax.axis_size(axis))]
    return lax.ppermute(value, axis, pairs)


def whole_of(shard):
    return lax.all_gather(shard.astype(jnp.bfloat16), "chan", axis=0, tiled=False)


def quarters_of(shard):
    span = shard.shape[1] // 4
    piece = lax.dynamic_slice_in_dim(
        shard.astype(jnp.bfloat16), lax.axis_index("clip") * span, span, axis=1
    )[None]
    chips = jnp.concatenate(
        [piece] + [flipped(piece, "chan", 2 * turn) for turn in range(1, 4)]
    )[None]
    mine = jnp.concatenate([chips] + [flipped(chips, "clip", turn) for turn in range(1, 4)])
    return mine, flipped(mine, "chan", 1)


def tap_of(weights, tap):
    return weights[:, tap].reshape(weights.shape[0] * weights.shape[2], weights.shape[3])


def beside(cells, spots):
    ends = lax.axis_size("chan") - 1
    upward = [(index, index + 1) for index in range(ends)]
    downward = [(index + 1, index) for index in range(ends)]
    return (
        lax.ppermute(cells[-1:], "chan", upward).reshape(spots, cells.shape[-1]),
        lax.ppermute(cells[:1], "chan", downward).reshape(spots, cells.shape[-1]),
    )


def total(value, beside=()):
    steps = [("chan", group) for group in level_groups("chan")]
    steps += [("clip", group) for group in level_groups("clip")]
    for index, (axis, group) in enumerate(steps):
        base = 1 << group[0]
        parts = [flipped(value, axis, base * turn) for turn in range(1, 1 << len(group))]
        if beside and index == len(steps) - 1:
            tie = lax.optimization_barrier((parts, list(beside)))
            parts, beside = tie
        value = value + sum(parts[1:], parts[0])
    return (value, *beside) if beside else value


def level_groups(axis):
    bits = lax.axis_size(axis).bit_length() - 1
    levels = list(range(bits))
    groups = [levels[:1]] if axis == "chan" else []
    rest = levels[len(groups) :]
    return groups + [rest[index : index + 2] for index in range(0, len(rest), 2)]


def level_steps():
    order = [("chan", group) for group in level_groups("chan")]
    order = order[:1] + [("clip", group) for group in level_groups("clip")] + order[1:]
    steps = []
    for axis, group in order:
        base, count = 1 << group[0], 1 << len(group)
        steps.append((axis, base, count, (lax.axis_index(axis) >> group[0]) & (count - 1)))
    return steps


def half_kernel(mine, arrived, out_ref):
    out_ref[...] = (mine[...].astype(F32) + arrived[...].astype(F32)).astype(LOW)


def core_step(mine, others):
    arrived = flipped(others, "chan", 1)
    return call(half_kernel, [(mine.shape, LOW)], (mine, arrived), scalars=0)[0]


def deal(place, halves, mine, others, sems):
    copies = [
        pltpu.make_async_copy(halves.at[place[0]], mine, sems.at[0]),
        pltpu.make_async_copy(halves.at[1 - place[0]], others, sems.at[1]),
    ]
    for copy in copies:
        copy.start()
    for copy in copies:
        copy.wait()


def put_rows(halves, at, values):
    size = halves.shape[1]
    cut = max(0, min(values.shape[0], size - at))
    if cut:
        halves[0, pl.ds(at, cut), :] = values[:cut]
    if cut < values.shape[0]:
        halves[1, pl.ds(at + cut - size, values.shape[0] - cut), :] = values[cut:]


def scatter_sum(value, steps):
    for axis, base, count, place in steps:
        size = value.shape[0] // count
        mine = lax.dynamic_slice_in_dim(value, place * size, size).astype(F32)
        arrived = [
            flipped(
                lax.dynamic_slice_in_dim(value, (place ^ turn) * size, size), axis, base * turn
            )
            for turn in range(1, count)
        ]
        for item in arrived:
            mine = mine + item.astype(F32)
        value = mine.astype(LOW)
    return value


def laid_out(rows, frames):
    grid = rows.reshape(frames, -1, rows.shape[1])
    return with_layout_constraint(grid, Layout(major_to_minor=(1, 0, 2)))


def tied(*values):
    return lax.optimization_barrier(values)


def gather_sum(value, steps):
    for axis, base, count, place in reversed(steps):
        size = value.shape[0]
        parts = [value] + [flipped(value, axis, base * turn) for turn in range(1, count)]
        whole = jnp.zeros((count,) + value.shape, LOW)
        for turn, part in enumerate(parts):
            whole = lax.dynamic_update_index_in_dim(whole, part, place ^ turn, 0)
        value = whole.reshape((count * size,) + value.shape[1:])
    return value


NEG = -1e30
MIB = 1 << 20
NN = (((1,), (0,)), ((), ()))
NT = (((1,), (1,)), ((), ()))
TN = (((0,), (0,)), ((), ()))
F32 = jnp.float32
LOW = jnp.bfloat16


def dot(left, right, dims=NN):
    return lax.dot_general(left, right, dims, preferred_element_type=F32)


def sig(values):
    return 0.5 * jnp.tanh(0.5 * values) + 0.5


def slope(values):
    gate = sig(values)
    return gate * (1.0 + values * (1.0 - gate))


def moments(sums, inverse):
    mean = sums[0:1] * inverse
    return mean, lax.rsqrt(sums[1:2] * inverse - mean * mean + EPS_NORM)


def column_sums(values):
    return jnp.sum(values, axis=0, keepdims=True)


def call(kernel, outs, args, scalars=1, scratch=(), vmem=16, far=(), far_out=(), micros=2):
    spaces = []
    for index in range(len(args)):
        if index < scalars:
            spaces.append(pl.BlockSpec(memory_space=pltpu.SMEM))
        elif index in far:
            spaces.append(pl.BlockSpec(memory_space=pltpu.HBM))
        else:
            spaces.append(pl.BlockSpec(memory_space=pltpu.VMEM))
    shapes = tuple(jax.ShapeDtypeStruct(shape, dtype) for shape, dtype in outs)
    out_specs = tuple(
        pl.BlockSpec(memory_space=pltpu.HBM if index in far_out else pltpu.VMEM)
        for index in range(len(outs))
    )
    return pl.pallas_call(
        kernel,
        out_shape=shapes,
        in_specs=spaces,
        out_specs=out_specs,
        scratch_shapes=list(scratch),
        compiler_params=pltpu.CompilerParams(vmem_limit_bytes=vmem * MIB),
        cost_estimate=pl.CostEstimate(
            flops=int(micros * 1e9), bytes_accessed=0, transcendentals=0
        ),
    )(*args)


def first_tail(flags, cells, before, after, weights, pre_ref, sums_ref, early, late):
    rows = cells.shape[0]
    spots = before.shape[0]
    valid = flags[0]
    late[pl.ds(0, rows), :] = dot(cells[...], tap_of(weights, 2)) * valid
    late[pl.ds(rows, spots), :] = dot(after[...], tap_of(weights, 2)) * flags[2]
    early[pl.ds(0, spots), :] = dot(before[...], tap_of(weights, 0)) * flags[1]
    early[pl.ds(spots, rows), :] = dot(cells[...], tap_of(weights, 0)) * valid
    pre = (
        dot(cells[...], tap_of(weights, 1)) * valid
        + early[pl.ds(0, rows), :]
        + late[pl.ds(spots, rows), :]
    )
    pre_ref[...] = pre
    sums_ref[0:1, :] = column_sums(pre) * valid
    sums_ref[1:2, :] = column_sums(pre * pre) * valid


def first_parts_kernel(place, flags, cells, before, after, mine, others, pre_ref, sums_ref, weights, early, late):
    for index in range(mine.shape[0]):
        span = mine.shape[3]
        rows = pl.ds(pl.multiple_of((place[2] ^ index) * span, span), span)
        for turn in range(mine.shape[1]):
            weights[place[1] ^ (2 * turn), :, rows, :] = mine[index, turn]
            weights[place[1] ^ (2 * turn + 1), :, rows, :] = others[index, turn]
    first_tail(flags, cells, before, after, weights, pre_ref, sums_ref, early, late)


def first_conv_parts(place, flags, cells, before, after, mine, others):
    rows = cells.shape[0]
    clips, chips, taps, span, narrow = mine.shape
    spots = before.shape[0]
    return call(
        first_parts_kernel,
        [
            ((rows, narrow), F32),
            ((2, narrow), F32),
            ((2 * chips, taps, clips * span, narrow), LOW),
        ],
        (place, flags, cells, before, after, mine, others),
        scalars=2,
        scratch=[pltpu.VMEM((rows + spots, narrow), F32)] * 2,
    )


def first_conv(flags, cells, before, after, weights):
    rows, width = cells.shape
    narrow = weights.shape[3]
    spots = before.shape[0]
    return call(
        first_tail,
        [((rows, narrow), F32), ((2, narrow), F32)],
        (flags, cells, before, after, weights),
        scratch=[pltpu.VMEM((rows + spots, narrow), F32)] * 2,
    )


def spread(values, edges, buffer, columns, rows):
    narrow = values.shape[1]
    margin = 16
    buffer[0, pl.ds(0, margin), :] = jnp.zeros((margin, narrow), F32)
    buffer[0, pl.ds(margin + rows, margin), :] = jnp.zeros((margin, narrow), F32)
    buffer[1, pl.ds(0, margin), :] = jnp.zeros((margin, narrow), F32)
    buffer[1, pl.ds(margin + rows, margin), :] = jnp.zeros((margin, narrow), F32)
    buffer[0, pl.ds(margin, rows), :] = values
    for across in range(3):
        moved = buffer[0, pl.ds(margin + across - 1, rows), :]
        if across == 0:
            moved = moved * edges[:, 0:1]
        if across == 2:
            moved = moved * edges[:, 1:2]
        buffer[1, pl.ds(margin, rows), :] = moved
        for down in range(3):
            part = buffer[1, pl.ds(margin + WW * (down - 1), rows), :]
            if down == 0:
                part = part * edges[:, 2:3]
            if down == 2:
                part = part * edges[:, 3:4]
            at = (3 * down + across) * narrow
            columns[:, at : at + narrow] = part.astype(LOW)


def spread_scratch(rows, narrow):
    return [pltpu.VMEM((2, rows + 32, narrow), F32), pltpu.VMEM((rows, 9 * narrow), LOW)]


def act_of(flags, pre, sums, scale_shift):
    mean, scale = moments(sums, flags[3])
    normal = (pre - mean) * scale
    return normal, normal * scale_shift[0:1] + scale_shift[1:2], scale


def middle_kernel(flags, pre, sums, gains, weights, edges, out_ref, sums_ref, buffer, columns):
    rows, narrow = pre.shape
    valid = flags[0]
    _, act, _ = act_of(flags, pre[...], sums[...], gains[...])
    spread(act * sig(act) * valid, edges[...], buffer, columns, rows)
    out = None
    for tap in range(9):
        part = dot(columns[:, tap * narrow : (tap + 1) * narrow], tap_of(weights, tap))
        out = part if out is None else out + part
    out_ref[...] = out
    sums_ref[0:1, :] = column_sums(out) * valid
    sums_ref[1:2, :] = column_sums(out * out) * valid


def middle_conv(flags, pre, sums, gains, weights, edges):
    rows, narrow = pre.shape
    return call(
        middle_kernel,
        [((rows, narrow), F32), ((2, narrow), F32)],
        (flags, pre, sums, gains, weights, edges),
        scratch=spread_scratch(rows, narrow),
    )


def last_kernel(flags, pre, sums, gains, weights, act_ref, sums_ref):
    valid = flags[0]
    _, act, _ = act_of(flags, pre[...], sums[...], gains[...])
    act_ref[...] = (act * sig(act) * valid).astype(LOW)
    for at in range(0, weights.shape[1], 256):
        out = dot(act_ref[...], weights[:, at : at + 256])
        sums_ref[0:1, at : at + 256] = column_sums(out) * valid
        sums_ref[1:2, at : at + 256] = column_sums(out * out) * valid


def last_conv(flags, pre, sums, gains, weights):
    rows, narrow = pre.shape
    width = weights.shape[1]
    return call(
        last_kernel,
        [((rows, narrow), LOW), ((2, width), F32)],
        (flags, pre, sums, gains, weights),
    )


def residual_tile(flags, act, cells, weights, sums, gains, at):
    mean, scale = moments(sums[:, at : at + 256], flags[3])
    normal = (dot(act[...], weights[:, at : at + 256]) - mean) * scale
    pre = cells[:, at : at + 256].astype(F32) + (
        normal * gains[0:1, at : at + 256] + gains[1:2, at : at + 256]
    )
    return normal, pre, scale


def embed_kernel(flags, act, cells, weights, sums, gains, embed, res_ref, query_ref, pair_ref):
    width = weights.shape[1]
    inner = query_ref.shape[1]
    for at in range(0, width, 256):
        _, pre, _ = residual_tile(flags, act, cells, weights, sums, gains, at)
        res_ref[:, at : at + 256] = (pre * sig(pre) * flags[0]).astype(LOW)
    for at in range(0, inner, 256):
        query_ref[:, at : at + 256] = dot(res_ref[...], embed[:, at : at + 256]).astype(LOW)
    for at in range(0, 2 * inner, 256):
        pair_ref[:, at : at + 256] = dot(
            res_ref[...], embed[:, inner + at : inner + at + 256]
        ).astype(LOW)


def embed_rows(flags, act, cells, weights, sums, gains, embed):
    rows, width = cells.shape
    inner = embed.shape[1] // 3
    return call(
        embed_kernel,
        [((rows, width), LOW), ((rows, inner), LOW), ((rows, 2 * inner), LOW)],
        (flags, act, cells, weights, sums, gains, embed),
        micros=7,
    )


def copies_of(refs, slots, sems):
    return [
        pltpu.make_async_copy(ref, slots.at[index], sems.at[index])
        for index, ref in enumerate(refs)
    ]


def attend_kernel(
    away, count, query, one, two, three, four, out_ref, log_ref, pairs, tails, scores, total, peak, sums, sems
):
    rows, inner = query.shape
    full = rows // 256 * 256
    rest = rows - full
    wide = 4 * rest
    turn = inner**-0.5 * math.log2(math.e)
    blocks = count[0]
    copies = copies_of((one, two, three, four), pairs, sems)
    for copy in copies:
        copy.start()

    @pl.when(blocks == 0)
    def _():
        out_ref[...] = jnp.zeros_like(out_ref)
        if away:
            log_ref[...] = jnp.zeros_like(log_ref)
            log_ref[0:1, :] = jnp.full((1, log_ref.shape[1]), NEG, F32)
        else:
            log_ref[...] = jnp.full_like(log_ref, NEG)

    peak[...] = jnp.full_like(peak, NEG)
    sums[...] = jnp.zeros_like(sums)

    def score(index, _):
        pltpu.make_async_copy(one, pairs.at[index], sems.at[index]).wait()

        @pl.when(index < blocks)
        def _():
            found = dot(query[...], pairs[index, pl.ds(0, full), :inner], NT)
            scores[index] = found
            top = peak[...]
            for at in range(0, full, 128):
                top = jnp.maximum(top, found[:, at : at + 128])
            peak[...] = top

        return 0

    lax.fori_loop(0, 4, score, 0)

    @pl.when(blocks > 0)
    def _():
        for index in range(4):
            tails[pl.ds(index * rest, rest), :] = pairs[index, pl.ds(full, rest), :]
        lane = lax.broadcasted_iota(jnp.int32, (rows, wide), 1)
        end = jnp.where(lane < blocks * rest, dot(query[...], tails[:, :inner], NT), NEG)
        top = jnp.maximum(
            jnp.max(peak[...], axis=1, keepdims=True), jnp.max(end, axis=1, keepdims=True)
        )
        top = top * turn
        lifted = jnp.exp2(end * turn - top)
        end_sum = jnp.sum(lifted, axis=1, keepdims=True)
        total[...] = dot(lifted.astype(LOW), tails[:, inner:])
        peak[...] = jnp.broadcast_to(top, peak.shape)

        def weigh(index, _):
            base = peak[...]
            running = sums[...]
            parts = []
            for at in range(0, full, 128):
                part = jnp.exp2(scores[index, :, at : at + 128] * turn - base)
                running = running + part
                parts.append(part.astype(LOW))
            sums[...] = running
            total[...] += dot(
                jnp.concatenate(parts, axis=1), pairs[index, pl.ds(0, full), inner:]
            )
            return 0

        lax.fori_loop(0, blocks, weigh, 0)
        found = jnp.sum(sums[...], axis=1, keepdims=True) + end_sum
        logs = jnp.broadcast_to(top + jnp.log2(found), peak.shape)
        if away:
            out = total[...] / found
            mean = column_sums(out) * (1.0 / rows)
            out_ref[...] = (out - mean).astype(out_ref.dtype)
            log_ref[...] = row_of(logs, log_ref.shape[1])
            log_ref[1:2, :inner] = mean
        else:
            out_ref[...] = (total[...] / found).astype(out_ref.dtype)
            log_ref[...] = logs


def attend(count, query, blocks, away):
    rows, inner = query.shape
    span = -(-rows // 128) * 128
    full = rows // 256 * 256
    rest = rows - full
    return call(
        functools.partial(attend_kernel, away),
        [((rows, inner), LOW), ((8, span) if away else (rows, 128), F32)],
        (count, query) + tuple(blocks),
        scratch=[
            pltpu.VMEM((4, rows, 2 * inner), LOW),
            pltpu.VMEM((4 * rest, 2 * inner), LOW),
            pltpu.VMEM((4, rows, full), F32),
            pltpu.VMEM((rows, inner), F32),
            pltpu.VMEM((rows, 128), F32),
            pltpu.VMEM((rows, 128), F32),
            pltpu.SemaphoreType.DMA((4,)),
        ],
        vmem=36,
        far=(2, 3, 4, 5),
        micros=10,
    )


def attend_back_kernel(away, held, split, count, query, grad, *refs):
    size = len(held)
    refs = list(refs)
    if away:
        packed = refs.pop(0)
    else:
        log_ref, term_ref = refs.pop(0), refs.pop(0)
    given_query = refs.pop(0) if away and held[0] == 0 else None
    blocks_in = [refs.pop(0) for _ in held]
    given = [refs.pop(0) for _ in held] if away else ()
    query_ref = refs.pop(0)
    outs = [[refs.pop(0) for _ in range(2 if place in split else 1)] for place in held]
    pairs, tails, stage, stage_tails, total, sems, out_sems = refs[:7]
    if away:
        log_ref, term_ref, in_sems = refs[7:]
    rows, inner = query.shape
    full = rows // 256 * 256
    rest = rows - full
    wide = size * rest
    scaling = inner**-0.5
    turn = scaling * math.log2(math.e)
    blocks = count[0]

    def main_of(ref):
        return ref.at[pl.ds(0, full)]

    def tail_of(ref):
        return ref.at[pl.ds(full, rest)]

    def tail_at(index):
        return pl.ds(index * rest, rest)

    begin = [
        pltpu.make_async_copy(tail_of(ref), tails.at[tail_at(index)], sems.at[1, index])
        for index, ref in enumerate(blocks_in)
    ] + [
        pltpu.make_async_copy(tail_of(ref), stage_tails.at[tail_at(index)], in_sems.at[1, index])
        for index, ref in enumerate(given)
    ]
    for copy in begin:
        copy.start()
    for index in range(size):
        pltpu.make_async_copy(main_of(blocks_in[index]), pairs.at[index], sems.at[0, index]).start()
        if away:
            pltpu.make_async_copy(main_of(given[index]), stage.at[index], in_sems.at[0, index]).start()
    if away:
        log_ref[...] = column_of(packed[0:1, :])[:rows]
        term_ref[...] = column_of(packed[1:2, :])[:rows]
    for copy in begin:
        copy.wait()

    def tile(keys, values, span, mask):
        found = dot(query[...], keys, NT)
        back = dot(grad[...], values, NT)
        logs = log_ref[...]
        terms = term_ref[...]
        kept = []
        slopes = []
        for at in range(0, span, 128):
            end = min(at + 128, span)
            weight = jnp.exp2(found[:, at:end] * turn - logs[:, : end - at])
            if mask is not None:
                weight = jnp.where(mask, weight, 0.0)
            kept.append(weight.astype(LOW))
            slopes.append((weight * (back[:, at:end] - terms[:, : end - at])).astype(LOW))
        kept = kept[0] if len(kept) == 1 else jnp.concatenate(kept, axis=1)
        slopes = slopes[0] if len(slopes) == 1 else jnp.concatenate(slopes, axis=1)
        return slopes, dot(slopes, query[...], TN) * scaling, dot(kept, grad[...], TN)

    active = blocks > held[0]

    @pl.when(jnp.logical_not(active))
    def _():
        if given_query is None:
            query_ref[...] = jnp.zeros_like(query_ref)
        else:
            query_ref[...] = given_query[...].astype(query_ref.dtype)
        if not away:
            stage_tails[...] = jnp.zeros_like(stage_tails)

    @pl.when(active)
    def _():
        keys = tails[:, :inner]
        lane = lax.broadcasted_iota(jnp.int32, (rows, wide), 1)
        ok = lane < (blocks - held[0]) * rest
        slopes, key_part, value_part = tile(keys, tails[:, inner:], wide, ok)
        total[...] = dot(slopes, keys)
        if away:
            key_part = key_part + stage_tails[:, :inner].astype(F32)
            value_part = value_part + stage_tails[:, inner:].astype(F32)
        stage_tails[:, :inner] = key_part.astype(LOW)
        stage_tails[:, inner:] = value_part.astype(LOW)

    def columns(which, part):
        width = 2 * inner // len(outs[which])
        return pl.ds(part * width, width)

    def main_outs(which):
        return [
            pltpu.make_async_copy(
                stage.at[which, :, columns(which, part)], main_of(ref), out_sems.at[0, which, part]
            )
            for part, ref in enumerate(outs[which])
        ]

    def one_block(index, _):
        pltpu.make_async_copy(main_of(blocks_in[0]), pairs.at[index], sems.at[0, index]).wait()
        if away:
            pltpu.make_async_copy(main_of(given[0]), stage.at[index], in_sems.at[0, index]).wait()

        @pl.when(index < blocks - held[0])
        def _():
            block = pairs[index, :, :inner]
            slopes, key_part, value_part = tile(block, pairs[index, :, inner:], full, None)
            total[...] += dot(slopes, block)
            if away:
                key_part = key_part + stage[index, :, :inner].astype(F32)
                value_part = value_part + stage[index, :, inner:].astype(F32)
            stage[index, :, :inner] = key_part.astype(LOW)
            stage[index, :, inner:] = value_part.astype(LOW)

        if not away:

            @pl.when(index >= blocks - held[0])
            def _():
                stage[index] = jnp.zeros(stage.shape[1:], LOW)

        for which in range(size):

            @pl.when(index == which)
            def _():
                for copy in main_outs(which):
                    copy.start()

        return 0

    lax.fori_loop(0, size, one_block, 0)
    ends = [
        pltpu.make_async_copy(
            stage_tails.at[tail_at(index), columns(index, part)],
            tail_of(ref),
            out_sems.at[1, index, part],
        )
        for index in range(size)
        for part, ref in enumerate(outs[index])
    ]
    for copy in ends:
        copy.start()

    @pl.when(active)
    def _():
        found = total[...] * scaling
        if given_query is not None:
            found = found + given_query[...]
        query_ref[...] = found.astype(query_ref.dtype)

    for index in range(size):
        for copy in main_outs(index):
            copy.wait()
    for copy in ends:
        copy.wait()


def attend_back(
    count, query, grad, terms, blocks, held, given, given_query, out_type, split=()
):
    rows, inner = query.shape
    full = rows // 256 * 256
    rest = rows - full
    away = given is not None
    size = len(held)
    more = () if given_query is None else (given_query,)
    near = (count, query, grad) + tuple(terms) + more
    distant = tuple(blocks) + (tuple(given) if away else ())
    scratch = [
        pltpu.VMEM((size, full, 2 * inner), LOW),
        pltpu.VMEM((size * rest, 2 * inner), LOW),
        pltpu.VMEM((size, full, 2 * inner), LOW),
        pltpu.VMEM((size * rest, 2 * inner), LOW),
        pltpu.VMEM((rows, inner), F32),
        pltpu.SemaphoreType.DMA((2, size)),
        pltpu.SemaphoreType.DMA((2, size, 2)),
    ]
    widths = []
    for at in held:
        widths += [inner] * 2 if at in split else [2 * inner]
    if away:
        scratch += [pltpu.VMEM((rows, 128), F32)] * 2 + [pltpu.SemaphoreType.DMA((2, size))]
    found = call(
        functools.partial(attend_back_kernel, away, held, split),
        [((rows, inner), out_type)] + [((rows, width), LOW) for width in widths],
        near + distant,
        scratch=scratch,
        vmem=36,
        far=tuple(range(len(near), len(near) + len(distant))),
        far_out=tuple(range(1, 1 + len(widths))),
        micros=17,
    )
    return found[0], found[1:]


def column_of(row):
    return jnp.transpose(jnp.broadcast_to(row, (128, row.shape[1])))


def row_of(column, span):
    tall = jnp.concatenate([column, jnp.zeros((span - column.shape[0], 128), F32)], axis=0)
    return jnp.transpose(tall)[0:8, :]


def merge_kernel(
    flags, own, own_log, far, far_log, weights, cot, out_ref, log_ref, sums_ref
):
    rows, inner = own.shape
    logs = own_log[...]
    others = column_of(far_log[0:1, :])[:rows]
    top = jnp.maximum(logs, others)
    whole = top + jnp.log2(jnp.exp2(logs - top) + jnp.exp2(others - top))
    log_ref[...] = whole
    share = jnp.exp2(logs - whole)
    other = jnp.exp2(others - whole)
    for at in range(0, inner, 128):
        out_ref[:, at : at + 128] = (
            own[:, at : at + 128].astype(F32) * share + (far[:, at : at + 128].astype(F32) + far_log[1:2, at : at + 128]) * other
        ).astype(LOW)
    valid = flags[0]
    for at in range(0, weights.shape[1], 256):
        out = dot(out_ref[...], weights[:, at : at + 256])
        grad = cot[:, at : at + 256].astype(F32)
        sums_ref[0:1, at : at + 256] = column_sums(out) * valid
        sums_ref[1:2, at : at + 256] = column_sums(out * out) * valid
        sums_ref[2:3, at : at + 256] = column_sums(grad) * valid
        sums_ref[3:4, at : at + 256] = column_sums(grad * out) * valid
    sums_ref[4:5, :] = jnp.zeros((1, weights.shape[1]), F32)
    sums_ref[4:5, :inner] = column_sums(out_ref[...].astype(F32)) * valid


def merge(flags, own, own_log, far, far_log, weights, cot):
    rows, inner = own.shape
    width = weights.shape[1]
    return call(
        merge_kernel,
        [((rows, inner), LOW), ((rows, 128), F32), ((5, width), F32)],
        (flags, own, own_log, far, far_log, weights, cot),
    )


def outer_kernel(
    flags,
    att,
    weights,
    sums,
    gains,
    cot,
    res,
    logs,
    mixed_ref,
    grad_ref,
    back_ref,
    term_ref,
    rows_ref,
    norm_ref,
):
    valid = flags[0]
    inverse = flags[3]
    width = weights.shape[1]
    for at in range(0, width, 256):
        span = slice(at, at + 256)
        mean, scale = moments(sums[0:2, span], inverse)
        normal = (dot(att[...], weights[:, span]) - mean) * scale
        gain = gains[0:1, span]
        mixed_ref[:, span] = (
            (res[:, span].astype(F32) + (normal * gain + gains[1:2, span])) * valid
        ).astype(LOW)
        shift_grad = sums[2:3, span]
        gain_grad = scale * (sums[3:4, span] - mean * shift_grad)
        norm_ref[0:1, span] = gain_grad
        norm_ref[1:2, span] = shift_grad
        removed = (shift_grad + normal * gain_grad) * inverse
        grad = ((gain * scale * valid) * (cot[:, span].astype(F32) - removed)).astype(LOW)
        grad_ref[:, span] = grad
        norm_ref[2:3, span] = column_sums(grad.astype(F32))
    back = dot(grad_ref[...], weights[...], NT).astype(LOW)
    back_ref[...] = back
    term = jnp.sum(back.astype(F32) * att[...].astype(F32), axis=1, keepdims=True)
    term = jnp.broadcast_to(term, term_ref.shape)
    term_ref[...] = term
    rows_ref[...] = row_of(logs[...], rows_ref.shape[1])
    rows_ref[1:2, :] = row_of(term, rows_ref.shape[1])[0:1]


def outer(flags, att, weights, sums, gains, cot, res, logs):
    rows, inner = att.shape
    width = weights.shape[1]
    span = -(-rows // 128) * 128
    return call(
        outer_kernel,
        [
            ((rows, width), LOW),
            ((rows, width), LOW),
            ((rows, inner), LOW),
            ((rows, 128), F32),
            ((8, span), F32),
            ((3, width), F32),
        ],
        (flags, att, weights, sums, gains, cot, res, logs),
        micros=5,
    )


def project_kernel(
    flags,
    query_own,
    query_far,
    keep,
    near_keys,
    near_values,
    far,
    act,
    cells,
    weights,
    sums,
    gains,
    embed_far,
    cot_far,
    proj_ref,
    pre_ref,
    sums_ref,
    embed,
    cot,
    sems,
):
    valid = flags[0]
    inner = query_own.shape[1]
    copies = [
        pltpu.make_async_copy(embed_far, embed, sems.at[0]),
        pltpu.make_async_copy(cot_far, cot, sems.at[1]),
    ]
    for copy in copies:
        copy.start()
    proj_ref[:, :inner] = (query_own[...].astype(F32) + query_far[...].astype(F32)).astype(LOW)
    for at in range(0, 2 * inner, 256):
        span = slice(at, at + 256)
        near = near_keys[:, span] if at < inner else near_values[:, at - inner : at - inner + 256]
        proj_ref[:, inner + at : inner + at + 256] = (
            keep[:, span].astype(F32) + near.astype(F32) + far[:, span].astype(F32)
        ).astype(LOW)
    for copy in copies:
        copy.wait()
    for at in range(0, weights.shape[1], 256):
        span = slice(at, at + 256)
        normal, pre, _ = residual_tile(flags, act, cells, weights, sums, gains, at)
        grad = cot[:, span].astype(F32) + dot(proj_ref[...], embed[span, :], NT)
        out = grad * valid * slope(pre)
        pre_ref[:, span] = out
        sums_ref[0:1, span] = column_sums(out)
        sums_ref[1:2, span] = column_sums(out * normal)


def project_back(flags, query_own, query_far, keep, near_keys, near_values, far, act, cells, weights, sums, gains, embed, cot):
    rows, width = cells.shape
    inner = query_own.shape[1]
    return call(
        project_kernel,
        [((rows, 3 * inner), LOW), ((rows, width), F32), ((2, width), F32)],
        (flags, query_own, query_far, keep, near_keys, near_values, far, act, cells, weights, sums, gains, embed, cot),
        scratch=[
            pltpu.VMEM(embed.shape, LOW),
            pltpu.VMEM(cot.shape, LOW),
            pltpu.SemaphoreType.DMA((2,)),
        ],
        far=(12, 13),
        micros=10,
    )


def last_back_kernel(
    flags, pre_grad, act, weights, sums, gains, back_sums, pre_two, sums_two, gains_two, grad_ref, two_ref, sums_ref
):
    valid = flags[0]
    inverse = flags[3]
    two = None
    for at in range(0, weights.shape[1], 256):
        span = slice(at, at + 256)
        mean, scale = moments(sums[:, span], inverse)
        normal = (dot(act[...], weights[:, span]) - mean) * scale
        removed = (back_sums[0:1, span] + normal * back_sums[1:2, span]) * inverse
        grad = ((gains[0:1, span] * scale * valid) * (pre_grad[:, span] - removed)).astype(LOW)
        grad_ref[:, span] = grad
        part = dot(grad, weights[:, span], NT)
        two = part if two is None else two + part
    normal, active, _ = act_of(flags, pre_two[...], sums_two[...], gains_two[...])
    two = two * valid * slope(active)
    two_ref[...] = two
    sums_ref[0:1, :] = column_sums(two)
    sums_ref[1:2, :] = column_sums(two * normal)


def last_back(flags, pre_grad, act, weights, sums, gains, back_sums, pre_two, sums_two, gains_two):
    rows, width = pre_grad.shape
    narrow = act.shape[1]
    return call(
        last_back_kernel,
        [((rows, width), LOW), ((rows, narrow), F32), ((2, narrow), F32)],
        (flags, pre_grad, act, weights, sums, gains, back_sums, pre_two, sums_two, gains_two),
    )


def middle_back_kernel(
    flags, two, back_sums, pre_two, sums_two, gains_two, pre_one, sums_one, gains_one, weights, edges,
    grad_ref, one_ref, sums_ref, buffer, columns
):
    rows, narrow = two.shape
    valid = flags[0]
    inverse = flags[3]
    normal, _, scale = act_of(flags, pre_two[...], sums_two[...], gains_two[...])
    removed = (back_sums[0:1] + normal * back_sums[1:2]) * inverse
    grad = (gains_two[0:1, :] * scale * valid) * (two[...] - removed)
    grad_ref[...] = grad.astype(LOW)
    spread(grad, edges[...], buffer, columns, rows)
    one = None
    for tap in range(9):
        part = dot(columns[:, tap * narrow : (tap + 1) * narrow], tap_of(weights, 8 - tap), NT)
        one = part if one is None else one + part
    normal, active, _ = act_of(flags, pre_one[...], sums_one[...], gains_one[...])
    one = one * valid * slope(active)
    one_ref[...] = one
    sums_ref[0:1, :] = column_sums(one)
    sums_ref[1:2, :] = column_sums(one * normal)


def middle_back(flags, two, back_sums, pre_two, sums_two, gains_two, pre_one, sums_one, gains_one, weights, edges):
    rows, narrow = two.shape
    return call(
        middle_back_kernel,
        [((rows, narrow), LOW), ((rows, narrow), F32), ((2, narrow), F32)],
        (flags, two, back_sums, pre_two, sums_two, gains_two, pre_one, sums_one, gains_one, weights, edges),
        scratch=spread_scratch(rows, narrow),
    )


def middle_weight_kernel(flags, pre_one, sums_one, gains_one, grad, edges, out_ref, buffer, columns):
    rows, narrow = pre_one.shape
    _, act, _ = act_of(flags, pre_one[...], sums_one[...], gains_one[...])
    spread(act * sig(act) * flags[0], edges[...], buffer, columns, rows)
    for tap in range(9):
        out_ref[pl.ds(tap * narrow, narrow), :] = dot(
            columns[:, tap * narrow : (tap + 1) * narrow], grad[...], TN
        ).astype(LOW)


def middle_weight(flags, pre_one, sums_one, gains_one, grad, edges):
    rows, narrow = pre_one.shape
    return call(
        middle_weight_kernel,
        [((9 * narrow, narrow), LOW)],
        (flags, pre_one, sums_one, gains_one, grad, edges),
        scratch=spread_scratch(rows, narrow),
    )[0]


def first_grad_kernel(flags, one, back_sums, pre_one, sums_one, gains_one, grad_ref):
    normal, _, scale = act_of(flags, pre_one[...], sums_one[...], gains_one[...])
    removed = (back_sums[0:1] + normal * back_sums[1:2]) * flags[3]
    grad_ref[...] = (
        (gains_one[0:1, :] * scale * flags[0]) * (one[...] - removed)
    ).astype(LOW)


def first_grad_of(flags, one, back_sums, pre_one, sums_one, gains_one):
    rows, narrow = one.shape
    return call(
        first_grad_kernel,
        [((rows, narrow), LOW)],
        (flags, one, back_sums, pre_one, sums_one, gains_one),
    )[0]


def first_back_kernel(
    place, flags, grad, before, after, cells, middle, last, mine, others, cols_ref, buffer, halves, sems
):
    rows, narrow = grad.shape
    width = cells.shape[1]
    spots = before.shape[0]
    buffer[pl.ds(0, spots), :] = before[...].astype(F32) * flags[1]
    buffer[pl.ds(spots, rows), :] = grad[...].astype(F32)
    buffer[pl.ds(spots + rows, spots), :] = after[...].astype(F32) * flags[2]
    at = middle.shape[0]
    put_rows(halves, 0, middle[...])
    for tap in range(3):
        part = (buffer[pl.ds(spots * (2 - tap), rows), :] * flags[0]).astype(LOW)
        cols_ref[:, tap * narrow : (tap + 1) * narrow] = part
        put_rows(halves, at, dot(cells[...], part, TN).astype(LOW))
        at += width
    put_rows(halves, at, last[...])
    deal(place, halves, mine, others, sems)


def first_back(place, flags, grad, before, after, cells, middle, last):
    rows, narrow = grad.shape
    spots = before.shape[0]
    width = cells.shape[1]
    mine, others, cols = halves_call(
        first_back_kernel,
        middle.shape[0] + 3 * width + last.shape[0],
        [((rows, 3 * narrow), LOW)],
        (place, flags, grad, before, after, cells, middle, last),
        scratch=[pltpu.VMEM((rows + 2 * spots, narrow), F32)],
    )
    return (mine, others), cols


def early_weight_kernel(
    place, flags, res, proj, att, sums, grad, mine, others, halves, sems
):
    height, inner = res.shape[1], att.shape[1]
    left = (att[...].astype(F32) - sums[...] * flags[3]).astype(LOW)
    at = 0
    for index in range(proj.shape[1] // 256):
        put_rows(
            halves, at, dot(res[...], proj[:, index * 256 : (index + 1) * 256], TN).astype(LOW)
        )
        at += height
    for index in range(grad.shape[1] // 256):
        put_rows(
            halves, at, dot(left, grad[:, index * 256 : (index + 1) * 256], TN).astype(LOW)
        )
        at += inner
    deal(place, halves, mine, others, sems)


def halves_call(kernel, height, outs, args, scratch=()):
    shape = (height // 2, 256)
    return call(
        kernel,
        [(shape, LOW), (shape, LOW)] + outs,
        args,
        scalars=2,
        scratch=list(scratch)
        + [pltpu.VMEM((2,) + shape, LOW), pltpu.SemaphoreType.DMA((2,))],
        far_out=(0, 1),
        micros=8,
    )


def early_weight(place, flags, res, proj, att, sums, grad):
    height = res.shape[1] * proj.shape[1] // 256 + att.shape[1] * grad.shape[1] // 256
    return halves_call(
        early_weight_kernel, height, [], (place, flags, res, proj, att, sums, grad)
    )


def weight_kernel(left, right, out_ref):
    height = left.shape[1]
    for index in range(right.shape[1] // 256):
        out_ref[pl.ds(index * height, height), :] = dot(
            left[...], right[:, index * 256 : (index + 1) * 256], TN
        ).astype(LOW)


def weight_grad(left, right):
    rows, height = left.shape
    width = right.shape[1]
    return call(
        weight_kernel,
        [((height * width // 256, 256), LOW)],
        (left, right),
        scalars=0,
    )[0]


def pieces_of(low_half, high_half, start, stop):
    middle = low_half.shape[0]
    if start < middle:
        yield 0, low_half[pl.ds(start, min(stop, middle) - start), :]
    if stop > middle:
        begin = max(start, middle)
        yield begin - start, high_half[pl.ds(begin - middle, stop - begin), :]


def squares_of(values):
    return jnp.sum((values * values).reshape(-1, 8, values.shape[-1]), axis=0)


def emit(place, half, other, shares, squares):
    def write(low_half, high_half):
        squares[...] = jnp.zeros_like(squares)
        for start, stop, store, extra in shares:
            for offset, rows in pieces_of(low_half, high_half, start, stop):
                values = rows.astype(F32)
                if extra is not None:
                    values = values + extra[offset : offset + values.shape[0]]
                squares[...] += squares_of(values)
                store(offset, values)

    @pl.when(place[0] == 0)
    def _():
        write(half, other)

    @pl.when(place[0] == 1)
    def _():
        write(other, half)


def store_rows(ref, lead, cols):
    def store(offset, values):
        ref[lead + (pl.ds(offset, values.shape[0]), cols)] = values

    return store


def early_shares(embed_ref, back_ref, mean, grad_sum):
    width, inner = embed_ref.shape[1], embed_ref.shape[2]
    shares = []
    at = 0
    for index in range(3 * inner // 256):
        part, col = divmod(index * 256, inner)
        shares.append((at, at + width, store_rows(embed_ref, (part,), slice(col, col + 256)), None))
        at += width
    for index in range(width // 256):
        cols = slice(index * 256, index * 256 + 256)
        extra = mean[:, 0:1] * grad_sum[0:1, cols]
        shares.append((at, at + inner, store_rows(back_ref, (), cols), extra))
        at += inner
    return shares


def early_kernel(place, flags, half, other, sums, grad_sum, embed_ref, back_ref, embed_own, back_own, squares_ref):
    mean = sums[...] * flags[3]
    emit(place, half, other, early_shares(embed_ref, back_ref, column_of(mean), grad_sum), squares_ref)
    span = embed_own.shape[1]
    embed_own[...] = embed_ref[:, pl.ds(pl.multiple_of(place[1] * span, span), span), :]
    span = back_own.shape[0]
    back_own[...] = back_ref[pl.ds(pl.multiple_of(place[1] * span, span), span), :]


def early_grads(place, flags, half, other, sums, grad_sum, width, inner, shards):
    return call(
        early_kernel,
        [
            ((3, width, inner), F32),
            ((inner, width), F32),
            ((3, width // shards, inner), F32),
            ((inner // shards, width), F32),
            ((8, 256), F32),
        ],
        (place, flags, half, other, sums, grad_sum),
        scalars=2,
        micros=6,
    )


def late_shares(first_ref, middle_ref, last_ref):
    shares = []
    at = 0
    for ref in (middle_ref, first_ref):
        for index in range(ref.shape[0]):
            shares.append((at, at + ref.shape[1], store_rows(ref, (index,), slice(None)), None))
            at += ref.shape[1]
    for index in range(last_ref.shape[1] // 256):
        cols = slice(index * 256, index * 256 + 256)
        shares.append((at, at + last_ref.shape[0], store_rows(last_ref, (), cols), None))
        at += last_ref.shape[0]
    return shares


def late_kernel(rates, place, half, other, squares, extra, embed_own, back_own, *refs):
    given = [refs[3 * index : 3 * index + 3] for index in range(5)]
    first_ref, middle_ref, last_ref, norm_ref = refs[15:19]
    made = [refs[19 + 3 * index : 22 + 3 * index] for index in range(5)]
    tally = refs[34]
    emit(place, half, other, late_shares(first_ref, middle_ref, last_ref), tally)
    found = jnp.sum(tally[...] + squares[...], axis=0, keepdims=True)
    norm = jnp.sqrt(jnp.sum(found, axis=1, keepdims=True) + extra[0:1, 0:1])
    factor = jnp.minimum(1.0, CLIP_AT / (norm + 1e-06))
    norm_ref[0:1, :] = jnp.broadcast_to(norm, (1, 128))
    norm_ref[1:2, :] = jnp.broadcast_to(factor, (1, 128))

    def mine(span):
        return pl.ds(pl.multiple_of(place[1] * span, span), span)

    def own(index, part):
        if index == 0:
            return first_ref[part, mine(given[0][0].shape[1]), :]
        if index == 1:
            return middle_ref[part, mine(given[1][0].shape[1]), :]
        if index == 2:
            return last_ref[mine(given[2][0].shape[0]), :]
        return embed_own[part] if index == 3 else back_own[...]

    for index in range(5):
        master, moment, second = given[index]
        outs = made[index]
        for part in range(master.shape[0]) if len(master.shape) == 3 else (slice(None),):
            values = adam_step(
                master[part], own(index, part), moment[part], second[part], factor, rates[index]
            )
            for ref, value in zip(outs, values):
                ref[part] = value


def late_grads(rates, place, half, other, squares, extra, embed_own, back_own, states, shapes):
    flat = tuple(item for state in states for item in state)
    outs = [(shape, F32) for shape in shapes] + [((2, 128), F32)]
    outs += [(state[0].shape, F32) for state in states for _ in range(3)]
    found = call(
        functools.partial(late_kernel, rates),
        outs,
        (place, half, other, squares, extra, embed_own, back_own) + flat,
        scratch=[pltpu.VMEM((8, 256), F32)],
        micros=8,
    )
    return found[:3], found[3], [found[4 + 3 * index : 7 + 3 * index] for index in range(5)]


def unfold(value, height):
    return jnp.moveaxis(value.reshape(-1, height, 256), 0, 1).reshape(height, -1)


def plain_tail(early, late, mean, grad_sum, sizes, norm_square, states, rates, chan_at):
    width, inner, narrow = sizes
    core = chan_at & 1
    early, late = [
        jnp.where(core == 0, jnp.concatenate([half, other]), jnp.concatenate([other, half])).astype(
            F32
        )
        for half, other in (early, late)
    ]
    cut = 3 * inner * width // 256
    embed = unfold(early[:cut], width).reshape(width, 3, inner)
    back = unfold(early[cut:], inner) + mean[:, None] * grad_sum[None, :]
    middle = late[: 9 * narrow].reshape(9, narrow, narrow)
    first = late[9 * narrow : 9 * narrow + 3 * width].reshape(3, width, narrow)
    last = unfold(late[9 * narrow + 3 * width :], narrow)
    grads = (first, middle, last, jnp.moveaxis(embed, 1, 0), back)
    norm = jnp.sqrt(sum(jnp.sum(item * item) for item in grads) + norm_square)
    factor = jnp.minimum(1.0, CLIP_AT / (norm + 1e-06))
    made = []
    for grad, state, rate in zip(grads, states, rates):
        axis = grad.ndim - 2
        span = state[0].shape[axis]
        owned = lax.dynamic_slice_in_dim(grad, chan_at * span, span, axis)
        made.append(adam_step(state[0], owned, state[1], state[2], factor, rate))
    return grads, norm, factor, made


def input_kernel(cols, weights, pre_grad, out_ref):
    shards, _, span, narrow = weights.shape
    each = 256 // span
    for at in range(0, pre_grad.shape[1], 256):
        out = pre_grad[:, at : at + 256]
        begin = at // span
        for tap in range(3):
            rows = weights[pl.ds(begin, each), tap].reshape(256, narrow)
            out = out + dot(cols[:, tap * narrow : (tap + 1) * narrow], rows, NT)
        span_at = slice(at, at + 256)
        out_ref[:, span_at] = out.astype(LOW)


def input_grad(cols, weights, pre_grad):
    rows, width = pre_grad.shape
    return call(
        input_kernel,
        [((rows, width), LOW)],
        (cols, weights, pre_grad),
        scalars=0,
    )[0]


def adam_step(master, gradient, moment, second, factor, rate):
    clipped = gradient * factor
    moment_new = BETA_ONE * moment + (1.0 - BETA_ONE) * clipped
    second_new = BETA_TWO * second + (1.0 - BETA_TWO) * clipped * clipped
    moment_hat = moment_new / (1.0 - BETA_ONE**STEP)
    second_hat = second_new / (1.0 - BETA_TWO**STEP)
    master_new = master - rate * (
        moment_hat / (jnp.sqrt(second_hat) + ADAM_EPS) + WEIGHT_DECAY * master
    )
    return (moment_new, second_new, master_new)


def body(
    features,
    cotangent,
    frame_counts,
    weight_first,
    weight_middle,
    weight_last,
    weight_embed,
    weight_back,
    norm_params,
    moment_first,
    moment_middle,
    moment_last,
    moment_embed,
    moment_back,
    moment_norm,
    second_first,
    second_middle,
    second_last,
    second_embed,
    second_back,
    second_norm,
):
    chan_at = lax.axis_index("chan")
    device = lax.axis_index("clip") * lax.axis_size("chan") + chan_at
    frames, spot_count, model_width = features.shape
    row_count = frames * spot_count
    narrow = BOT
    inner_width = INNER
    clip_place = chan_at % DPC
    clip_at = device // DPC
    clip_ids = jnp.arange(frame_counts.shape[0], dtype=jnp.int32)
    length = jnp.sum(jnp.where(clip_ids == clip_at, frame_counts, 0))

    def valid_at(place):
        return ((place >= 0) & (place < DPC) & (place * frames < length)).astype(jnp.float32)

    place = jnp.stack([chan_at & 1, chan_at, lax.axis_index("clip")]).astype(jnp.int32)
    own_ok = valid_at(clip_place)
    row_total = jnp.sum(frame_counts).astype(jnp.float32) * spot_count
    zero = jnp.zeros((), jnp.float32)
    flags = jnp.stack(
        [own_ok, valid_at(clip_place - 1), valid_at(clip_place + 1), 1.0 / row_total]
        + [valid_at(clip_place ^ 2)] + [zero] * 3
    )
    held = sum(valid_at(clip_place ^ turn) for turn in range(4)) * own_ok
    blocks_own = held.astype(jnp.int32).reshape(1)
    blocks_far = (held * valid_at(clip_place ^ 4)).astype(jnp.int32).reshape(1)
    span_list = [narrow] * 4 + [model_width] * 4
    starts = [sum(span_list[:index]) for index in range(8)]
    gains_one, gains_two, gains_three, gains_four = [
        norm_params[starts[index] : starts[index] + 2 * span_list[index]].reshape(2, -1)
        for index in range(0, 8, 2)
    ]
    shards = lax.axis_size("chan")
    tall = weight_middle.shape[0] * weight_middle.shape[1]
    packed = jnp.concatenate(
        [
            weight_middle.reshape(tall, narrow),
            jnp.moveaxis(weight_last.reshape(-1, model_width // 256, 256), 1, 0).reshape(-1, 256),
        ]
    ).astype(LOW)
    packed = lax.all_gather(packed, "chan", axis=0, tiled=False)
    middle_low = packed[:, :tall].reshape((shards,) + weight_middle.shape)
    last_low = jnp.moveaxis(
        packed[:, tall:].reshape(shards, model_width // 256, -1, 256), 1, 2
    ).reshape(narrow, model_width)
    if weight_middle.shape[1] % 16:
        middle_low = jnp.moveaxis(middle_low, 0, 1).reshape(1, 9, narrow, narrow)
    embed_low, back_low = (
        lax.all_gather(weight_embed.astype(LOW).reshape(-1, 3 * inner_width), "chan", axis=0, tiled=True),
        lax.all_gather(weight_back.astype(LOW), "chan", axis=0, tiled=True),
    )
    spots = np.arange(row_count)
    across, down = spots % WW, spots // WW % HH
    edges = jnp.asarray(
        np.stack([across > 0, across < WW - 1, down > 0, down < HH - 1] + [across < 0] * 4, axis=1)
        .astype(np.float32)
    )
    cells = features.reshape(row_count, model_width)
    cot = cotangent.reshape(row_count, model_width)
    before, after = beside(features, spot_count)
    if shards == 8 and lax.axis_size("clip") == 4:
        pre_one, sums_one, first_low = first_conv_parts(
            place, flags, cells, before, after, *quarters_of(weight_first)
        )
    else:
        first_low = whole_of(weight_first)
        pre_one, sums_one = first_conv(flags, cells, before, after, first_low)
    sums_one = total(sums_one)
    pre_two, sums_two = middle_conv(
        flags, pre_one, sums_one, gains_one, middle_low, edges
    )
    sums_two = total(sums_two)
    act_two, sums_three = last_conv(flags, pre_two, sums_two, gains_two, last_low)
    sums_three, cot = total(sums_three, (cot,))
    residual_low, query, pair_own = embed_rows(
        flags, act_two, cells, last_low, sums_three, gains_three, embed_low
    )
    pair_core = flipped(pair_own, "chan", 1)
    query_far, pair_far = flipped(query, "chan", 4), flipped(pair_own, "chan", 2)
    query_far, pair_far, back_low = tied(query_far, pair_far, back_low)
    blocks = (pair_own, pair_core, pair_far, flipped(pair_far, "chan", 1))
    part_far, log_far = attend(blocks_far, query_far, blocks, True)
    part_far = flipped(part_far, "chan", 4)
    log_far = flipped(log_far, "chan", 4)
    part_own, log_own = attend(blocks_own, query, blocks, False)
    attended, logs, sums_four = merge(flags, part_own, log_own, part_far, log_far, back_low, cot)
    sums_four = total(sums_four)
    mixed, attn_grad, attended_grad, terms, packed, norm_four = outer(
        flags, attended, back_low, sums_four, gains_four, cot, residual_low, logs
    )
    mixed = laid_out(mixed, frames)
    attended_grad_far = flipped(attended_grad, "chan", 4)
    packed_far = flipped(packed, "chan", 4)
    query_own, held = attend_back(
        blocks_own, query, attended_grad, (logs, terms), blocks, (0, 1, 2, 3), None, None, F32
    )
    query_part, (far, far_core) = attend_back(
        blocks_far, query_far, attended_grad_far, (packed_far,), blocks[2:], (2, 3), held[2:], None, F32
    )
    far = (far.astype(F32) + flipped(far_core, "chan", 1).astype(F32)).astype(LOW)
    far, near_own = tied(far, held[0])
    far = flipped(far, "chan", 2)
    query_part, (keep, give_keys, give_values) = attend_back(
        blocks_far, query_far, attended_grad_far, (packed_far,), blocks[:2], (0, 1), (near_own, held[1]),
        query_part, LOW, (1,),
    )
    query_part = flipped(query_part, "chan", 4)
    near_keys, near_values = flipped(give_keys, "chan", 1), flipped(give_values, "chan", 1)
    projected_grad, pre_grad, back_three = project_back(
        flags, query_own, query_part, keep, near_keys, near_values, far, act_two, cells, last_low, sums_three,
        gains_three, embed_low, cot,
    )
    early = early_weight(
        place, flags, residual_low, projected_grad, attended, sums_four[4:5, :inner_width], attn_grad
    )
    back_three, *early = total(jnp.concatenate([back_three, norm_four[2:3]]), early)
    last_grad, two_grad, back_two = last_back(
        flags, pre_grad, act_two, last_low, sums_three, gains_three, back_three, pre_two, sums_two,
        gains_two,
    )
    back_two = total(back_two)
    last_local = weight_grad(act_two, last_grad)
    middle_grad, one_grad, back_one = middle_back(
        flags, two_grad, back_two, pre_two, sums_two, gains_two, pre_one, sums_one, gains_one,
        middle_low, edges,
    )
    back_one = total(back_one)
    middle_local = middle_weight(flags, pre_one, sums_one, gains_one, middle_grad, edges)
    first_grad = first_grad_of(flags, one_grad, back_one, pre_one, sums_one, gains_one)
    before, after = beside(first_grad.reshape(frames, spot_count, narrow), spot_count)
    late, grad_cols = first_back(place, flags, first_grad, before, after, cells, middle_local, last_local)
    features_gradient = laid_out(input_grad(grad_cols, first_low, pre_grad), frames)
    gain_one_grad, shift_one_grad = back_one[1], back_one[0]
    gain_two_grad, shift_two_grad = back_two[1], back_two[0]
    gain_three_grad, shift_three_grad = back_three[1], back_three[0]
    gain_four_grad, shift_four_grad = norm_four[0], norm_four[1]
    norm_gradient = jnp.concatenate(
        [
            gain_one_grad,
            shift_one_grad,
            gain_two_grad,
            shift_two_grad,
            gain_three_grad,
            shift_three_grad,
            gain_four_grad,
            shift_four_grad,
        ]
    )
    groups = [list(range(core, shards, 2)) for core in range(2)]
    early = lax.psum_scatter(core_step(*early), "clip", scatter_dimension=0, tiled=True)
    early = lax.psum(early, "chan", axis_index_groups=groups)
    steps = level_steps()[1:]
    late = scatter_sum(core_step(*late), steps)
    early, late = tied(early, late)
    early = lax.all_gather(early, "clip", axis=0, tiled=True)
    late = gather_sum(late, steps)
    early, late, mixed, features_gradient = tied(early, late, mixed, features_gradient)
    early = (early, flipped(early, "chan", 1))
    late = (late, flipped(late, "chan", 1))
    fans = (3 * D, 9 * BOT, BOT, D, INNER)
    rates = tuple(0.5 * fan ** (-0.5) for fan in fans)
    states = (
        (weight_first, moment_first, second_first),
        (weight_middle, moment_middle, second_middle),
        (weight_last, moment_last, second_last),
        tuple(jnp.moveaxis(item, 1, 0) for item in (weight_embed, moment_embed, second_embed)),
        (weight_back, moment_back, second_back),
    )
    norm_square = jnp.sum(norm_gradient * norm_gradient)
    if weight_middle.shape[1] % 16 == 0:
        embed, back, embed_own, back_own, squares = early_grads(
            place,
            flags,
            *early,
            sums_four[4:5, :inner_width],
            back_three[2:3],
            model_width,
            inner_width,
            shards,
        )
        shapes = ((3, model_width, narrow), (9, narrow, narrow), (narrow, model_width))
        (first, middle, last), norm_row, results = late_grads(
            rates, place, *late, squares, norm_square.reshape(1, 1), embed_own, back_own, states, shapes
        )
        gradient_norm, factor = norm_row[0, 0], norm_row[1, 0]
    else:
        (first, middle, last, embed, back), gradient_norm, factor, results = plain_tail(
            early,
            late,
            sums_four[4, :inner_width] * flags[3],
            back_three[2],
            (model_width, inner_width, narrow), norm_square, states, rates, chan_at
        )
    results = list(results)
    results[3] = tuple(jnp.moveaxis(item, 0, 1) for item in results[3])
    results.append(adam_step(norm_params, norm_gradient, moment_norm, second_norm, factor, GAIN_RATE))
    return (
        mixed,
        features_gradient,
        first,
        middle,
        last,
        jnp.moveaxis(embed, 0, 1),
        back,
        norm_gradient,
    ) + tuple(results[index][kind] for kind in range(3) for index in range(6)) + (gradient_norm,)


def solution(mesh):
    placed = (
        P(("clip", "chan"), None, None),
        P(("clip", "chan"), None, None),
        P(),
        P(None, "chan", None),
        P(None, "chan", None),
        P("chan", None),
        P("chan", None, None),
        P("chan", None),
        P(),
        P(None, "chan", None),
        P(None, "chan", None),
        P("chan", None),
        P("chan", None, None),
        P("chan", None),
        P(),
        P(None, "chan", None),
        P(None, "chan", None),
        P("chan", None),
        P("chan", None, None),
        P("chan", None),
        P(),
    )
    return jax.shard_map(
        body,
        mesh=mesh,
        in_specs=placed,
        out_specs=(
            P(("clip", "chan"), None, None),
            P(("clip", "chan"), None, None),
            P(),
            P(),
            P(),
            P(),
            P(),
            P(),
            P(None, "chan", None),
            P(None, "chan", None),
            P("chan", None),
            P("chan", None, None),
            P("chan", None),
            P(),
            P(None, "chan", None),
            P(None, "chan", None),
            P("chan", None),
            P("chan", None, None),
            P("chan", None),
            P(),
            P(None, "chan", None),
            P(None, "chan", None),
            P("chan", None),
            P("chan", None, None),
            P("chan", None),
            P(),
            P(),
        ),
        check_vma=False,
    )
```

```python
import functools
import math

import jax
import jax.numpy as jnp
import numpy as np
from jax import lax
from jax.experimental import pallas as pl
from jax.experimental.layout import Layout, with_layout_constraint
from jax.experimental.pallas import tpu as pltpu
from jax.sharding import PartitionSpec as P

D = 1024
BOT = 256
INNER = 512
HH = 14
WW = 14
STEP = 10
DPC = 8


EPS_NORM = 1e-05
BETA_ONE = 0.9
BETA_TWO = 0.95
ADAM_EPS = 1e-08
WEIGHT_DECAY = 0.01
CLIP_AT = 1.0
GAIN_RATE = 0.5


def flipped(value, axis, mask):
    pairs = [(source, source ^ mask) for source in range(lax.axis_size(axis))]
    return lax.ppermute(value, axis, pairs)


def whole_of(shard):
    return lax.all_gather(shard.astype(jnp.bfloat16), "chan", axis=0, tiled=False)


def quarter_of(shard):
    span = shard.shape[1] // 4
    return lax.dynamic_slice_in_dim(
        shard, lax.axis_index("clip") * span, span, axis=1
    ).astype(jnp.bfloat16)[None]


def quarters_of(piece):
    chips = jnp.concatenate(
        [piece] + [flipped(piece, "chan", 2 * turn) for turn in range(1, 4)]
    )[None]
    mine = jnp.concatenate([chips] + [flipped(chips, "clip", turn) for turn in range(1, 4)])
    return mine, flipped(mine, "chan", 1)


def tap_of(weights, tap):
    return weights[:, tap].reshape(weights.shape[0] * weights.shape[2], weights.shape[3])


def beside(cells, spots):
    ends = lax.axis_size("chan") - 1
    upward = [(index, index + 1) for index in range(ends)]
    downward = [(index + 1, index) for index in range(ends)]
    return (
        lax.ppermute(cells[-1:], "chan", upward).reshape(spots, cells.shape[-1]),
        lax.ppermute(cells[:1], "chan", downward).reshape(spots, cells.shape[-1]),
    )


def total(value, beside=()):
    steps = [("chan", group) for group in level_groups("chan")]
    steps += [("clip", group) for group in level_groups("clip")]
    for index, (axis, group) in enumerate(steps):
        base = 1 << group[0]
        parts = [flipped(value, axis, base * turn) for turn in range(1, 1 << len(group))]
        if beside and index == len(steps) - 1:
            tie = lax.optimization_barrier((parts, list(beside)))
            parts, beside = tie
        value = value + sum(parts[1:], parts[0])
    return (value, *beside) if beside else value


def level_groups(axis):
    bits = lax.axis_size(axis).bit_length() - 1
    levels = list(range(bits))
    groups = [levels[:1]] if axis == "chan" else []
    rest = levels[len(groups) :]
    return groups + [rest[index : index + 2] for index in range(0, len(rest), 2)]


def level_steps():
    order = [("chan", group) for group in level_groups("chan")]
    order = order[:1] + [("clip", group) for group in level_groups("clip")] + order[1:]
    steps = []
    for axis, group in order:
        base, count = 1 << group[0], 1 << len(group)
        steps.append((axis, base, count, (lax.axis_index(axis) >> group[0]) & (count - 1)))
    return steps


def half_kernel(mine, arrived, out_ref):
    out_ref[...] = (mine[...].astype(F32) + arrived[...].astype(F32)).astype(LOW)


def core_step(mine, others):
    arrived = flipped(others, "chan", 1)
    return call(half_kernel, [(mine.shape, LOW)], (mine, arrived), scalars=0)[0]


def deal(place, halves, mine, others, sems):
    copies = [
        pltpu.make_async_copy(halves.at[place[0]], mine, sems.at[0]),
        pltpu.make_async_copy(halves.at[1 - place[0]], others, sems.at[1]),
    ]
    for copy in copies:
        copy.start()
    for copy in copies:
        copy.wait()


def put_rows(halves, at, values):
    size = halves.shape[1]
    cut = max(0, min(values.shape[0], size - at))
    if cut:
        halves[0, pl.ds(at, cut), :] = values[:cut]
    if cut < values.shape[0]:
        halves[1, pl.ds(at + cut - size, values.shape[0] - cut), :] = values[cut:]


def scatter_sum(value, steps):
    for axis, base, count, place in steps:
        size = value.shape[0] // count
        mine = lax.dynamic_slice_in_dim(value, place * size, size).astype(F32)
        arrived = [
            flipped(
                lax.dynamic_slice_in_dim(value, (place ^ turn) * size, size), axis, base * turn
            )
            for turn in range(1, count)
        ]
        for item in arrived:
            mine = mine + item.astype(F32)
        value = mine.astype(LOW)
    return value


def laid_out(rows, frames):
    grid = rows.reshape(frames, -1, rows.shape[1])
    return with_layout_constraint(grid, Layout(major_to_minor=(1, 0, 2)))


def tied(*values):
    return lax.optimization_barrier(values)


def gather_sum(value, steps):
    for axis, base, count, place in reversed(steps):
        size = value.shape[0]
        parts = [value] + [flipped(value, axis, base * turn) for turn in range(1, count)]
        whole = jnp.zeros((count,) + value.shape, LOW)
        for turn, part in enumerate(parts):
            whole = lax.dynamic_update_index_in_dim(whole, part, place ^ turn, 0)
        value = whole.reshape((count * size,) + value.shape[1:])
    return value


NEG = -1e30
MIB = 1 << 20
NN = (((1,), (0,)), ((), ()))
NT = (((1,), (1,)), ((), ()))
TN = (((0,), (0,)), ((), ()))
F32 = jnp.float32
LOW = jnp.bfloat16


def dot(left, right, dims=NN):
    return lax.dot_general(left, right, dims, preferred_element_type=F32)


def sig(values):
    return 0.5 * jnp.tanh(0.5 * values) + 0.5


def slope(values):
    gate = sig(values)
    return gate * (1.0 + values * (1.0 - gate))


def moments(sums, inverse):
    mean = sums[0:1] * inverse
    return mean, lax.rsqrt(sums[1:2] * inverse - mean * mean + EPS_NORM)


def column_sums(values):
    return jnp.sum(values, axis=0, keepdims=True)


def call(kernel, outs, args, scalars=1, scratch=(), vmem=16, far=(), far_out=(), micros=2):
    spaces = []
    for index in range(len(args)):
        if index < scalars:
            spaces.append(pl.BlockSpec(memory_space=pltpu.SMEM))
        elif index in far:
            spaces.append(pl.BlockSpec(memory_space=pltpu.HBM))
        else:
            spaces.append(pl.BlockSpec(memory_space=pltpu.VMEM))
    shapes = tuple(jax.ShapeDtypeStruct(shape, dtype) for shape, dtype in outs)
    out_specs = tuple(
        pl.BlockSpec(memory_space=pltpu.HBM if index in far_out else pltpu.VMEM)
        for index in range(len(outs))
    )
    return pl.pallas_call(
        kernel,
        out_shape=shapes,
        in_specs=spaces,
        out_specs=out_specs,
        scratch_shapes=list(scratch),
        compiler_params=pltpu.CompilerParams(vmem_limit_bytes=vmem * MIB),
        cost_estimate=pl.CostEstimate(
            flops=int(micros * 1e9), bytes_accessed=0, transcendentals=0
        ),
    )(*args)


def first_tail(flags, cells, before, after, weights, pre_ref, sums_ref, early, late):
    rows = cells.shape[0]
    spots = before.shape[0]
    valid = flags[0]
    late[pl.ds(0, rows), :] = dot(cells[...], tap_of(weights, 2)) * valid
    late[pl.ds(rows, spots), :] = dot(after[...], tap_of(weights, 2)) * flags[2]
    early[pl.ds(0, spots), :] = dot(before[...], tap_of(weights, 0)) * flags[1]
    early[pl.ds(spots, rows), :] = dot(cells[...], tap_of(weights, 0)) * valid
    pre = (
        dot(cells[...], tap_of(weights, 1)) * valid
        + early[pl.ds(0, rows), :]
        + late[pl.ds(spots, rows), :]
    )
    pre_ref[...] = pre
    sums_ref[0:1, :] = column_sums(pre) * valid
    sums_ref[1:2, :] = column_sums(pre * pre) * valid


def first_parts_kernel(place, flags, cells, before, after, mine, others, pre_ref, sums_ref, weights, early, late):
    for index in range(mine.shape[0]):
        span = mine.shape[3]
        rows = pl.ds(pl.multiple_of((place[2] ^ index) * span, span), span)
        for turn in range(mine.shape[1]):
            weights[place[1] ^ (2 * turn), :, rows, :] = mine[index, turn]
            weights[place[1] ^ (2 * turn + 1), :, rows, :] = others[index, turn]
    first_tail(flags, cells, before, after, weights, pre_ref, sums_ref, early, late)


def first_conv_parts(place, flags, cells, before, after, mine, others):
    rows = cells.shape[0]
    clips, chips, taps, span, narrow = mine.shape
    spots = before.shape[0]
    return call(
        first_parts_kernel,
        [
            ((rows, narrow), F32),
            ((2, narrow), F32),
            ((2 * chips, taps, clips * span, narrow), LOW),
        ],
        (place, flags, cells, before, after, mine, others),
        scalars=2,
        scratch=[pltpu.VMEM((rows + spots, narrow), F32)] * 2,
    )


def first_conv(flags, cells, before, after, weights):
    rows, width = cells.shape
    narrow = weights.shape[3]
    spots = before.shape[0]
    return call(
        first_tail,
        [((rows, narrow), F32), ((2, narrow), F32)],
        (flags, cells, before, after, weights),
        scratch=[pltpu.VMEM((rows + spots, narrow), F32)] * 2,
    )


def spread(values, edges, buffer, columns, rows):
    narrow = values.shape[1]
    margin = 16
    buffer[0, pl.ds(0, margin), :] = jnp.zeros((margin, narrow), F32)
    buffer[0, pl.ds(margin + rows, margin), :] = jnp.zeros((margin, narrow), F32)
    buffer[1, pl.ds(0, margin), :] = jnp.zeros((margin, narrow), F32)
    buffer[1, pl.ds(margin + rows, margin), :] = jnp.zeros((margin, narrow), F32)
    buffer[0, pl.ds(margin, rows), :] = values
    for across in range(3):
        moved = buffer[0, pl.ds(margin + across - 1, rows), :]
        if across == 0:
            moved = moved * edges[:, 0:1]
        if across == 2:
            moved = moved * edges[:, 1:2]
        buffer[1, pl.ds(margin, rows), :] = moved
        for down in range(3):
            part = buffer[1, pl.ds(margin + WW * (down - 1), rows), :]
            if down == 0:
                part = part * edges[:, 2:3]
            if down == 2:
                part = part * edges[:, 3:4]
            at = (3 * down + across) * narrow
            columns[:, at : at + narrow] = part.astype(LOW)


def spread_scratch(rows, narrow):
    return [pltpu.VMEM((2, rows + 32, narrow), F32), pltpu.VMEM((rows, 9 * narrow), LOW)]


def act_of(flags, pre, sums, scale_shift):
    mean, scale = moments(sums, flags[3])
    normal = (pre - mean) * scale
    return normal, normal * scale_shift[0:1] + scale_shift[1:2], scale


def middle_kernel(flags, pre, sums, gains, weights, edges, out_ref, sums_ref, buffer, columns):
    rows, narrow = pre.shape
    valid = flags[0]
    _, act, _ = act_of(flags, pre[...], sums[...], gains[...])
    spread(act * sig(act) * valid, edges[...], buffer, columns, rows)
    out = None
    for tap in range(9):
        part = dot(columns[:, tap * narrow : (tap + 1) * narrow], tap_of(weights, tap))
        out = part if out is None else out + part
    out_ref[...] = out
    sums_ref[0:1, :] = column_sums(out) * valid
    sums_ref[1:2, :] = column_sums(out * out) * valid


def middle_conv(flags, pre, sums, gains, weights, edges):
    rows, narrow = pre.shape
    return call(
        middle_kernel,
        [((rows, narrow), F32), ((2, narrow), F32)],
        (flags, pre, sums, gains, weights, edges),
        scratch=spread_scratch(rows, narrow),
    )


def last_kernel(flags, pre, sums, gains, weights, act_ref, sums_ref):
    valid = flags[0]
    _, act, _ = act_of(flags, pre[...], sums[...], gains[...])
    act_ref[...] = (act * sig(act) * valid).astype(LOW)
    for at in range(0, weights.shape[1], 256):
        out = dot(act_ref[...], weights[:, at : at + 256])
        sums_ref[0:1, at : at + 256] = column_sums(out) * valid
        sums_ref[1:2, at : at + 256] = column_sums(out * out) * valid


def last_conv(flags, pre, sums, gains, weights):
    rows, narrow = pre.shape
    width = weights.shape[1]
    return call(
        last_kernel,
        [((rows, narrow), LOW), ((2, width), F32)],
        (flags, pre, sums, gains, weights),
    )


def residual_tile(flags, act, cells, weights, sums, gains, at):
    mean, scale = moments(sums[:, at : at + 256], flags[3])
    normal = (dot(act[...], weights[:, at : at + 256]) - mean) * scale
    pre = cells[:, at : at + 256].astype(F32) + (
        normal * gains[0:1, at : at + 256] + gains[1:2, at : at + 256]
    )
    return normal, pre, scale


def embed_kernel(flags, act, cells, weights, sums, gains, embed, res_ref, query_ref, pair_ref):
    width = weights.shape[1]
    inner = query_ref.shape[1]
    for at in range(0, width, 256):
        _, pre, _ = residual_tile(flags, act, cells, weights, sums, gains, at)
        res_ref[:, at : at + 256] = (pre * sig(pre) * flags[0]).astype(LOW)
    for at in range(0, inner, 256):
        query_ref[:, at : at + 256] = dot(res_ref[...], embed[:, at : at + 256]).astype(LOW)
    for at in range(0, 2 * inner, 256):
        pair_ref[:, at : at + 256] = dot(
            res_ref[...], embed[:, inner + at : inner + at + 256]
        ).astype(LOW)


def embed_rows(flags, act, cells, weights, sums, gains, embed):
    rows, width = cells.shape
    inner = embed.shape[1] // 3
    return call(
        embed_kernel,
        [((rows, width), LOW), ((rows, inner), LOW), ((rows, 2 * inner), LOW)],
        (flags, act, cells, weights, sums, gains, embed),
        micros=7,
    )


def copies_of(refs, slots, sems):
    return [
        pltpu.make_async_copy(ref, slots.at[index], sems.at[index])
        for index, ref in enumerate(refs)
    ]


def attend_kernel(
    away, count, query, one, two, three, four, out_ref, log_ref, pairs, tails, scores, total, peak, sums, sems
):
    rows, inner = query.shape
    full = rows // 256 * 256
    rest = rows - full
    wide = 4 * rest
    turn = inner**-0.5 * math.log2(math.e)
    blocks = count[0]
    copies = copies_of((one, two, three, four), pairs, sems)
    for copy in copies:
        copy.start()

    @pl.when(blocks == 0)
    def _():
        out_ref[...] = jnp.zeros_like(out_ref)
        if away:
            log_ref[...] = jnp.zeros_like(log_ref)
            log_ref[0:1, :] = jnp.full((1, log_ref.shape[1]), NEG, F32)
        else:
            log_ref[...] = jnp.full_like(log_ref, NEG)

    peak[...] = jnp.full_like(peak, NEG)
    sums[...] = jnp.zeros_like(sums)

    def score(index, _):
        pltpu.make_async_copy(one, pairs.at[index], sems.at[index]).wait()

        @pl.when(index < blocks)
        def _():
            found = dot(query[...], pairs[index, pl.ds(0, full), :inner], NT)
            scores[index] = found
            top = peak[...]
            for at in range(0, full, 128):
                top = jnp.maximum(top, found[:, at : at + 128])
            peak[...] = top

        return 0

    lax.fori_loop(0, 4, score, 0)

    @pl.when(blocks > 0)
    def _():
        for index in range(4):
            tails[pl.ds(index * rest, rest), :] = pairs[index, pl.ds(full, rest), :]
        lane = lax.broadcasted_iota(jnp.int32, (rows, wide), 1)
        end = jnp.where(lane < blocks * rest, dot(query[...], tails[:, :inner], NT), NEG)
        top = jnp.maximum(
            jnp.max(peak[...], axis=1, keepdims=True), jnp.max(end, axis=1, keepdims=True)
        )
        top = top * turn
        lifted = jnp.exp2(end * turn - top)
        end_sum = jnp.sum(lifted, axis=1, keepdims=True)
        total[...] = dot(lifted.astype(LOW), tails[:, inner:])
        peak[...] = jnp.broadcast_to(top, peak.shape)

        def weigh(index, _):
            base = peak[...]
            running = sums[...]
            parts = []
            for at in range(0, full, 128):
                part = jnp.exp2(scores[index, :, at : at + 128] * turn - base)
                running = running + part
                parts.append(part.astype(LOW))
            sums[...] = running
            total[...] += dot(
                jnp.concatenate(parts, axis=1), pairs[index, pl.ds(0, full), inner:]
            )
            return 0

        lax.fori_loop(0, blocks, weigh, 0)
        found = jnp.sum(sums[...], axis=1, keepdims=True) + end_sum
        logs = jnp.broadcast_to(top + jnp.log2(found), peak.shape)
        if away:
            out = total[...] / found
            mean = column_sums(out) * (1.0 / rows)
            out_ref[...] = (out - mean).astype(out_ref.dtype)
            log_ref[...] = row_of(logs, log_ref.shape[1])
            log_ref[1:2, :inner] = mean
        else:
            out_ref[...] = (total[...] / found).astype(out_ref.dtype)
            log_ref[...] = logs


def attend(count, query, blocks, away):
    rows, inner = query.shape
    span = -(-rows // 128) * 128
    full = rows // 256 * 256
    rest = rows - full
    return call(
        functools.partial(attend_kernel, away),
        [((rows, inner), LOW), ((8, span) if away else (rows, 128), F32)],
        (count, query) + tuple(blocks),
        scratch=[
            pltpu.VMEM((4, rows, 2 * inner), LOW),
            pltpu.VMEM((4 * rest, 2 * inner), LOW),
            pltpu.VMEM((4, rows, full), F32),
            pltpu.VMEM((rows, inner), F32),
            pltpu.VMEM((rows, 128), F32),
            pltpu.VMEM((rows, 128), F32),
            pltpu.SemaphoreType.DMA((4,)),
        ],
        vmem=36,
        far=(2, 3, 4, 5),
        micros=10,
    )


def attend_back_kernel(away, held, split, count, query, grad, *refs):
    size = len(held)
    refs = list(refs)
    if away:
        packed = refs.pop(0)
    else:
        log_ref, term_ref = refs.pop(0), refs.pop(0)
    given_query = refs.pop(0) if away and held[0] == 0 else None
    blocks_in = [refs.pop(0) for _ in held]
    given = [refs.pop(0) for _ in held] if away else ()
    query_ref = refs.pop(0)
    outs = [[refs.pop(0) for _ in range(2 if place in split else 1)] for place in held]
    pairs, tails, stage, stage_tails, total, sems, out_sems = refs[:7]
    if away:
        log_ref, term_ref, in_sems = refs[7:]
    rows, inner = query.shape
    full = rows // 256 * 256
    rest = rows - full
    wide = size * rest
    scaling = inner**-0.5
    turn = scaling * math.log2(math.e)
    blocks = count[0]

    def main_of(ref):
        return ref.at[pl.ds(0, full)]

    def tail_of(ref):
        return ref.at[pl.ds(full, rest)]

    def tail_at(index):
        return pl.ds(index * rest, rest)

    begin = [
        pltpu.make_async_copy(tail_of(ref), tails.at[tail_at(index)], sems.at[1, index])
        for index, ref in enumerate(blocks_in)
    ] + [
        pltpu.make_async_copy(tail_of(ref), stage_tails.at[tail_at(index)], in_sems.at[1, index])
        for index, ref in enumerate(given)
    ]
    for copy in begin:
        copy.start()
    for index in range(size):
        pltpu.make_async_copy(main_of(blocks_in[index]), pairs.at[index], sems.at[0, index]).start()
        if away:
            pltpu.make_async_copy(main_of(given[index]), stage.at[index], in_sems.at[0, index]).start()
    if away:
        log_ref[...] = column_of(packed[0:1, :])[:rows]
        term_ref[...] = column_of(packed[1:2, :])[:rows]
    for copy in begin:
        copy.wait()

    def tile(keys, values, span, mask):
        found = dot(query[...], keys, NT)
        back = dot(grad[...], values, NT)
        logs = log_ref[...]
        terms = term_ref[...]
        kept = []
        slopes = []
        for at in range(0, span, 128):
            end = min(at + 128, span)
            weight = jnp.exp2(found[:, at:end] * turn - logs[:, : end - at])
            if mask is not None:
                weight = jnp.where(mask, weight, 0.0)
            kept.append(weight.astype(LOW))
            slopes.append((weight * (back[:, at:end] - terms[:, : end - at])).astype(LOW))
        kept = kept[0] if len(kept) == 1 else jnp.concatenate(kept, axis=1)
        slopes = slopes[0] if len(slopes) == 1 else jnp.concatenate(slopes, axis=1)
        return slopes, dot(slopes, query[...], TN) * scaling, dot(kept, grad[...], TN)

    active = blocks > held[0]

    @pl.when(jnp.logical_not(active))
    def _():
        if given_query is None:
            query_ref[...] = jnp.zeros_like(query_ref)
        else:
            query_ref[...] = given_query[...].astype(query_ref.dtype)
        if not away:
            stage_tails[...] = jnp.zeros_like(stage_tails)

    @pl.when(active)
    def _():
        keys = tails[:, :inner]
        lane = lax.broadcasted_iota(jnp.int32, (rows, wide), 1)
        ok = lane < (blocks - held[0]) * rest
        slopes, key_part, value_part = tile(keys, tails[:, inner:], wide, ok)
        total[...] = dot(slopes, keys)
        if away:
            key_part = key_part + stage_tails[:, :inner].astype(F32)
            value_part = value_part + stage_tails[:, inner:].astype(F32)
        stage_tails[:, :inner] = key_part.astype(LOW)
        stage_tails[:, inner:] = value_part.astype(LOW)

    def columns(which, part):
        width = 2 * inner // len(outs[which])
        return pl.ds(part * width, width)

    def main_outs(which):
        return [
            pltpu.make_async_copy(
                stage.at[which, :, columns(which, part)], main_of(ref), out_sems.at[0, which, part]
            )
            for part, ref in enumerate(outs[which])
        ]

    def one_block(index, _):
        pltpu.make_async_copy(main_of(blocks_in[0]), pairs.at[index], sems.at[0, index]).wait()
        if away:
            pltpu.make_async_copy(main_of(given[0]), stage.at[index], in_sems.at[0, index]).wait()

        @pl.when(index < blocks - held[0])
        def _():
            block = pairs[index, :, :inner]
            slopes, key_part, value_part = tile(block, pairs[index, :, inner:], full, None)
            total[...] += dot(slopes, block)
            if away:
                key_part = key_part + stage[index, :, :inner].astype(F32)
                value_part = value_part + stage[index, :, inner:].astype(F32)
            stage[index, :, :inner] = key_part.astype(LOW)
            stage[index, :, inner:] = value_part.astype(LOW)

        if not away:

            @pl.when(index >= blocks - held[0])
            def _():
                stage[index] = jnp.zeros(stage.shape[1:], LOW)

        for which in range(size):

            @pl.when(index == which)
            def _():
                for copy in main_outs(which):
                    copy.start()

        return 0

    lax.fori_loop(0, size, one_block, 0)
    ends = [
        pltpu.make_async_copy(
            stage_tails.at[tail_at(index), columns(index, part)],
            tail_of(ref),
            out_sems.at[1, index, part],
        )
        for index in range(size)
        for part, ref in enumerate(outs[index])
    ]
    for copy in ends:
        copy.start()

    @pl.when(active)
    def _():
        found = total[...] * scaling
        if given_query is not None:
            found = found + given_query[...]
        query_ref[...] = found.astype(query_ref.dtype)

    for index in range(size):
        for copy in main_outs(index):
            copy.wait()
    for copy in ends:
        copy.wait()


def attend_back(
    count, query, grad, terms, blocks, held, given, given_query, out_type, split=()
):
    rows, inner = query.shape
    full = rows // 256 * 256
    rest = rows - full
    away = given is not None
    size = len(held)
    more = () if given_query is None else (given_query,)
    near = (count, query, grad) + tuple(terms) + more
    distant = tuple(blocks) + (tuple(given) if away else ())
    scratch = [
        pltpu.VMEM((size, full, 2 * inner), LOW),
        pltpu.VMEM((size * rest, 2 * inner), LOW),
        pltpu.VMEM((size, full, 2 * inner), LOW),
        pltpu.VMEM((size * rest, 2 * inner), LOW),
        pltpu.VMEM((rows, inner), F32),
        pltpu.SemaphoreType.DMA((2, size)),
        pltpu.SemaphoreType.DMA((2, size, 2)),
    ]
    widths = []
    for at in held:
        widths += [inner] * 2 if at in split else [2 * inner]
    if away:
        scratch += [pltpu.VMEM((rows, 128), F32)] * 2 + [pltpu.SemaphoreType.DMA((2, size))]
    found = call(
        functools.partial(attend_back_kernel, away, held, split),
        [((rows, inner), out_type)] + [((rows, width), LOW) for width in widths],
        near + distant,
        scratch=scratch,
        vmem=36,
        far=tuple(range(len(near), len(near) + len(distant))),
        far_out=tuple(range(1, 1 + len(widths))),
        micros=17,
    )
    return found[0], found[1:]


def column_of(row):
    return jnp.transpose(jnp.broadcast_to(row, (128, row.shape[1])))


def row_of(column, span):
    tall = jnp.concatenate([column, jnp.zeros((span - column.shape[0], 128), F32)], axis=0)
    return jnp.transpose(tall)[0:8, :]


def merge_kernel(
    flags, own, own_log, far, far_log, weights, cot, out_ref, log_ref, sums_ref
):
    rows, inner = own.shape
    logs = own_log[...]
    others = column_of(far_log[0:1, :])[:rows]
    top = jnp.maximum(logs, others)
    whole = top + jnp.log2(jnp.exp2(logs - top) + jnp.exp2(others - top))
    log_ref[...] = whole
    share = jnp.exp2(logs - whole)
    other = jnp.exp2(others - whole)
    for at in range(0, inner, 128):
        out_ref[:, at : at + 128] = (
            own[:, at : at + 128].astype(F32) * share + (far[:, at : at + 128].astype(F32) + far_log[1:2, at : at + 128]) * other
        ).astype(LOW)
    valid = flags[0]
    for at in range(0, weights.shape[1], 256):
        out = dot(out_ref[...], weights[:, at : at + 256])
        grad = cot[:, at : at + 256].astype(F32)
        sums_ref[0:1, at : at + 256] = column_sums(out) * valid
        sums_ref[1:2, at : at + 256] = column_sums(out * out) * valid
        sums_ref[2:3, at : at + 256] = column_sums(grad) * valid
        sums_ref[3:4, at : at + 256] = column_sums(grad * out) * valid
    sums_ref[4:5, :] = jnp.zeros((1, weights.shape[1]), F32)
    sums_ref[4:5, :inner] = column_sums(out_ref[...].astype(F32)) * valid


def merge(flags, own, own_log, far, far_log, weights, cot):
    rows, inner = own.shape
    width = weights.shape[1]
    return call(
        merge_kernel,
        [((rows, inner), LOW), ((rows, 128), F32), ((5, width), F32)],
        (flags, own, own_log, far, far_log, weights, cot),
    )


def outer_kernel(
    flags,
    att,
    weights,
    sums,
    gains,
    cot,
    res,
    logs,
    mixed_ref,
    grad_ref,
    back_ref,
    term_ref,
    rows_ref,
    norm_ref,
):
    valid = flags[0]
    inverse = flags[3]
    width = weights.shape[1]
    for at in range(0, width, 256):
        span = slice(at, at + 256)
        mean, scale = moments(sums[0:2, span], inverse)
        normal = (dot(att[...], weights[:, span]) - mean) * scale
        gain = gains[0:1, span]
        mixed_ref[:, span] = (
            (res[:, span].astype(F32) + (normal * gain + gains[1:2, span])) * valid
        ).astype(LOW)
        shift_grad = sums[2:3, span]
        gain_grad = scale * (sums[3:4, span] - mean * shift_grad)
        norm_ref[0:1, span] = gain_grad
        norm_ref[1:2, span] = shift_grad
        removed = (shift_grad + normal * gain_grad) * inverse
        grad = ((gain * scale * valid) * (cot[:, span].astype(F32) - removed)).astype(LOW)
        grad_ref[:, span] = grad
        norm_ref[2:3, span] = column_sums(grad.astype(F32))
    back = dot(grad_ref[...], weights[...], NT).astype(LOW)
    back_ref[...] = back
    term = jnp.sum(back.astype(F32) * att[...].astype(F32), axis=1, keepdims=True)
    term = jnp.broadcast_to(term, term_ref.shape)
    term_ref[...] = term
    rows_ref[...] = row_of(logs[...], rows_ref.shape[1])
    rows_ref[1:2, :] = row_of(term, rows_ref.shape[1])[0:1]


def outer(flags, att, weights, sums, gains, cot, res, logs):
    rows, inner = att.shape
    width = weights.shape[1]
    span = -(-rows // 128) * 128
    return call(
        outer_kernel,
        [
            ((rows, width), LOW),
            ((rows, width), LOW),
            ((rows, inner), LOW),
            ((rows, 128), F32),
            ((8, span), F32),
            ((3, width), F32),
        ],
        (flags, att, weights, sums, gains, cot, res, logs),
        micros=5,
    )


def project_kernel(
    flags,
    query_own,
    query_far,
    keep,
    near_keys,
    near_values,
    far,
    act,
    cells,
    weights,
    sums,
    gains,
    embed_far,
    cot_far,
    proj_ref,
    pre_ref,
    sums_ref,
    embed,
    cot,
    sems,
):
    valid = flags[0]
    inner = query_own.shape[1]
    copies = [
        pltpu.make_async_copy(embed_far, embed, sems.at[0]),
        pltpu.make_async_copy(cot_far, cot, sems.at[1]),
    ]
    for copy in copies:
        copy.start()
    proj_ref[:, :inner] = (query_own[...].astype(F32) + query_far[...].astype(F32)).astype(LOW)
    for at in range(0, 2 * inner, 256):
        span = slice(at, at + 256)
        near = near_keys[:, span] if at < inner else near_values[:, at - inner : at - inner + 256]
        proj_ref[:, inner + at : inner + at + 256] = (
            keep[:, span].astype(F32) + near.astype(F32) + far[:, span].astype(F32)
        ).astype(LOW)
    for copy in copies:
        copy.wait()
    for at in range(0, weights.shape[1], 256):
        span = slice(at, at + 256)
        normal, pre, _ = residual_tile(flags, act, cells, weights, sums, gains, at)
        grad = cot[:, span].astype(F32) + dot(proj_ref[...], embed[span, :], NT)
        out = grad * valid * slope(pre)
        pre_ref[:, span] = out
        sums_ref[0:1, span] = column_sums(out)
        sums_ref[1:2, span] = column_sums(out * normal)


def project_back(flags, query_own, query_far, keep, near_keys, near_values, far, act, cells, weights, sums, gains, embed, cot):
    rows, width = cells.shape
    inner = query_own.shape[1]
    return call(
        project_kernel,
        [((rows, 3 * inner), LOW), ((rows, width), F32), ((2, width), F32)],
        (flags, query_own, query_far, keep, near_keys, near_values, far, act, cells, weights, sums, gains, embed, cot),
        scratch=[
            pltpu.VMEM(embed.shape, LOW),
            pltpu.VMEM(cot.shape, LOW),
            pltpu.SemaphoreType.DMA((2,)),
        ],
        far=(12, 13),
        micros=10,
    )


def last_back_kernel(
    flags, pre_grad, act, weights, sums, gains, back_sums, pre_two, sums_two, gains_two, grad_ref, two_ref, sums_ref
):
    valid = flags[0]
    inverse = flags[3]
    two = None
    for at in range(0, weights.shape[1], 256):
        span = slice(at, at + 256)
        mean, scale = moments(sums[:, span], inverse)
        normal = (dot(act[...], weights[:, span]) - mean) * scale
        removed = (back_sums[0:1, span] + normal * back_sums[1:2, span]) * inverse
        grad = ((gains[0:1, span] * scale * valid) * (pre_grad[:, span] - removed)).astype(LOW)
        grad_ref[:, span] = grad
        part = dot(grad, weights[:, span], NT)
        two = part if two is None else two + part
    normal, active, _ = act_of(flags, pre_two[...], sums_two[...], gains_two[...])
    two = two * valid * slope(active)
    two_ref[...] = two
    sums_ref[0:1, :] = column_sums(two)
    sums_ref[1:2, :] = column_sums(two * normal)


def last_back(flags, pre_grad, act, weights, sums, gains, back_sums, pre_two, sums_two, gains_two):
    rows, width = pre_grad.shape
    narrow = act.shape[1]
    return call(
        last_back_kernel,
        [((rows, width), LOW), ((rows, narrow), F32), ((2, narrow), F32)],
        (flags, pre_grad, act, weights, sums, gains, back_sums, pre_two, sums_two, gains_two),
    )


def middle_back_kernel(
    flags, two, back_sums, pre_two, sums_two, gains_two, pre_one, sums_one, gains_one, weights, edges,
    grad_ref, one_ref, sums_ref, buffer, columns
):
    rows, narrow = two.shape
    valid = flags[0]
    inverse = flags[3]
    normal, _, scale = act_of(flags, pre_two[...], sums_two[...], gains_two[...])
    removed = (back_sums[0:1] + normal * back_sums[1:2]) * inverse
    grad = (gains_two[0:1, :] * scale * valid) * (two[...] - removed)
    grad_ref[...] = grad.astype(LOW)
    spread(grad, edges[...], buffer, columns, rows)
    one = None
    for tap in range(9):
        part = dot(columns[:, tap * narrow : (tap + 1) * narrow], tap_of(weights, 8 - tap), NT)
        one = part if one is None else one + part
    normal, active, _ = act_of(flags, pre_one[...], sums_one[...], gains_one[...])
    one = one * valid * slope(active)
    one_ref[...] = one
    sums_ref[0:1, :] = column_sums(one)
    sums_ref[1:2, :] = column_sums(one * normal)


def middle_back(flags, two, back_sums, pre_two, sums_two, gains_two, pre_one, sums_one, gains_one, weights, edges):
    rows, narrow = two.shape
    return call(
        middle_back_kernel,
        [((rows, narrow), LOW), ((rows, narrow), F32), ((2, narrow), F32)],
        (flags, two, back_sums, pre_two, sums_two, gains_two, pre_one, sums_one, gains_one, weights, edges),
        scratch=spread_scratch(rows, narrow),
    )


def middle_weight_kernel(flags, pre_one, sums_one, gains_one, grad, edges, out_ref, buffer, columns):
    rows, narrow = pre_one.shape
    _, act, _ = act_of(flags, pre_one[...], sums_one[...], gains_one[...])
    spread(act * sig(act) * flags[0], edges[...], buffer, columns, rows)
    for tap in range(9):
        out_ref[pl.ds(tap * narrow, narrow), :] = dot(
            columns[:, tap * narrow : (tap + 1) * narrow], grad[...], TN
        ).astype(LOW)


def middle_weight(flags, pre_one, sums_one, gains_one, grad, edges):
    rows, narrow = pre_one.shape
    return call(
        middle_weight_kernel,
        [((9 * narrow, narrow), LOW)],
        (flags, pre_one, sums_one, gains_one, grad, edges),
        scratch=spread_scratch(rows, narrow),
    )[0]


def first_grad_kernel(flags, one, back_sums, pre_one, sums_one, gains_one, grad_ref):
    normal, _, scale = act_of(flags, pre_one[...], sums_one[...], gains_one[...])
    removed = (back_sums[0:1] + normal * back_sums[1:2]) * flags[3]
    grad_ref[...] = (
        (gains_one[0:1, :] * scale * flags[0]) * (one[...] - removed)
    ).astype(LOW)


def first_grad_of(flags, one, back_sums, pre_one, sums_one, gains_one):
    rows, narrow = one.shape
    return call(
        first_grad_kernel,
        [((rows, narrow), LOW)],
        (flags, one, back_sums, pre_one, sums_one, gains_one),
    )[0]


def first_back_kernel(
    place, flags, grad, before, after, cells, middle, last, mine, others, cols_ref, buffer, halves, sems
):
    rows, narrow = grad.shape
    width = cells.shape[1]
    spots = before.shape[0]
    buffer[pl.ds(0, spots), :] = before[...].astype(F32) * flags[1]
    buffer[pl.ds(spots, rows), :] = grad[...].astype(F32)
    buffer[pl.ds(spots + rows, spots), :] = after[...].astype(F32) * flags[2]
    at = middle.shape[0]
    put_rows(halves, 0, middle[...])
    for tap in range(3):
        part = (buffer[pl.ds(spots * (2 - tap), rows), :] * flags[0]).astype(LOW)
        cols_ref[:, tap * narrow : (tap + 1) * narrow] = part
        put_rows(halves, at, dot(cells[...], part, TN).astype(LOW))
        at += width
    put_rows(halves, at, last[...])
    deal(place, halves, mine, others, sems)


def first_back(place, flags, grad, before, after, cells, middle, last):
    rows, narrow = grad.shape
    spots = before.shape[0]
    width = cells.shape[1]
    mine, others, cols = halves_call(
        first_back_kernel,
        middle.shape[0] + 3 * width + last.shape[0],
        [((rows, 3 * narrow), LOW)],
        (place, flags, grad, before, after, cells, middle, last),
        scratch=[pltpu.VMEM((rows + 2 * spots, narrow), F32)],
    )
    return (mine, others), cols


def early_weight_kernel(
    place, flags, res, proj, att, sums, grad, mine, others, halves, sems
):
    height, inner = res.shape[1], att.shape[1]
    left = (att[...].astype(F32) - sums[...] * flags[3]).astype(LOW)
    at = 0
    for index in range(proj.shape[1] // 256):
        put_rows(
            halves, at, dot(res[...], proj[:, index * 256 : (index + 1) * 256], TN).astype(LOW)
        )
        at += height
    for index in range(grad.shape[1] // 256):
        put_rows(
            halves, at, dot(left, grad[:, index * 256 : (index + 1) * 256], TN).astype(LOW)
        )
        at += inner
    deal(place, halves, mine, others, sems)


def halves_call(kernel, height, outs, args, scratch=()):
    shape = (height // 2, 256)
    return call(
        kernel,
        [(shape, LOW), (shape, LOW)] + outs,
        args,
        scalars=2,
        scratch=list(scratch)
        + [pltpu.VMEM((2,) + shape, LOW), pltpu.SemaphoreType.DMA((2,))],
        far_out=(0, 1),
        micros=8,
    )


def early_weight(place, flags, res, proj, att, sums, grad):
    height = res.shape[1] * proj.shape[1] // 256 + att.shape[1] * grad.shape[1] // 256
    return halves_call(
        early_weight_kernel, height, [], (place, flags, res, proj, att, sums, grad)
    )


def weight_kernel(left, right, out_ref):
    height = left.shape[1]
    for index in range(right.shape[1] // 256):
        out_ref[pl.ds(index * height, height), :] = dot(
            left[...], right[:, index * 256 : (index + 1) * 256], TN
        ).astype(LOW)


def weight_grad(left, right):
    rows, height = left.shape
    width = right.shape[1]
    return call(
        weight_kernel,
        [((height * width // 256, 256), LOW)],
        (left, right),
        scalars=0,
    )[0]


def pieces_of(low_half, high_half, start, stop):
    middle = low_half.shape[0]
    if start < middle:
        yield 0, low_half[pl.ds(start, min(stop, middle) - start), :]
    if stop > middle:
        begin = max(start, middle)
        yield begin - start, high_half[pl.ds(begin - middle, stop - begin), :]


def squares_of(values):
    return jnp.sum((values * values).reshape(-1, 8, values.shape[-1]), axis=0)


def emit(place, half, other, shares, squares):
    def write(low_half, high_half):
        squares[...] = jnp.zeros_like(squares)
        for start, stop, store, extra in shares:
            for offset, rows in pieces_of(low_half, high_half, start, stop):
                values = rows.astype(F32)
                if extra is not None:
                    values = values + extra[offset : offset + values.shape[0]]
                squares[...] += squares_of(values)
                store(offset, values)

    @pl.when(place[0] == 0)
    def _():
        write(half, other)

    @pl.when(place[0] == 1)
    def _():
        write(other, half)


def store_rows(ref, lead, cols):
    def store(offset, values):
        ref[lead + (pl.ds(offset, values.shape[0]), cols)] = values

    return store


def early_shares(embed_ref, back_ref, mean, grad_sum):
    width, inner = embed_ref.shape[1], embed_ref.shape[2]
    shares = []
    at = 0
    for index in range(3 * inner // 256):
        part, col = divmod(index * 256, inner)
        shares.append((at, at + width, store_rows(embed_ref, (part,), slice(col, col + 256)), None))
        at += width
    for index in range(width // 256):
        cols = slice(index * 256, index * 256 + 256)
        extra = mean[:, 0:1] * grad_sum[0:1, cols]
        shares.append((at, at + inner, store_rows(back_ref, (), cols), extra))
        at += inner
    return shares


def early_kernel(place, flags, half, other, sums, grad_sum, embed_ref, back_ref, embed_own, back_own, squares_ref):
    mean = sums[...] * flags[3]
    emit(place, half, other, early_shares(embed_ref, back_ref, column_of(mean), grad_sum), squares_ref)
    span = embed_own.shape[1]
    embed_own[...] = embed_ref[:, pl.ds(pl.multiple_of(place[1] * span, span), span), :]
    span = back_own.shape[0]
    back_own[...] = back_ref[pl.ds(pl.multiple_of(place[1] * span, span), span), :]


def early_grads(place, flags, half, other, sums, grad_sum, width, inner, shards):
    return call(
        early_kernel,
        [
            ((3, width, inner), F32),
            ((inner, width), F32),
            ((3, width // shards, inner), F32),
            ((inner // shards, width), F32),
            ((8, 256), F32),
        ],
        (place, flags, half, other, sums, grad_sum),
        scalars=2,
        micros=6,
    )


def late_shares(first_ref, middle_ref, last_ref):
    shares = []
    at = 0
    for ref in (middle_ref, first_ref):
        for index in range(ref.shape[0]):
            shares.append((at, at + ref.shape[1], store_rows(ref, (index,), slice(None)), None))
            at += ref.shape[1]
    for index in range(last_ref.shape[1] // 256):
        cols = slice(index * 256, index * 256 + 256)
        shares.append((at, at + last_ref.shape[0], store_rows(last_ref, (), cols), None))
        at += last_ref.shape[0]
    return shares


def late_kernel(rates, place, half, other, squares, extra, embed_own, back_own, *refs):
    given = [refs[3 * index : 3 * index + 3] for index in range(5)]
    first_ref, middle_ref, last_ref, norm_ref = refs[15:19]
    made = [refs[19 + 3 * index : 22 + 3 * index] for index in range(5)]
    tally = refs[34]
    emit(place, half, other, late_shares(first_ref, middle_ref, last_ref), tally)
    found = jnp.sum(tally[...] + squares[...], axis=0, keepdims=True)
    norm = jnp.sqrt(jnp.sum(found, axis=1, keepdims=True) + extra[0:1, 0:1])
    factor = jnp.minimum(1.0, CLIP_AT / (norm + 1e-06))
    norm_ref[0:1, :] = jnp.broadcast_to(norm, (1, 128))
    norm_ref[1:2, :] = jnp.broadcast_to(factor, (1, 128))

    def mine(span):
        return pl.ds(pl.multiple_of(place[1] * span, span), span)

    def own(index, part):
        if index == 0:
            return first_ref[part, mine(given[0][0].shape[1]), :]
        if index == 1:
            return middle_ref[part, mine(given[1][0].shape[1]), :]
        if index == 2:
            return last_ref[mine(given[2][0].shape[0]), :]
        return embed_own[part] if index == 3 else back_own[...]

    for index in range(5):
        master, moment, second = given[index]
        outs = made[index]
        for part in range(master.shape[0]) if len(master.shape) == 3 else (slice(None),):
            values = adam_step(
                master[part], own(index, part), moment[part], second[part], factor, rates[index]
            )
            for ref, value in zip(outs, values):
                ref[part] = value


def late_grads(rates, place, half, other, squares, extra, embed_own, back_own, states, shapes):
    flat = tuple(item for state in states for item in state)
    outs = [(shape, F32) for shape in shapes] + [((2, 128), F32)]
    outs += [(state[0].shape, F32) for state in states for _ in range(3)]
    found = call(
        functools.partial(late_kernel, rates),
        outs,
        (place, half, other, squares, extra, embed_own, back_own) + flat,
        scratch=[pltpu.VMEM((8, 256), F32)],
        micros=8,
    )
    return found[:3], found[3], [found[4 + 3 * index : 7 + 3 * index] for index in range(5)]


def unfold(value, height):
    return jnp.moveaxis(value.reshape(-1, height, 256), 0, 1).reshape(height, -1)


def plain_tail(early, late, mean, grad_sum, sizes, norm_square, states, rates, chan_at):
    width, inner, narrow = sizes
    core = chan_at & 1
    early, late = [
        jnp.where(core == 0, jnp.concatenate([half, other]), jnp.concatenate([other, half])).astype(
            F32
        )
        for half, other in (early, late)
    ]
    cut = 3 * inner * width // 256
    embed = unfold(early[:cut], width).reshape(width, 3, inner)
    back = unfold(early[cut:], inner) + mean[:, None] * grad_sum[None, :]
    middle = late[: 9 * narrow].reshape(9, narrow, narrow)
    first = late[9 * narrow : 9 * narrow + 3 * width].reshape(3, width, narrow)
    last = unfold(late[9 * narrow + 3 * width :], narrow)
    grads = (first, middle, last, jnp.moveaxis(embed, 1, 0), back)
    norm = jnp.sqrt(sum(jnp.sum(item * item) for item in grads) + norm_square)
    factor = jnp.minimum(1.0, CLIP_AT / (norm + 1e-06))
    made = []
    for grad, state, rate in zip(grads, states, rates):
        axis = grad.ndim - 2
        span = state[0].shape[axis]
        owned = lax.dynamic_slice_in_dim(grad, chan_at * span, span, axis)
        made.append(adam_step(state[0], owned, state[1], state[2], factor, rate))
    return grads, norm, factor, made


def input_kernel(cols, weights, pre_grad, out_ref):
    shards, _, span, narrow = weights.shape
    each = 256 // span
    for at in range(0, pre_grad.shape[1], 256):
        out = pre_grad[:, at : at + 256]
        begin = at // span
        for tap in range(3):
            rows = weights[pl.ds(begin, each), tap].reshape(256, narrow)
            out = out + dot(cols[:, tap * narrow : (tap + 1) * narrow], rows, NT)
        span_at = slice(at, at + 256)
        out_ref[:, span_at] = out.astype(LOW)


def input_grad(cols, weights, pre_grad):
    rows, width = pre_grad.shape
    return call(
        input_kernel,
        [((rows, width), LOW)],
        (cols, weights, pre_grad),
        scalars=0,
    )[0]


def adam_step(master, gradient, moment, second, factor, rate):
    clipped = gradient * factor
    moment_new = BETA_ONE * moment + (1.0 - BETA_ONE) * clipped
    second_new = BETA_TWO * second + (1.0 - BETA_TWO) * clipped * clipped
    moment_hat = moment_new / (1.0 - BETA_ONE**STEP)
    second_hat = second_new / (1.0 - BETA_TWO**STEP)
    master_new = master - rate * (
        moment_hat / (jnp.sqrt(second_hat) + ADAM_EPS) + WEIGHT_DECAY * master
    )
    return (moment_new, second_new, master_new)


def body(
    features,
    cotangent,
    frame_counts,
    weight_first,
    weight_middle,
    weight_last,
    weight_embed,
    weight_back,
    norm_params,
    moment_first,
    moment_middle,
    moment_last,
    moment_embed,
    moment_back,
    moment_norm,
    second_first,
    second_middle,
    second_last,
    second_embed,
    second_back,
    second_norm,
):
    chan_at = lax.axis_index("chan")
    device = lax.axis_index("clip") * lax.axis_size("chan") + chan_at
    frames, spot_count, model_width = features.shape
    row_count = frames * spot_count
    narrow = BOT
    inner_width = INNER
    clip_place = chan_at % DPC
    clip_at = device // DPC
    clip_ids = jnp.arange(frame_counts.shape[0], dtype=jnp.int32)
    length = jnp.sum(jnp.where(clip_ids == clip_at, frame_counts, 0))

    def valid_at(place):
        return ((place >= 0) & (place < DPC) & (place * frames < length)).astype(jnp.float32)

    place = jnp.stack([chan_at & 1, chan_at, lax.axis_index("clip")]).astype(jnp.int32)
    own_ok = valid_at(clip_place)
    row_total = jnp.sum(frame_counts).astype(jnp.float32) * spot_count
    zero = jnp.zeros((), jnp.float32)
    flags = jnp.stack(
        [own_ok, valid_at(clip_place - 1), valid_at(clip_place + 1), 1.0 / row_total]
        + [valid_at(clip_place ^ 2)] + [zero] * 3
    )
    held = sum(valid_at(clip_place ^ turn) for turn in range(4)) * own_ok
    blocks_own = held.astype(jnp.int32).reshape(1)
    blocks_far = (held * valid_at(clip_place ^ 4)).astype(jnp.int32).reshape(1)
    span_list = [narrow] * 4 + [model_width] * 4
    starts = [sum(span_list[:index]) for index in range(8)]
    gains_one, gains_two, gains_three, gains_four = [
        norm_params[starts[index] : starts[index] + 2 * span_list[index]].reshape(2, -1)
        for index in range(0, 8, 2)
    ]
    shards = lax.axis_size("chan")
    piece, middle_next, last_next, embed_next, back_next = tied(
        quarter_of(weight_first), weight_middle, weight_last, weight_embed, weight_back
    )
    tall = weight_middle.shape[0] * weight_middle.shape[1]
    packed = jnp.concatenate(
        [
            middle_next.reshape(tall, narrow),
            jnp.moveaxis(last_next.reshape(-1, model_width // 256, 256), 1, 0).reshape(-1, 256),
        ]
    ).astype(LOW)
    packed = lax.all_gather(packed, "chan", axis=0, tiled=False)
    middle_low = packed[:, :tall].reshape((shards,) + weight_middle.shape)
    last_low = jnp.moveaxis(
        packed[:, tall:].reshape(shards, model_width // 256, -1, 256), 1, 2
    ).reshape(narrow, model_width)
    if weight_middle.shape[1] % 16:
        middle_low = jnp.moveaxis(middle_low, 0, 1).reshape(1, 9, narrow, narrow)
    embed_low, back_low = (
        lax.all_gather(embed_next.astype(LOW).reshape(-1, 3 * inner_width), "chan", axis=0, tiled=True),
        lax.all_gather(back_next.astype(LOW), "chan", axis=0, tiled=True),
    )
    spots = np.arange(row_count)
    across, down = spots % WW, spots // WW % HH
    edges = jnp.asarray(
        np.stack([across > 0, across < WW - 1, down > 0, down < HH - 1] + [across < 0] * 4, axis=1)
        .astype(np.float32)
    )
    cells = features.reshape(row_count, model_width)
    cot = cotangent.reshape(row_count, model_width)
    before, after = beside(features, spot_count)
    if shards == 8 and lax.axis_size("clip") == 4:
        pre_one, sums_one, first_low = first_conv_parts(
            place, flags, cells, before, after, *quarters_of(piece)
        )
    else:
        first_low = whole_of(weight_first)
        pre_one, sums_one = first_conv(flags, cells, before, after, first_low)
    sums_one = total(sums_one)
    pre_two, sums_two = middle_conv(
        flags, pre_one, sums_one, gains_one, middle_low, edges
    )
    sums_two = total(sums_two)
    act_two, sums_three = last_conv(flags, pre_two, sums_two, gains_two, last_low)
    sums_three, cot = total(sums_three, (cot,))
    residual_low, query, pair_own = embed_rows(
        flags, act_two, cells, last_low, sums_three, gains_three, embed_low
    )
    pair_core = flipped(pair_own, "chan", 1)
    query_far, pair_far = flipped(query, "chan", 4), flipped(pair_own, "chan", 2)
    query_far, pair_far, back_low = tied(query_far, pair_far, back_low)
    blocks = (pair_own, pair_core, pair_far, flipped(pair_far, "chan", 1))
    part_far, log_far = attend(blocks_far, query_far, blocks, True)
    part_far = flipped(part_far, "chan", 4)
    log_far = flipped(log_far, "chan", 4)
    part_own, log_own = attend(blocks_own, query, blocks, False)
    attended, logs, sums_four = merge(flags, part_own, log_own, part_far, log_far, back_low, cot)
    sums_four = total(sums_four)
    mixed, attn_grad, attended_grad, terms, packed, norm_four = outer(
        flags, attended, back_low, sums_four, gains_four, cot, residual_low, logs
    )
    mixed = laid_out(mixed, frames)
    attended_grad_far = flipped(attended_grad, "chan", 4)
    packed_far = flipped(packed, "chan", 4)
    query_own, held = attend_back(
        blocks_own, query, attended_grad, (logs, terms), blocks, (0, 1, 2, 3), None, None, F32
    )
    query_part, (far, far_core) = attend_back(
        blocks_far, query_far, attended_grad_far, (packed_far,), blocks[2:], (2, 3), held[2:], None, F32
    )
    far = (far.astype(F32) + flipped(far_core, "chan", 1).astype(F32)).astype(LOW)
    far, near_own = tied(far, held[0])
    far = flipped(far, "chan", 2)
    query_part, (keep, give_keys, give_values) = attend_back(
        blocks_far, query_far, attended_grad_far, (packed_far,), blocks[:2], (0, 1), (near_own, held[1]),
        query_part, LOW, (1,),
    )
    query_part = flipped(query_part, "chan", 4)
    near_keys, near_values = flipped(give_keys, "chan", 1), flipped(give_values, "chan", 1)
    projected_grad, pre_grad, back_three = project_back(
        flags, query_own, query_part, keep, near_keys, near_values, far, act_two, cells, last_low, sums_three,
        gains_three, embed_low, cot,
    )
    early = early_weight(
        place, flags, residual_low, projected_grad, attended, sums_four[4:5, :inner_width], attn_grad
    )
    back_three, *early = total(jnp.concatenate([back_three, norm_four[2:3]]), early)
    last_grad, two_grad, back_two = last_back(
        flags, pre_grad, act_two, last_low, sums_three, gains_three, back_three, pre_two, sums_two,
        gains_two,
    )
    back_two = total(back_two)
    last_local = weight_grad(act_two, last_grad)
    middle_grad, one_grad, back_one = middle_back(
        flags, two_grad, back_two, pre_two, sums_two, gains_two, pre_one, sums_one, gains_one,
        middle_low, edges,
    )
    back_one = total(back_one)
    middle_local = middle_weight(flags, pre_one, sums_one, gains_one, middle_grad, edges)
    first_grad = first_grad_of(flags, one_grad, back_one, pre_one, sums_one, gains_one)
    before, after = beside(first_grad.reshape(frames, spot_count, narrow), spot_count)
    late, grad_cols = first_back(place, flags, first_grad, before, after, cells, middle_local, last_local)
    features_gradient = laid_out(input_grad(grad_cols, first_low, pre_grad), frames)
    gain_one_grad, shift_one_grad = back_one[1], back_one[0]
    gain_two_grad, shift_two_grad = back_two[1], back_two[0]
    gain_three_grad, shift_three_grad = back_three[1], back_three[0]
    gain_four_grad, shift_four_grad = norm_four[0], norm_four[1]
    norm_gradient = jnp.concatenate(
        [
            gain_one_grad,
            shift_one_grad,
            gain_two_grad,
            shift_two_grad,
            gain_three_grad,
            shift_three_grad,
            gain_four_grad,
            shift_four_grad,
        ]
    )
    groups = [list(range(core, shards, 2)) for core in range(2)]
    early = lax.psum_scatter(core_step(*early), "clip", scatter_dimension=0, tiled=True)
    early = lax.psum(early, "chan", axis_index_groups=groups)
    steps = level_steps()[1:]
    late = scatter_sum(core_step(*late), steps)
    early, late = tied(early, late)
    early = lax.all_gather(early, "clip", axis=0, tiled=True)
    late = gather_sum(late, steps)
    early, late, mixed, features_gradient = tied(early, late, mixed, features_gradient)
    early = (early, flipped(early, "chan", 1))
    late = (late, flipped(late, "chan", 1))
    fans = (3 * D, 9 * BOT, BOT, D, INNER)
    rates = tuple(0.5 * fan ** (-0.5) for fan in fans)
    states = (
        (weight_first, moment_first, second_first),
        (weight_middle, moment_middle, second_middle),
        (weight_last, moment_last, second_last),
        tuple(jnp.moveaxis(item, 1, 0) for item in (weight_embed, moment_embed, second_embed)),
        (weight_back, moment_back, second_back),
    )
    norm_square = jnp.sum(norm_gradient * norm_gradient)
    if weight_middle.shape[1] % 16 == 0:
        embed, back, embed_own, back_own, squares = early_grads(
            place,
            flags,
            *early,
            sums_four[4:5, :inner_width],
            back_three[2:3],
            model_width,
            inner_width,
            shards,
        )
        shapes = ((3, model_width, narrow), (9, narrow, narrow), (narrow, model_width))
        (first, middle, last), norm_row, results = late_grads(
            rates, place, *late, squares, norm_square.reshape(1, 1), embed_own, back_own, states, shapes
        )
        gradient_norm, factor = norm_row[0, 0], norm_row[1, 0]
    else:
        (first, middle, last, embed, back), gradient_norm, factor, results = plain_tail(
            early,
            late,
            sums_four[4, :inner_width] * flags[3],
            back_three[2],
            (model_width, inner_width, narrow), norm_square, states, rates, chan_at
        )
    results = list(results)
    results[3] = tuple(jnp.moveaxis(item, 0, 1) for item in results[3])
    results.append(adam_step(norm_params, norm_gradient, moment_norm, second_norm, factor, GAIN_RATE))
    return (
        mixed,
        features_gradient,
        first,
        middle,
        last,
        jnp.moveaxis(embed, 0, 1),
        back,
        norm_gradient,
    ) + tuple(results[index][kind] for kind in range(3) for index in range(6)) + (gradient_norm,)


def solution(mesh):
    placed = (
        P(("clip", "chan"), None, None),
        P(("clip", "chan"), None, None),
        P(),
        P(None, "chan", None),
        P(None, "chan", None),
        P("chan", None),
        P("chan", None, None),
        P("chan", None),
        P(),
        P(None, "chan", None),
        P(None, "chan", None),
        P("chan", None),
        P("chan", None, None),
        P("chan", None),
        P(),
        P(None, "chan", None),
        P(None, "chan", None),
        P("chan", None),
        P("chan", None, None),
        P("chan", None),
        P(),
    )
    return jax.shard_map(
        body,
        mesh=mesh,
        in_specs=placed,
        out_specs=(
            P(("clip", "chan"), None, None),
            P(("clip", "chan"), None, None),
            P(),
            P(),
            P(),
            P(),
            P(),
            P(),
            P(None, "chan", None),
            P(None, "chan", None),
            P("chan", None),
            P("chan", None, None),
            P("chan", None),
            P(),
            P(None, "chan", None),
            P(None, "chan", None),
            P("chan", None),
            P("chan", None, None),
            P("chan", None),
            P(),
            P(None, "chan", None),
            P(None, "chan", None),
            P("chan", None),
            P("chan", None, None),
            P("chan", None),
            P(),
            P(),
        ),
        check_vma=False,
    )
```
